32 devices in a mesh: dp: 8 (over z, x), tp: 4 (over y, core).
Axes of the slice: x: 2, y: 2, z: 4, core: 2. Of those that a mesh axis runs over, the one named last changes fastest.
Arguments:
- tokens: bfloat16 [8192, 768], P('dp'), may hold values from -6 to 6
- cotangent: bfloat16 [8192, 768], P('dp'), may hold values from -6 to 6
- w_qkv: bfloat16 [3, 768, 768], P(None, 'dp', 'tp'), may hold values from -0.21875 to 0.21875
- w_out: bfloat16 [768, 768], P('tp', 'dp'), may hold values from -1.75 to 1.75
- w_up: bfloat16 [768, 3072], P('dp', 'tp'), may hold values from -0.21875 to 0.21875
- w_down: bfloat16 [3072, 768], P('tp', 'dp'), may hold values from -0.109375 to 0.109375
- gains: bfloat16 [2, 768], P(None, 'dp'), may hold values from 0.099609375 to 1.8984375
- shifts: bfloat16 [4, 768], P(None, 'dp'), may hold values from -3 to 3
- b_qkv: bfloat16 [2, 12, 64], P(None, 'tp', 'dp'), may hold values from -3 to 3
- b_up: bfloat16 [24, 128], P('tp', 'dp'), may hold values from -3 to 3
- clip_lengths: int32 [16, 4], P('dp'), may hold values from 1 to 307, 512 in all within a row
Outputs:
- mixed: bfloat16 [8192, 768], P('dp')
- tokens_grad: float32 [8192, 768], P('dp')
- w_qkv_grad: float32 [3, 768, 768], P(None, 'dp', 'tp')
- w_out_grad: float32 [768, 768], P('tp', 'dp')
- w_up_grad: float32 [768, 3072], P('dp', 'tp')
- w_down_grad: float32 [3072, 768], P('tp', 'dp')
- gains_grad: float32 [2, 768], P(None, 'dp')
- shifts_grad: float32 [4, 768], P(None, 'dp')
- b_qkv_grad: float32 [2, 12, 64], P(None, 'tp', 'dp')
- b_up_grad: float32 [24, 128], P('tp', 'dp')
The draws below stay inside these ranges and needn't reach their ends.
Inputs may be any that keep to these rules, and one draw needn't show every extreme that they name: `clip_lengths`: each row holds the lengths of the 4 clips packed in order into one block of 512 rows; they sum to 512 and the longest of each row is exactly 307.
All inputs are finite; a program needn't handle non-finite values.
Results may differ from the reference program's by a relative error of at most 0.015.
Values may be sent and summed in bfloat16 or wider, within the bound.
A program may use at most 128 MiB of HBM per device.

```python
import math
import jax
import jax.numpy as jnp
import numpy as np
from jax import lax

D = 768
H = 12
HD = 64
FF = 3072
ROWS = 512
LONGEST = 307
CLIPS = 4
BLOCKS = 16
TOKENS = 8192


def raised(drawn, own_key, source, target, blocks, factor):
    def block_of(axis_at):
        return (jnp.arange(drawn.shape[axis_at]) // (drawn.shape[axis_at] // blocks)).reshape((-1,) + (1,) * (drawn.ndim - 1 - axis_at))

    one_side = jax.random.permutation(own_key, blocks)[block_of(target)]
    other_side = (block_of(target) + blocks // 2) % blocks
    return jnp.where((block_of(source) == one_side) | (block_of(source) == other_side), factor * drawn, drawn)


def block_levels(key, shape, shards, least, top_value):
    factor_of = 1.0
    for position, parts in shards:
        steps = jax.random.uniform(jax.random.fold_in(jax.random.fold_in(key, 6), position), (parts,), jnp.float32, least / len(shards), top_value / len(shards))
        factor_of = factor_of * jnp.repeat(jnp.exp(steps), shape[position] // parts).reshape((-1,) + (1,) * (len(shape) - 1 - position))
    return factor_of


def length_profile(amount, total, reach, lean):
    weights = [(1 << 20) // math.isqrt(grade ** lean) + 1 for grade in range(2, amount + 1)]
    surplus, holding = total - reach - (amount - 1), [1] * (amount - 1)
    while surplus > 0:
        free = [i for i in range(amount - 1) if holding[i] < reach]
        mass, budget = sum([weights[i] for i in free]), surplus
        for i in free:
            addition = min(reach - holding[i], max(1, budget * weights[i] // mass), surplus)
            holding[i] = holding[i] + addition
            surplus = surplus - addition
    return np.array([reach] + holding)


def ragged_sizes(key, count, total, limit, slope):
    if count == 2:
        one = jax.random.randint(key, (), max(1, total - limit), min(limit, total - 1) + 1)
        return jnp.stack([one, total - one])
    tallies = jnp.asarray(length_profile(count, total, limit, slope), jnp.int32)
    pairs = (count - 1) // 2
    donor, sink = tallies[1:1 + 2 * pairs:2], tallies[2:2 + 2 * pairs:2]
    room = jnp.minimum(donor - 1, limit - sink)
    shifted = jax.random.randint(jax.random.fold_in(key, 1), (pairs,), 0, 1 << 20) % (room + 1)
    tallies = tallies.at[1:1 + 2 * pairs:2].set(donor - shifted).at[2:2 + 2 * pairs:2].set(sink + shifted)
    return tallies[jax.random.permutation(jax.random.fold_in(key, 2), count)]


def bell_draw(own_key, dims, deviation, most, cuts=(), held_as=jnp.bfloat16):
    values = deviation * jax.random.normal(own_key, dims, jnp.float32)
    if cuts:
        values = values * block_levels(own_key, dims, cuts, -0.22, 0.18)
    return jnp.clip(values, -most, most).astype(held_as)


def gaussian_with(key, shape, scale, limit, cuts, heavy, held_as=jnp.bfloat16):
    drawn = scale * jax.random.normal(key, shape, jnp.float32)
    if cuts:
        drawn = drawn * block_levels(key, shape, cuts, -0.22, 0.18)
    return jnp.clip(raised(drawn, jax.random.fold_in(key, 3), *heavy), -limit, limit).astype(held_as)


def setup_inputs(seed: int = 0) -> dict:
    streams_of = jax.random.split(jax.random.key(seed), 12)
    return {
        "tokens": bell_draw(streams_of[0], (TOKENS, D), 1.0, 6.0, ((0, 8),)),
        "cotangent": gaussian_with(streams_of[1], (TOKENS, D), 1.0, 6.0, ((0, 8),), (0, 1, 8, 2.0)),
        "w_qkv": bell_draw(streams_of[2], (3, D, D), D ** -0.5, 0.21875, ((1, 8), (2, 4))),
        "w_out": bell_draw(streams_of[3], (D, D), (D // 64) ** -0.5, 1.75, ((0, 4), (1, 8))),
        "w_up": bell_draw(streams_of[4], (D, FF), D ** -0.5, 0.21875, ((0, 8), (1, 4))),
        "w_down": bell_draw(streams_of[5], (FF, D), FF ** -0.5, 0.109375, ((0, 4), (1, 8))),
        "gains": jnp.clip(1.0 + 0.18 * jax.random.normal(streams_of[6], (2, D), jnp.float32), 0.099609375, 1.8984375).astype(jnp.bfloat16),
        "shifts": bell_draw(streams_of[7], (4, D), 0.5, 3.0, ((1, 8),)),
        "b_qkv": bell_draw(streams_of[8], (2, H, HD), 0.5, 3.0, ((1, 4), (2, 8))),
        "b_up": bell_draw(streams_of[9], (FF // 128, 128), 0.5, 3.0, ((0, 4), (1, 8))),
        "clip_lengths": jax.vmap(lambda own: ragged_sizes(own, CLIPS, ROWS, LONGEST, 1))(jax.random.split(streams_of[10], BLOCKS)).reshape((BLOCKS, CLIPS)).astype(jnp.int32),
    }


eps = 1e-06
masked = -1e+30

@jax.custom_vjp
def low(v):
    return lax.optimization_barrier(v.astype(jnp.bfloat16)).astype(jnp.float32)

@jax.custom_vjp
def low_back(v):
    return v

def low_keep(v):
    return (low(v), None)

def low_pass(kept, grad):
    return (grad,)

def back_keep(v):
    return (v, None)

def back_low(kept, grad):
    return (low(grad),)
low.defvjp(low_keep, low_pass)
low_back.defvjp(back_keep, back_low)

def product(left_hand, right_hand):
    return jnp.dot(left_hand, right_hand, precision=lax.Precision.HIGHEST)

def layer_norm(values, gain_vec, shift_vec):
    centred = values - lax.optimization_barrier(jnp.mean(values, axis=-1, keepdims=True))
    spread = lax.optimization_barrier(jnp.mean(centred * centred, axis=-1, keepdims=True))
    return centred * lax.rsqrt(spread + eps) * gain_vec + shift_vec

def segment_ids(lengths):
    clip_ends = jnp.cumsum(lengths).astype(jnp.int32)
    positions = jnp.arange(ROWS, dtype=jnp.int32)
    return lax.optimization_barrier(jnp.sum((positions[:, None] >= clip_ends[None, :]).astype(jnp.int32), axis=1)).astype(jnp.int32)

def attend_block(inputs):
    queries, key_rows, values, segments = inputs
    raw_scores = jnp.einsum('qhd,khd->hqk', queries, key_rows, precision=lax.Precision.HIGHEST) * HD ** (-0.5)
    scores = low_back(raw_scores)
    same_clip = segments[:, None] == segments[None, :]
    scores = jnp.where(same_clip[None], scores, masked)
    weights = low(jax.nn.softmax(scores, axis=-1))
    return jnp.einsum('hqk,khd->qhd', weights, values, precision=lax.Precision.HIGHEST)

def forward(tokens, w_qkv, w_out, w_up, w_down, gains, shifts, b_qkv, b_up, segments):
    normed = low(layer_norm(tokens, gains[0], shifts[0]))
    queries = low(low_back(product(normed, w_qkv[0]) + b_qkv[0].reshape(D)))
    key_rows = low(low_back(product(normed, w_qkv[1])))
    values = low(low_back(product(normed, w_qkv[2]) + b_qkv[1].reshape(D)))
    block_shape = (BLOCKS, ROWS, H, HD)
    attended = lax.map(jax.checkpoint(attend_block), (queries.reshape(block_shape), key_rows.reshape(block_shape), values.reshape(block_shape), segments))
    attended = low(low_back(attended.reshape(TOKENS, D)))
    middle = tokens + low_back(product(attended, w_out)) + shifts[2]
    normed_two = low(layer_norm(middle, gains[1], shifts[1]))
    hidden = low_back(product(normed_two, w_up) + b_up.reshape(FF))
    activated = low(jax.nn.gelu(hidden, approximate=False))
    return middle + low_back(product(activated, w_down)) + shifts[3]

def reference(tokens, cotangent, w_qkv, w_out, w_up, w_down, gains, shifts, b_qkv, b_up, clip_lengths):
    segments = jax.vmap(segment_ids)(clip_lengths)
    params = tuple((array.astype(jnp.float32) for array in (tokens, w_qkv, w_out, w_up, w_down, gains, shifts, b_qkv, b_up)))

    def layer_fn(*inputs):
        return forward(*inputs, segments)
    mixed_rows, pullback = jax.vjp(layer_fn, *params)
    gradient = pullback(cotangent.astype(jnp.float32))
    return (mixed_rows.astype(jnp.bfloat16), gradient[0], gradient[1], gradient[2], gradient[3], gradient[4], gradient[5], gradient[6], gradient[7], gradient[8])
```

```python
import functools
import math

import jax
import jax.numpy as jnp
from jax import lax
from jax.experimental import pallas as pl
from jax.experimental.pallas import tpu as pltpu
from jax.sharding import PartitionSpec as P

MESH = pl.DeviceIdType.MESH
F32 = jnp.float32
BF16 = jnp.bfloat16
D = 768
BLK = 512
HALF = 256
PARTS = 8
PIECE = D // PARTS
eps = 1e-06
masked = -1e30


def mm(a, b, ca, cb):
    return lax.dot_general(a, b, (((ca,), (cb,)), ((), ())), preferred_element_type=F32)


def standardize(v):
    centred = v - jnp.mean(v, axis=-1, keepdims=True)
    rstd = lax.rsqrt(jnp.mean(centred * centred, axis=-1, keepdims=True) + eps)
    return centred * rstd, rstd


def norm_back(grad, gain, z, rstd):
    n = grad * gain
    return (
        n - jnp.mean(n, axis=-1, keepdims=True) - z * jnp.mean(n * z, axis=-1, keepdims=True)
    ) * rstd


def layer_kernel(inner, nb, refs):
    (tok_h, cot_h, ws, wa, wu, wd, lens) = refs[:7]
    (mixed_h, tgrad_h, gra_o, gru_o, grd_o, small_o) = refs[7:13]
    (
        tok, cot, g, gs, prm, nrm, qh, kh, vh, pr, att, mid, n2, act, dgl, hg, ml, mgr, dqkv,
        dka, dva, pb, rc, sy, ry, mxs, tgs, gr, rx, hs, rz, sg, sgc, sgx, sgz,
        lsem, zss, zrs, xss, xrs, css, crs, yss, yrs, nss, nrs, oss, ors, rxs, rxr, rzs, rzr, sms, smr,
    ) = refs[13:]
    d = lax.axis_index("dp")
    t = lax.axis_index("tp")
    z = d // 2
    x = d % 2
    c = t % 2
    xn = d + 1 - 2 * x
    sib = t + 1 - 2 * c
    yn = lax.rem(t + 2, 4)
    later = []

    def remote(src, dst, s, r, dd, tt):
        return pltpu.make_async_remote_copy(
            src_ref=src, dst_ref=dst, send_sem=s, recv_sem=r, device_id=(dd, tt), device_id_type=MESH
        )

    def launch(copy, guard=None):
        if guard is None:
            copy.start()
        else:
            pl.when(guard)(copy.start)
        later.append((copy.wait_send, guard))

    bar = pltpu.get_barrier_semaphore()
    greet = [(d, sib), (d, yn)]
    if inner:
        greet += [(xn, t)] + [(lax.rem(d + 2 * j, 8), t) for j in (1, 2, 3)]
    for who in greet:
        pl.semaphore_signal(bar, 1, device_id=who, device_id_type=MESH)
    cp_tok = pltpu.make_async_copy(tok_h, tok, lsem.at[0])
    cp_tok.start()
    cp_cot = pltpu.make_async_copy(cot_h, cot, lsem.at[1])
    cp_cot.start()
    pl.semaphore_wait(bar, len(greet))

    shards = (wa, wu, wd, ws)

    def slot(m, i):
        return gs.at[i] if m == 3 else g.at[m, i]

    def zcopy(m, side, src, i, s):
        return remote(src, slot(m, i), zss.at[m, side, s], zrs.at[m, side, s], d + 2 - 4 * side, t)

    def xcopy(m, src, i, zsrc):
        return remote(src, slot(m, i), xss.at[m, zsrc], xrs.at[m, zsrc], xn, t)

    def gather_start(m):
        launch(zcopy(m, 0, shards[m], d, 0), z < 3)
        launch(zcopy(m, 1, shards[m], d, 0), z > 0)
        launch(xcopy(m, shards[m], d, z))

    def gather_step(m, s):
        for side in (0, 1):
            i = d - 2 * s if side == 0 else d + 2 * s
            here = z >= s if side == 0 else z + s <= 3
            onward = z < 3 if side == 0 else z > 0

            @pl.when(here)
            def _():
                zcopy(m, side, slot(m, i), i, s - 1).wait_recv()

            if s < 3:
                launch(zcopy(m, side, slot(m, i), i, s), jnp.logical_and(here, onward))
            launch(xcopy(m, slot(m, i), i, i // 2), here)

    def gather_end(m):
        for k in range(4):
            i = 2 * k + 1 - x
            xcopy(m, slot(m, i), i, k).wait_recv()

    def half_rows(b, j):
        return pl.ds(pl.multiple_of(b * BLK + lax.rem(1 - c + j, 2) * HALF, HALF), HALF)

    def own_rows(b):
        return pl.ds(pl.multiple_of(b * BLK + c * HALF, HALF), HALF)

    def ccopy(st, b):
        return remote(pb.at[st, b, 0], rc.at[st, b], css.at[st, b], crs.at[st, b], d, sib)

    def ycopy(st, b):
        return remote(sy.at[st, b], ry.at[st, b], yss.at[st, b], yrs.at[st, b], d, yn)

    def sum_part(st, b, product):
        def one(j, carry):
            pb[st, b, j] = product(half_rows(b, j)).astype(BF16)

            @pl.when(j == 0)
            def _():
                ccopy(st, b).start()

            return carry

        lax.fori_loop(0, 2, one, 0)
        later.append((ccopy(st, b).wait_send, None))

    def sum_mid(st, b):
        ccopy(st, b).wait_recv()
        sy[st, b] = (pb[st, b, 1].astype(F32) + rc[st, b].astype(F32)).astype(BF16)
        launch(ycopy(st, b))

    def sum_end(st, b):
        ycopy(st, b).wait_recv()
        return sy[st, b].astype(F32) + ry[st, b].astype(F32)

    def share(buf, k, b):
        return remote(buf.at[own_rows(b)], buf.at[own_rows(b)], nss.at[k, b], nrs.at[k, b], d, sib)

    def shared(buf, k, b):
        rows = half_rows(b, 0)
        remote(buf.at[rows], buf.at[rows], nss.at[k, b], nrs.at[k, b], d, sib).wait_recv()

    lane = lax.broadcasted_iota(jnp.int32, (1, 128), 1)
    low = lane < 64

    def mat(m):
        return g[m].reshape(D, D)

    def chunks(b, n, fn):
        def one(i, carry):
            fn(pl.ds(pl.multiple_of(b * BLK + i * (BLK // n), BLK // n), BLK // n), i)
            return carry

        lax.fori_loop(0, n, one, 0)

    def first_norm(b):
        def fn(rows, i):
            zz, _ = standardize(tok[rows].astype(F32))
            nrm[rows] = (zz * prm[0:1] + prm[2:3]).astype(BF16)

        chunks(b, 4, fn)

    def project(b):
        def fn(rows, i):
            p = mm(nrm[rows], mat(0), 1, 0) + prm[6:7]
            s0, s1, s2, s3, s4 = (p[:, 128 * k : 128 * k + 128] for k in range(5))
            for ref, s in ((qh, s0), (kh, s1), (vh, s2)):
                ref[0, rows] = jnp.where(low, s, 0.0).astype(BF16)
                ref[1, rows] = jnp.where(low, 0.0, s).astype(BF16)
            qh[2, rows] = jnp.where(low, s3, 0.0).astype(BF16)
            kh[2, rows] = jnp.where(low, pltpu.roll(s3, 64, 1), 0.0).astype(BF16)
            vh[2, rows] = jnp.where(low, s4, 0.0).astype(BF16)

        chunks(b, 2, fn)

    def attend(b):
        blk = slice(b * BLK, b * BLK + BLK)
        e0 = lens[b, 0]
        e1 = e0 + lens[b, 1]
        e2 = e1 + lens[b, 2]

        def clip_of(pos):
            return (
                (pos >= e0).astype(jnp.int32)
                + (pos >= e1).astype(jnp.int32)
                + (pos >= e2).astype(jnp.int32)
            )

        def fn(rows, i):
            q_clip = clip_of(lax.broadcasted_iota(jnp.int32, (HALF, 1), 0) + i * HALF)
            k_clip = clip_of(lax.broadcasted_iota(jnp.int32, (1, BLK), 1))
            same = q_clip == k_clip
            outs = []
            for h in range(3):
                s = mm(qh[h, rows], kh[h, blk], 1, 1) * 0.125
                s = jnp.where(same, s, masked)
                e = jnp.exp(s - jnp.max(s, axis=-1, keepdims=True))
                p = (e / jnp.sum(e, axis=-1, keepdims=True)).astype(BF16)
                pr[3 * b + h, pl.ds(pl.multiple_of(i * HALF, HALF), HALF)] = p
                outs.append(mm(p, vh[h, blk], 1, 0))
            att[rows, 0:128] = pltpu.roll(outs[2], 64, 1).astype(BF16)
            att[rows, 128:256] = (outs[0] + outs[1]).astype(BF16)

        chunks(b, 2, fn)

    def out_part(b):
        sum_part(0, b, lambda rows: mm(att[rows], g[0, :, :, 512:768].reshape(D, 256), 1, 1))

    def second_norm(b):
        rows = own_rows(b)
        m = tok[rows].astype(F32) + sum_end(0, b) + prm[4:5]
        mid[b] = m
        zz, _ = standardize(m)
        n2[rows] = (zz * prm[1:2] + prm[3:4]).astype(BF16)
        launch(share(n2, 0, b))

    def up(b):
        def fn(rows, i):
            h = mm(n2[rows], mat(1), 1, 0) + prm[7:8]
            cdf = 0.5 * (1.0 + lax.erf(h * (1.0 / math.sqrt(2.0))))
            act[rows] = (h * cdf).astype(BF16)
            dgl[rows] = cdf + h * (jnp.exp(-0.5 * h * h) * (1.0 / math.sqrt(2.0 * math.pi)))

        chunks(b, 4, fn)

    def hidden_back(b):
        def fn(rows, i):
            hgr = mm(cot[rows], mat(2), 1, 0) * dgl[rows]
            low_grad = hgr.astype(BF16)
            hg[rows] = low_grad
            sg[7:8] += jnp.sum(low_grad.astype(F32), axis=0, keepdims=True)

        chunks(b, 2, fn)

    def middle_back(b):
        rows = own_rows(b)
        total = sum_end(2, b)
        zz, rstd = standardize(mid[b])
        out_grad = cot[rows].astype(F32)
        m = out_grad + norm_back(total, prm[1:2], zz, rstd)
        mgr[b] = m
        ml[rows] = m.astype(BF16)
        launch(share(ml, 1, b))
        sg[1:2] += jnp.sum(total * zz, axis=0, keepdims=True)
        sg[3:4] += jnp.sum(total, axis=0, keepdims=True)
        sg[4:5] += jnp.sum(m, axis=0, keepdims=True)
        sg[5:6] += jnp.sum(out_grad, axis=0, keepdims=True)

    def attend_back(b):
        blk = slice(b * BLK, b * BLK + BLK)
        dka[...] = jnp.zeros_like(dka)
        dva[...] = jnp.zeros_like(dva)

        def fn(rows, i):
            da = mm(ml[rows], g[0, :, :, 512:768].reshape(D, 256), 1, 0)
            d2, d01 = da[:, 0:128], da[:, 128:256]
            dos = (
                jnp.where(low, d01, 0.0).astype(BF16),
                jnp.where(low, 0.0, d01).astype(BF16),
                jnp.where(low, pltpu.roll(d2, 64, 1), 0.0).astype(BF16),
            )
            dqs = []
            for h in range(3):
                p = pr[3 * b + h, pl.ds(pl.multiple_of(i * HALF, HALF), HALF)]
                pf = p.astype(F32)
                dp = mm(dos[h], vh[h, blk], 1, 1)
                ds = (pf * (dp - jnp.sum(pf * dp, axis=-1, keepdims=True))).astype(BF16)
                dqs.append(mm(ds, kh[h, blk], 1, 0))
                dka[h] += mm(ds, qh[h, rows], 0, 0)
                dva[h] += mm(p, dos[h], 0, 0)
            dqkv[rows, 0:128] = ((dqs[0] + dqs[1]) * 0.125).astype(BF16)
            dqkv[rows, 384:512] = (dqs[2] * 0.125).astype(BF16)

        chunks(b, 2, fn)
        dqkv[blk, 128:256] = ((dka[0] + dka[1]) * 0.125).astype(BF16)
        dqkv[blk, 256:384] = (dva[0] + dva[1]).astype(BF16)
        dqkv[blk, 384:512] = (
            dqkv[blk, 384:512].astype(F32) + pltpu.roll(dka[2], 64, 1) * 0.125
        ).astype(BF16)
        dqkv[blk, 512:640] = dva[2].astype(BF16)
        sg[6:7, 0:640] += jnp.sum(dqkv[blk, 0:640].astype(F32), axis=0, keepdims=True)

    def in_part(b):
        sum_part(3, b, lambda rows: mm(dqkv[rows, 0:640], g[0, :, :, 0:640].reshape(D, 640), 1, 1))

    def out_copies(k, buf, out, b):
        mine = pltpu.make_async_copy(buf.at[b], out.at[own_rows(b)], lsem.at[2 + 2 * k + b])
        mine.start()
        later.append((mine.wait, None))
        theirs = remote(buf.at[b], out.at[own_rows(b)], oss.at[k, b], ors.at[k, b], d, sib)
        launch(theirs)
        rows = half_rows(b, 0)
        back = remote(buf.at[b], out.at[rows], oss.at[k, b], ors.at[k, b], d, sib)
        later.append((back.wait_recv, None))

    def finish_mixed(b):
        mxs[b] = (mid[b] + sum_end(1, b) + prm[5:6]).astype(BF16)
        out_copies(0, mxs, mixed_h, b)

    def finish_tokens(b):
        total = sum_end(3, b)
        zz, rstd = standardize(tok[own_rows(b)].astype(F32))
        tgs[b] = mgr[b] + norm_back(total, prm[0:1], zz, rstd)
        out_copies(1, tgs, tgrad_h, b)
        sg[0:1] += jnp.sum(total * zz, axis=0, keepdims=True)
        sg[2:3] += jnp.sum(total, axis=0, keepdims=True)

    def xred(m, k):
        return remote(gr.at[m, 2 * k + 1 - x], rx.at[m, k], rxs.at[m, k], rxr.at[m, k], xn, t)

    def zred(m, k, zd):
        return remote(
            hs.at[m, zd], rz.at[m, k - 1], rzs.at[m, k - 1], rzr.at[m, k - 1], 2 * zd + x, t
        )

    def weight_grad(m, product):
        for half in range(2):
            gr[m, 4 * half : 4 * half + 4] = (
                product(slice(384 * half, 384 * half + 384)).astype(BF16).reshape(4, PIECE, D)
            )
            if inner:
                for k in (2 * half, 2 * half + 1):
                    launch(xred(m, k))

    outs = (gra_o, gru_o, grd_o)

    def reduce_mid(m):
        if not inner:
            return
        for k in (2, 1, 3, 0):
            zd = lax.rem(z + k, 4)
            xred(m, zd).wait_recv()
            both = gr[m, 2 * zd + x].astype(F32) + rx[m, zd].astype(F32)
            if k:
                hs[m, zd] = both.astype(BF16)
                launch(zred(m, k, zd))
            else:
                outs[m][...] = both

    def reduce_end(m):
        if not inner:
            outs[m][...] = gr[m]
            return
        for k in (1, 3, 2):
            zred(m, k, lax.rem(z + k, 4)).wait_recv()
            outs[m][...] += rz[m, k - 1].astype(F32)

    def down_grad(cols):
        return mm(cot[:, cols], act[...], 0, 0)

    def up_grad(cols):
        return mm(n2[:, cols], hg[...], 0, 0)

    def in_grad(cols):
        a1 = mm(nrm[:, cols], dqkv[:, 0:640], 0, 0)
        a2 = mm(ml[:, cols], att[...], 0, 0)
        return jnp.concatenate(
            [a1[:, 0:512], a1[:, 512:640] + a2[:, 0:128], a2[:, 128:256]], axis=1
        )

    sg[...] = jnp.zeros_like(sg)
    if inner:
        gather_start(3)
        gather_start(0)
        for m in range(3):
            cp = pltpu.make_async_copy(shards[m], g.at[m, d], lsem.at[6 + m])
            cp.start()
        cp = pltpu.make_async_copy(ws, gs.at[d], lsem.at[9])
        cp.start()
        for s in (1, 2, 3):
            gather_step(3, s)
        gather_start(1)
        gather_end(3)
        for m in range(3):
            pltpu.make_async_copy(shards[m], g.at[m, d], lsem.at[6 + m]).wait()
        cp.wait()
        total = gs[0].astype(F32)
        for i in range(1, PARTS):
            total = total + gs[i].astype(F32)
        prm[...] = total
    else:
        for m in range(3):
            pltpu.make_async_copy(shards[m], g.at[m], lsem.at[6 + m]).start()
        for m in range(3):
            pltpu.make_async_copy(shards[m], g.at[m], lsem.at[6 + m]).wait()
        prm[...] = ws[...].astype(F32)

    def step(m, s):
        if inner:
            gather_step(m, s)

    step(0, 1)
    cp_tok.wait()
    cp_cot.wait()
    for b in range(nb):
        first_norm(b)
    step(0, 2)
    step(0, 3)
    if inner:
        gather_start(2)
        gather_end(0)
    pumps = [(1, 1), (1, 2), (1, 3), (2, 1), (2, 2), (2, 3)]

    def pump():
        if pumps:
            step(*pumps.pop(0))

    for b in range(nb):
        project(b)
        attend(b)
        pump()
        out_part(b)
        pump()
        sum_mid(0, b)
        pump()
    while pumps:
        pump()
    if inner:
        gather_end(1)
    for b in range(nb):
        second_norm(b)
        shared(n2, 0, b)
        up(b)
    if inner:
        gather_end(2)
    for b in range(nb):
        hidden_back(b)
        sum_part(2, b, lambda rows: mm(hg[rows], mat(1), 1, 1))
        if b > 0:
            sum_mid(2, b - 1)
    sum_mid(2, nb - 1)
    for b in range(nb):
        sum_part(1, b, lambda rows: mm(act[rows], mat(2), 1, 1))
    weight_grad(2, down_grad)
    for b in range(nb):
        sum_mid(1, b)
    weight_grad(1, up_grad)
    for b in range(nb):
        middle_back(b)
        shared(ml, 1, b)
        attend_back(b)
        in_part(b)
        if b == 0:
            reduce_mid(2)
        sum_mid(3, b)
    weight_grad(0, in_grad)
    reduce_mid(1)
    for b in range(nb):
        finish_mixed(b)
    reduce_mid(0)
    for b in range(nb):
        finish_tokens(b)
    smc = remote(sg, sgc, sms.at[0], smr.at[0], d, sib)
    smc.start()
    reduce_end(2)
    reduce_end(1)
    smc.wait()
    row = lax.broadcasted_iota(jnp.int32, (8, 1), 0)
    total = sg[...] + jnp.where(row < 6, sgc[...], 0.0)
    if inner:
        sgx[0] = total
        smx = remote(sgx.at[0], sgx.at[1], sms.at[1], smr.at[1], xn, t)
        smx.start()
        smx.wait()
        sgz[0] = sgx[0] + sgx[1]
        for k in (1, 2, 3):
            launch(remote(sgz.at[0], sgz.at[k], sms.at[1 + k], smr.at[1 + k], lax.rem(d + 2 * k, 8), t))
        reduce_end(0)
        for k in (1, 2, 3):
            remote(sgz.at[0], sgz.at[k], sms.at[1 + k], smr.at[1 + k], xn, t).wait_recv()
        small_o[...] = (sgz[0] + sgz[1]) + (sgz[2] + sgz[3])
    else:
        small_o[...] = total
        reduce_end(0)
    for wait, guard in later:
        if guard is None:
            wait()
        else:
            pl.when(guard)(wait)


def call_kernel(inner, tokens, cotangent, ws, wa, wu, wd, lens):
    rows = tokens.shape[0]
    nb = rows // BLK
    vmem = pl.BlockSpec(memory_space=pltpu.VMEM)
    anywhere = pl.BlockSpec(memory_space=pl.ANY)
    grads = (
        jax.ShapeDtypeStruct((PIECE, D), F32)
        if inner
        else jax.ShapeDtypeStruct((PARTS, PIECE, D), BF16)
    )
    dma = pltpu.SemaphoreType.DMA
    scratch = [
        pltpu.VMEM((rows, D), BF16),
        pltpu.VMEM((rows, D), BF16),
        pltpu.VMEM((3, PARTS, PIECE, D), BF16),
        pltpu.VMEM((PARTS, 16, D), BF16),
        pltpu.VMEM((16, D), F32),
        pltpu.VMEM((rows, D), BF16),
        pltpu.VMEM((3, rows, 128), BF16),
        pltpu.VMEM((3, rows, 128), BF16),
        pltpu.VMEM((3, rows, 128), BF16),
        pltpu.VMEM((3 * nb, BLK, BLK), BF16),
        pltpu.VMEM((rows, 256), BF16),
        pltpu.VMEM((nb, HALF, D), F32),
        pltpu.VMEM((rows, D), BF16),
        pltpu.VMEM((rows, D), BF16),
        pltpu.VMEM((rows, D), F32),
        pltpu.VMEM((rows, D), BF16),
        pltpu.VMEM((rows, D), BF16),
        pltpu.VMEM((nb, HALF, D), F32),
        pltpu.VMEM((rows, 640), BF16),
        pltpu.VMEM((3, BLK, 128), F32),
        pltpu.VMEM((3, BLK, 128), F32),
        pltpu.VMEM((4, nb, 2, HALF, D), BF16),
        pltpu.VMEM((4, nb, HALF, D), BF16),
        pltpu.VMEM((4, nb, HALF, D), BF16),
        pltpu.VMEM((4, nb, HALF, D), BF16),
        pltpu.VMEM((nb, HALF, D), BF16),
        pltpu.VMEM((nb, HALF, D), F32),
        pltpu.VMEM((3, PARTS, PIECE, D), BF16),
        pltpu.VMEM((3, 4, PIECE, D), BF16),
        pltpu.VMEM((3, 4, PIECE, D), BF16),
        pltpu.VMEM((3, 3, PIECE, D), BF16),
        pltpu.VMEM((8, D), F32),
        pltpu.VMEM((8, D), F32),
        pltpu.VMEM((2, 8, D), F32),
        pltpu.VMEM((4, 8, D), F32),
        dma((10,)),
        dma((4, 2, 3)),
        dma((4, 2, 3)),
        dma((4, 4)),
        dma((4, 4)),
        dma((4, nb)),
        dma((4, nb)),
        dma((4, nb)),
        dma((4, nb)),
        dma((2, nb)),
        dma((2, nb)),
        dma((2, nb)),
        dma((2, nb)),
        dma((3, 4)),
        dma((3, 4)),
        dma((3, 3)),
        dma((3, 3)),
        dma((5,)),
        dma((5,)),
    ]

    def kernel(*refs):
        layer_kernel(inner, nb, refs)

    return pl.pallas_call(
        kernel,
        out_shape=(
            jax.ShapeDtypeStruct((rows, D), BF16),
            jax.ShapeDtypeStruct((rows, D), F32),
            grads,
            grads,
            grads,
            jax.ShapeDtypeStruct((8, D), F32),
        ),
        in_specs=[anywhere, anywhere, vmem, vmem, vmem, vmem, pl.BlockSpec(memory_space=pltpu.SMEM)],
        out_specs=(anywhere, anywhere, vmem, vmem, vmem, vmem),
        scratch_shapes=scratch,
        compiler_params=pltpu.CompilerParams(
            collective_id=0, has_side_effects=True, vmem_limit_bytes=60 * 2**20
        ),
    )(tokens, cotangent, ws, wa, wu, wd, lens)


def pack_heads(q, k, v, o):
    return jnp.concatenate(
        [
            q[..., :128], k[..., :128], v[..., :128],
            q[..., 128:], k[..., 128:], v[..., 128:], o[..., 128:], o[..., :128],
        ],
        axis=-1,
    )


def unpack_heads(w):
    q = jnp.concatenate([w[..., 0:128], w[..., 384:448]], axis=-1)
    k = jnp.concatenate([w[..., 128:256], w[..., 448:512]], axis=-1)
    v = jnp.concatenate([w[..., 256:384], w[..., 512:576]], axis=-1)
    o = jnp.concatenate([w[..., 640:768], w[..., 576:640]], axis=-1)
    return q, k, v, o


def body(tokens, cotangent, w_qkv, w_out, w_up, w_down, gains, shifts, b_qkv, b_up, clip_lengths):
    own = w_up.shape[0]
    dp = D // own
    inner = dp == 8
    d = lax.axis_index("dp")
    wa = pack_heads(w_qkv[0], w_qkv[1], w_qkv[2], w_out.T)
    wu = w_up
    wd = w_down.T

    wide = jnp.concatenate([gains, shifts], axis=0)
    wide = lax.dynamic_update_slice(jnp.zeros((6, D), BF16), wide, (0, d * own))
    heads = b_qkv.shape[1]
    per_head = b_qkv.shape[2]
    full_head = per_head * dp
    bq = lax.dynamic_update_slice(
        jnp.zeros((2, heads, full_head), BF16), b_qkv, (0, 0, d * per_head)
    ).reshape(2, heads * full_head)
    none = jnp.zeros((heads * full_head,), BF16)
    bq = pack_heads(bq[0], none, bq[1], none)
    bu = lax.dynamic_update_slice(
        jnp.zeros((b_up.shape[0], b_up.shape[1] * dp), BF16), b_up, (0, d * b_up.shape[1])
    ).reshape(1, D)
    ws = jnp.concatenate([wide, bq[None], bu, jnp.zeros((8, D), BF16)], axis=0)

    if not inner:
        wa, wu, wd = (
            lax.all_gather(w, "dp", axis=0, tiled=True).reshape(PARTS, PIECE, D)
            for w in (wa, wu, wd)
        )
        ws = lax.psum(ws.astype(F32), "dp").astype(BF16)
    mixed, tgrad, ga, gu, gd, small = call_kernel(
        inner, tokens, cotangent, ws, wa, wu, wd, clip_lengths
    )
    if not inner:
        ga, gu, gd = (
            lax.psum_scatter(
                w.astype(F32).reshape(D, D), "dp", scatter_dimension=0, tiled=True
            )
            for w in (ga, gu, gd)
        )
        small = lax.psum(small, "dp")

    q, k, v, o = unpack_heads(ga)
    wide = lax.dynamic_slice(small[0:6], (0, d * own), (6, own))
    bq, _, bv, _ = unpack_heads(small[6])
    b_qkv_grad = jnp.stack([bq, bv]).reshape(2, heads, full_head)
    b_qkv_grad = lax.dynamic_slice(b_qkv_grad, (0, 0, d * per_head), (2, heads, per_head))
    b_up_grad = lax.dynamic_slice(
        small[7].reshape(b_up.shape[0], -1), (0, d * b_up.shape[1]), b_up.shape
    )
    return (
        mixed,
        tgrad,
        jnp.stack([q, k, v]),
        o.T,
        gu,
        gd.T,
        wide[0:2],
        wide[2:6],
        b_qkv_grad,
        b_up_grad,
    )


def solution(mesh):
    return jax.shard_map(
        body,
        mesh=mesh,
        in_specs=(
            P("dp", None),
            P("dp", None),
            P(None, "dp", "tp"),
            P("tp", "dp"),
            P("dp", "tp"),
            P("tp", "dp"),
            P(None, "dp"),
            P(None, "dp"),
            P(None, "tp", "dp"),
            P("tp", "dp"),
            P("dp", None),
        ),
        out_specs=(
            P("dp", None),
            P("dp", None),
            P(None, "dp", "tp"),
            P("tp", "dp"),
            P("dp", "tp"),
            P("tp", "dp"),
            P(None, "dp"),
            P(None, "dp"),
            P(None, "tp", "dp"),
            P("tp", "dp"),
        ),
        check_vma=False,
    )
```

```python
import functools
import math

import jax
import jax.numpy as jnp
from jax import lax
from jax.experimental import pallas as pl
from jax.experimental.pallas import tpu as pltpu
from jax.sharding import PartitionSpec as P

MESH = pl.DeviceIdType.MESH
F32 = jnp.float32
BF16 = jnp.bfloat16
D = 768
BLK = 512
HALF = 256
PARTS = 8
PIECE = D // PARTS
eps = 1e-06
masked = -1e30


def mm(a, b, ca, cb):
    return lax.dot_general(a, b, (((ca,), (cb,)), ((), ())), preferred_element_type=F32)


def standardize(v):
    centred = v - jnp.mean(v, axis=-1, keepdims=True)
    rstd = lax.rsqrt(jnp.mean(centred * centred, axis=-1, keepdims=True) + eps)
    return centred * rstd, rstd


def norm_back(grad, gain, z, rstd):
    n = grad * gain
    return (
        n - jnp.mean(n, axis=-1, keepdims=True) - z * jnp.mean(n * z, axis=-1, keepdims=True)
    ) * rstd


def layer_kernel(inner, nb, refs):
    if inner:
        (tok_h, cot_h, w_qkv, w_out, wu, wd, gains, shifts, b_qkv, b_up, lens) = refs[:11]
        wa, ws, wt = refs[-3:]
        refs = refs[11:-3]
    else:
        (tok_h, cot_h, ws, wa, wu, wd, lens) = refs[:7]
        refs = refs[7:]
    (mixed_h, tgrad_h, gra_o, gru_o, grd_o, small_o) = refs[:6]
    (
        tok, cot, g, gs, prm, nrm, qh, kh, vh, pr, att, mid, n2, act, dgl, hg, ml, mgr, dqkv,
        dka, dva, pb, rc, sy, ry, mxs, tgs, gr, rx, hs, rz, sg, sgc, sgx, sgz,
        lsem, zss, zrs, xss, xrs, css, crs, yss, yrs, nss, nrs, oss, ors, rxs, rxr, rzs, rzr, sms, smr,
    ) = refs[6:]
    d = lax.axis_index("dp")
    t = lax.axis_index("tp")
    z = d // 2
    x = d % 2
    c = t % 2
    xn = d + 1 - 2 * x
    sib = t + 1 - 2 * c
    yn = lax.rem(t + 2, 4)
    later = []

    def remote(src, dst, s, r, dd, tt):
        return pltpu.make_async_remote_copy(
            src_ref=src, dst_ref=dst, send_sem=s, recv_sem=r, device_id=(dd, tt), device_id_type=MESH
        )

    def launch(copy, guard=None):
        if guard is None:
            copy.start()
        else:
            pl.when(guard)(copy.start)
        later.append((copy.wait_send, guard))

    bar = pltpu.get_barrier_semaphore()
    greet = [(d, sib), (d, yn)] + ([(xn, t)] if inner else [])
    greeted = len(greet)
    for who in greet:
        pl.semaphore_signal(bar, 1, device_id=who, device_id_type=MESH)
    if inner:
        for guard, who in ((z < 3, d + 2), (z > 0, d - 2)):

            @pl.when(guard)
            def _():
                pl.semaphore_signal(bar, 1, device_id=(who, t), device_id_type=MESH)

            greeted = greeted + guard.astype(jnp.int32)
    cp_tok = pltpu.make_async_copy(tok_h, tok, lsem.at[0])
    cp_tok.start()
    cp_cot = pltpu.make_async_copy(cot_h, cot, lsem.at[1])
    cp_cot.start()
    if inner:
        def spot(rows, shift):
            i = lax.broadcasted_iota(jnp.int32, (rows, 128), 0)
            return (lax.broadcasted_iota(jnp.int32, (rows, 128), 1) == i + shift).astype(F32).astype(BF16)

        for k in range(3):
            wa[:, 128 * k : 128 * k + 128] = w_qkv[k, :, 0:128]
        q2, k2, v2 = (w_qkv[k, :, 128:192] for k in range(3))
        wa[:, 384:512] = (mm(q2, spot(64, 0), 1, 0) + mm(k2, spot(64, 64), 1, 0)).astype(BF16)
        wa[:, 512:640] = (
            mm(v2, spot(64, 0), 1, 0) + mm(w_out[128:192, :], spot(64, 64), 0, 0)
        ).astype(BF16)
        wa[:, 640:768] = mm(w_out[0:128, :], spot(128, 0), 0, 0).astype(BF16)
        own = gains.shape[1]
        wt[...] = jnp.zeros_like(wt)
        wt[0:2, 0:own] = gains[...].astype(F32)
        wt[2:6, 0:own] = shifts[...].astype(F32)
        wide = pltpu.roll(wt[0:8], d * own, 1)
        wt[...] = jnp.zeros_like(wt)
        wt[0:8] = wide
        per = b_up.shape[1]
        sg[...] = jnp.zeros_like(sg)
        sg[0:6, 0:per] = b_up[...].astype(F32)
        turned = pltpu.roll(sg[0:8, 0:128], d * per, 1)
        for k in range(6):
            wt[7:8, 128 * k : 128 * k + 128] = turned[k : k + 1]
        per = b_qkv.shape[2]
        sg[...] = jnp.zeros_like(sg)
        for h in range(3):
            sg[h : h + 1, 0:per] = b_qkv[h, 0:1].astype(F32)
            sg[3 + h : 4 + h, 0:per] = b_qkv[h, 1:2].astype(F32)
        turned = pltpu.roll(sg[0:8, 0:128], d * per, 1)
        other = pltpu.roll(turned, 64, 1)
        wt[6:7, 0:128] = turned[0:1] + other[1:2]
        wt[6:7, 256:384] = turned[3:4] + other[4:5]
        wt[6:7, 384:512] = turned[2:3]
        wt[6:7, 512:640] = turned[5:6]
        ws[...] = wt[...].astype(BF16)
    pl.semaphore_wait(bar, greeted)

    shards = (wa, wu, wd, ws)

    def slot(m, i):
        return gs.at[i] if m == 3 else g.at[m, i]

    def zcopy(m, side, src, i, s):
        return remote(src, slot(m, i), zss.at[m, side, s], zrs.at[m, side, s], d + 2 - 4 * side, t)

    def xcopy(m, src, i, zsrc):
        return remote(src, slot(m, i), xss.at[m, zsrc], xrs.at[m, zsrc], xn, t)

    def gather_z(m):
        launch(zcopy(m, 0, shards[m], d, 0), z < 3)
        launch(zcopy(m, 1, shards[m], d, 0), z > 0)

    def gather_x(m):
        launch(xcopy(m, shards[m], d, z))

    def gather_step(m, s):
        for side in (0, 1):
            i = d - 2 * s if side == 0 else d + 2 * s
            here = z >= s if side == 0 else z + s <= 3
            onward = z < 3 if side == 0 else z > 0

            @pl.when(here)
            def _():
                zcopy(m, side, slot(m, i), i, s - 1).wait_recv()

            if s < 3:
                launch(zcopy(m, side, slot(m, i), i, s), jnp.logical_and(here, onward))
            launch(xcopy(m, slot(m, i), i, i // 2), here)

    def gather_end(m):
        for k in range(4):
            i = 2 * k + 1 - x
            xcopy(m, slot(m, i), i, k).wait_recv()

    def half_rows(b, j):
        return pl.ds(pl.multiple_of(b * BLK + lax.rem(1 - c + j, 2) * HALF, HALF), HALF)

    def own_rows(b):
        return pl.ds(pl.multiple_of(b * BLK + c * HALF, HALF), HALF)

    def ccopy(st, b):
        return remote(pb.at[st, b, 0], rc.at[st, b], css.at[st, b], crs.at[st, b], d, sib)

    def ycopy(st, b):
        return remote(sy.at[st, b], ry.at[st, b], yss.at[st, b], yrs.at[st, b], d, yn)

    def sum_part(st, b, product):
        def one(j, carry):
            pb[st, b, j] = product(half_rows(b, j)).astype(BF16)

            @pl.when(j == 0)
            def _():
                ccopy(st, b).start()

            return carry

        lax.fori_loop(0, 2, one, 0)
        later.append((ccopy(st, b).wait_send, None))

    def sum_mid(st, b):
        ccopy(st, b).wait_recv()
        sy[st, b] = (pb[st, b, 1].astype(F32) + rc[st, b].astype(F32)).astype(BF16)
        launch(ycopy(st, b))

    def sum_end(st, b):
        ycopy(st, b).wait_recv()
        return sy[st, b].astype(F32) + ry[st, b].astype(F32)

    def share(buf, k, b):
        return remote(buf.at[own_rows(b)], buf.at[own_rows(b)], nss.at[k, b], nrs.at[k, b], d, sib)

    def shared(buf, k, b):
        rows = half_rows(b, 0)
        remote(buf.at[rows], buf.at[rows], nss.at[k, b], nrs.at[k, b], d, sib).wait_recv()

    lane = lax.broadcasted_iota(jnp.int32, (1, 128), 1)
    low = lane < 64

    def mat(m):
        return g[m].reshape(D, D)

    def chunks(b, n, fn):
        def one(i, carry):
            fn(pl.ds(pl.multiple_of(b * BLK + i * (BLK // n), BLK // n), BLK // n), i)
            return carry

        lax.fori_loop(0, n, one, 0)

    def first_norm(b):
        def fn(rows, i):
            zz, _ = standardize(tok[rows].astype(F32))
            nrm[rows] = (zz * prm[0:1] + prm[2:3]).astype(BF16)

        chunks(b, 4, fn)

    def project(b):
        def fn(rows, i):
            p = mm(nrm[rows], mat(0), 1, 0) + prm[6:7]
            s0, s1, s2, s3, s4 = (p[:, 128 * k : 128 * k + 128] for k in range(5))
            for ref, s in ((qh, s0), (kh, s1), (vh, s2)):
                ref[0, rows] = jnp.where(low, s, 0.0).astype(BF16)
                ref[1, rows] = jnp.where(low, 0.0, s).astype(BF16)
            qh[2, rows] = jnp.where(low, s3, 0.0).astype(BF16)
            kh[2, rows] = jnp.where(low, pltpu.roll(s3, 64, 1), 0.0).astype(BF16)
            vh[2, rows] = jnp.where(low, s4, 0.0).astype(BF16)

        chunks(b, 2, fn)

    def attend(b):
        blk = slice(b * BLK, b * BLK + BLK)
        e0 = lens[b, 0]
        e1 = e0 + lens[b, 1]
        e2 = e1 + lens[b, 2]

        def clip_of(pos):
            return (
                (pos >= e0).astype(jnp.int32)
                + (pos >= e1).astype(jnp.int32)
                + (pos >= e2).astype(jnp.int32)
            )

        def fn(rows, i):
            q_clip = clip_of(lax.broadcasted_iota(jnp.int32, (HALF, 1), 0) + i * HALF)
            k_clip = clip_of(lax.broadcasted_iota(jnp.int32, (1, BLK), 1))
            same = q_clip == k_clip
            outs = []
            for h in range(3):
                s = mm(qh[h, rows], kh[h, blk], 1, 1) * 0.125
                s = jnp.where(same, s, masked)
                e = jnp.exp(s - jnp.max(s, axis=-1, keepdims=True))
                p = (e / jnp.sum(e, axis=-1, keepdims=True)).astype(BF16)
                pr[3 * b + h, pl.ds(pl.multiple_of(i * HALF, HALF), HALF)] = p
                outs.append(mm(p, vh[h, blk], 1, 0))
            att[rows, 0:128] = pltpu.roll(outs[2], 64, 1).astype(BF16)
            att[rows, 128:256] = (outs[0] + outs[1]).astype(BF16)

        chunks(b, 2, fn)

    def out_part(b):
        sum_part(0, b, lambda rows: mm(att[rows], g[0, :, :, 512:768].reshape(D, 256), 1, 1))

    def second_norm(b):
        rows = own_rows(b)
        m = tok[rows].astype(F32) + sum_end(0, b) + prm[4:5]
        mid[b] = m
        zz, _ = standardize(m)
        n2[rows] = (zz * prm[1:2] + prm[3:4]).astype(BF16)
        launch(share(n2, 0, b))

    def up(b):
        def fn(rows, i):
            h = mm(n2[rows], mat(1), 1, 0) + prm[7:8]
            cdf = 0.5 * (1.0 + lax.erf(h * (1.0 / math.sqrt(2.0))))
            act[rows] = (h * cdf).astype(BF16)
            dgl[rows] = cdf + h * (jnp.exp(-0.5 * h * h) * (1.0 / math.sqrt(2.0 * math.pi)))

        chunks(b, 4, fn)

    def hidden_back(b):
        def fn(rows, i):
            hgr = mm(cot[rows], mat(2), 1, 0) * dgl[rows]
            low_grad = hgr.astype(BF16)
            hg[rows] = low_grad
            sg[7:8] += jnp.sum(low_grad.astype(F32), axis=0, keepdims=True)

        chunks(b, 2, fn)

    def middle_back(b):
        rows = own_rows(b)
        total = sum_end(2, b)
        zz, rstd = standardize(mid[b])
        out_grad = cot[rows].astype(F32)
        m = out_grad + norm_back(total, prm[1:2], zz, rstd)
        mgr[b] = m
        ml[rows] = m.astype(BF16)
        launch(share(ml, 1, b))
        sg[1:2] += jnp.sum(total * zz, axis=0, keepdims=True)
        sg[3:4] += jnp.sum(total, axis=0, keepdims=True)
        sg[4:5] += jnp.sum(m, axis=0, keepdims=True)
        sg[5:6] += jnp.sum(out_grad, axis=0, keepdims=True)

    def attend_back(b):
        blk = slice(b * BLK, b * BLK + BLK)
        dka[...] = jnp.zeros_like(dka)
        dva[...] = jnp.zeros_like(dva)

        def fn(rows, i):
            da = mm(ml[rows], g[0, :, :, 512:768].reshape(D, 256), 1, 0)
            d2, d01 = da[:, 0:128], da[:, 128:256]
            dos = (
                jnp.where(low, d01, 0.0).astype(BF16),
                jnp.where(low, 0.0, d01).astype(BF16),
                jnp.where(low, pltpu.roll(d2, 64, 1), 0.0).astype(BF16),
            )
            dqs = []
            for h in range(3):
                p = pr[3 * b + h, pl.ds(pl.multiple_of(i * HALF, HALF), HALF)]
                pf = p.astype(F32)
                dp = mm(dos[h], vh[h, blk], 1, 1)
                ds = (pf * (dp - jnp.sum(pf * dp, axis=-1, keepdims=True))).astype(BF16)
                dqs.append(mm(ds, kh[h, blk], 1, 0))
                dka[h] += mm(ds, qh[h, rows], 0, 0)
                dva[h] += mm(p, dos[h], 0, 0)
            dqkv[rows, 0:128] = ((dqs[0] + dqs[1]) * 0.125).astype(BF16)
            dqkv[rows, 384:512] = (dqs[2] * 0.125).astype(BF16)

        chunks(b, 2, fn)
        dqkv[blk, 128:256] = ((dka[0] + dka[1]) * 0.125).astype(BF16)
        dqkv[blk, 256:384] = (dva[0] + dva[1]).astype(BF16)
        dqkv[blk, 384:512] = (
            dqkv[blk, 384:512].astype(F32) + pltpu.roll(dka[2], 64, 1) * 0.125
        ).astype(BF16)
        dqkv[blk, 512:640] = dva[2].astype(BF16)
        sg[6:7, 0:640] += jnp.sum(dqkv[blk, 0:640].astype(F32), axis=0, keepdims=True)

    def in_part(b):
        def product(rows):
            part = mm(dqkv[rows, 0:640], g[0, :, :, 0:640].reshape(D, 640), 1, 1)
            zz, _ = standardize(tok[rows].astype(F32))
            sg[0:1] += jnp.sum(part * zz, axis=0, keepdims=True)
            sg[2:3] += jnp.sum(part, axis=0, keepdims=True)
            return part

        sum_part(3, b, product)

    def out_copies(k, buf, out, b):
        mine = pltpu.make_async_copy(buf.at[b], out.at[own_rows(b)], lsem.at[2 + 2 * k + b])
        mine.start()
        later.append((mine.wait, None))
        theirs = remote(buf.at[b], out.at[own_rows(b)], oss.at[k, b], ors.at[k, b], d, sib)
        launch(theirs)
        rows = half_rows(b, 0)
        back = remote(buf.at[b], out.at[rows], oss.at[k, b], ors.at[k, b], d, sib)
        later.append((back.wait_recv, None))

    def finish_mixed(b):
        mxs[b] = (mid[b] + sum_end(1, b) + prm[5:6]).astype(BF16)
        out_copies(0, mxs, mixed_h, b)

    def finish_tokens(b):
        total = sum_end(3, b)
        zz, rstd = standardize(tok[own_rows(b)].astype(F32))
        tgs[b] = mgr[b] + norm_back(total, prm[0:1], zz, rstd)
        out_copies(1, tgs, tgrad_h, b)

    def xred(m, k):
        return remote(gr.at[m, 2 * k + 1 - x], rx.at[m, k], rxs.at[m, k], rxr.at[m, k], xn, t)

    def zred(m, k, zd):
        return remote(
            hs.at[m, zd], rz.at[m, k - 1], rzs.at[m, k - 1], rzr.at[m, k - 1], 2 * zd + x, t
        )

    def weight_grad(m, product):
        for half in range(2):
            gr[m, 4 * half : 4 * half + 4] = (
                product(slice(384 * half, 384 * half + 384)).astype(BF16).reshape(4, PIECE, D)
            )
            if inner:
                for k in (2 * half, 2 * half + 1):
                    launch(xred(m, k))

    outs = (gra_o, gru_o, grd_o)

    def reduce_mid(m):
        if not inner:
            return
        for k in (2, 1, 3, 0):
            zd = lax.rem(z + k, 4)
            xred(m, zd).wait_recv()
            both = gr[m, 2 * zd + x].astype(F32) + rx[m, zd].astype(F32)
            if k:
                hs[m, zd] = both.astype(BF16)
                launch(zred(m, k, zd))
            else:
                outs[m][...] = both

    def reduce_end(m):
        if not inner:
            outs[m][...] = gr[m]
            return
        for k in (1, 3, 2):
            zred(m, k, lax.rem(z + k, 4)).wait_recv()
            outs[m][...] += rz[m, k - 1].astype(F32)

    def down_grad(cols):
        return mm(cot[:, cols], act[...], 0, 0)

    def up_grad(cols):
        return mm(n2[:, cols], hg[...], 0, 0)

    def in_grad(cols):
        a1 = mm(nrm[:, cols], dqkv[:, 0:640], 0, 0)
        a2 = mm(ml[:, cols], att[...], 0, 0)
        return jnp.concatenate(
            [a1[:, 0:512], a1[:, 512:640] + a2[:, 0:128], a2[:, 128:256]], axis=1
        )

    row = lax.broadcasted_iota(jnp.int32, (8, 1), 0)

    def small_c():
        return remote(sg, sgc.at[0], sms.at[0], smr.at[0], d, sib)

    def small_y():
        return remote(sgc.at[1], sgc.at[2], sms.at[1], smr.at[1], d, yn)

    def small_x():
        return remote(sgx.at[0], sgx.at[1], sms.at[2], smr.at[2], xn, t)

    def small_z(k):
        return remote(
            sgz.at[0], sgz.at[k], sms.at[2 + k], smr.at[2 + k], lax.rem(d + 2 * k, 8), t
        )

    def small_step(n):
        if n == 0:
            launch(small_c())
        elif n == 1:
            small_c().wait_recv()
            sgc[1] = sg[...] + jnp.where(row < 6, sgc[0], 0.0)
            launch(small_y())
        elif n == 2:
            small_y().wait_recv()
            both = sgc[1] + jnp.where(jnp.logical_or(row == 0, row == 2), sgc[2], 0.0)
            if inner:
                sgx[0] = both
                launch(small_x())
            else:
                small_o[...] = both
        elif n == 3 and inner:
            small_x().wait_recv()
            sgz[0] = sgx[0] + sgx[1]
            for k in (1, 2, 3):
                launch(small_z(k))
        elif n == 4 and inner:
            for k in (1, 2, 3):
                small_z(k).wait_recv()
            small_o[...] = (sgz[0] + sgz[1]) + (sgz[2] + sgz[3])

    sg[...] = jnp.zeros_like(sg)
    own_pieces = []
    for m in range(3 if not inner else 4):
        own_pieces.append(
            pltpu.make_async_copy(shards[m], slot(m, d) if inner else g.at[m], lsem.at[6 + m])
        )

    def add_parameters():
        if inner:
            own_pieces[3].wait()
            gather_end(3)
            total = gs[0].astype(F32)
            for i in range(1, PARTS):
                total = total + gs[i].astype(F32)
            prm[...] = total
        else:
            prm[...] = ws[...].astype(F32)

    def step(m, s):
        if inner:
            gather_step(m, s)

    if inner:
        for m in (0, 3):
            gather_z(m)
            gather_x(m)
    for cp in own_pieces:
        cp.start()
    step(0, 1)
    step(3, 1)
    step(0, 2)
    step(3, 2)
    if inner:
        gather_z(1)
    step(0, 3)
    step(3, 3)
    if inner:
        gather_x(1)
    add_parameters()
    cp_tok.wait()
    first_norm(0)
    step(1, 1)
    if inner:
        gather_z(2)
    for b in range(1, nb):
        first_norm(b)
    for cp in own_pieces[:3]:
        cp.wait()
    if inner:
        gather_end(0)
    step(1, 2)
    for b in range(nb):
        project(b)
        if b:
            sum_mid(0, b - 1)
            step(2, 1)
        else:
            step(1, 3)
            if inner:
                gather_x(2)
        attend(b)
        out_part(b)
    cp_cot.wait()
    sum_mid(0, nb - 1)
    step(2, 2)
    step(2, 3)
    if inner:
        gather_end(1)
    for b in range(nb):
        second_norm(b)
        shared(n2, 0, b)
        up(b)
        if inner and b == 0:
            gather_end(2)
        hidden_back(b)
        sum_part(2, b, lambda rows: mm(hg[rows], mat(1), 1, 1))
        if b == 0:
            sum_part(1, b, lambda rows: mm(act[rows], mat(2), 1, 1))
        sum_mid(2, b)
    sum_mid(1, 0)
    weight_grad(2, down_grad)
    for b in range(1, nb):
        sum_part(1, b, lambda rows: mm(act[rows], mat(2), 1, 1))
    weight_grad(1, up_grad)
    for b in range(nb):
        middle_back(b)
        shared(ml, 1, b)
        attend_back(b)
        if b == nb - 1:
            weight_grad(0, in_grad)
        in_part(b)
        if b == nb - 1:
            small_step(0)
            small_step(1)
        sum_mid(3, b)
        if b == 0:
            reduce_mid(2)
    for b in range(1, nb):
        sum_mid(1, b)
    reduce_mid(1)
    finish_mixed(0)
    finish_tokens(0)
    small_step(2)
    reduce_mid(0)
    for b in range(1, nb):
        finish_tokens(b)
    small_step(3)
    reduce_end(2)
    reduce_end(1)
    small_step(4)
    reduce_end(0)
    for b in range(1, nb):
        finish_mixed(b)
    for wait, guard in later:
        if guard is None:
            wait()
        else:
            pl.when(guard)(wait)


def call_kernel(inner, *args):
    rows = args[0].shape[0]
    nb = rows // BLK
    vmem = pl.BlockSpec(memory_space=pltpu.VMEM)
    anywhere = pl.BlockSpec(memory_space=pl.ANY)
    grads = (
        jax.ShapeDtypeStruct((PIECE, D), F32)
        if inner
        else jax.ShapeDtypeStruct((PARTS, PIECE, D), BF16)
    )
    dma = pltpu.SemaphoreType.DMA
    scratch = [
        pltpu.VMEM((rows, D), BF16),
        pltpu.VMEM((rows, D), BF16),
        pltpu.VMEM((3, PARTS, PIECE, D), BF16),
        pltpu.VMEM((PARTS, 16, D), BF16),
        pltpu.VMEM((16, D), F32),
        pltpu.VMEM((rows, D), BF16),
        pltpu.VMEM((3, rows, 128), BF16),
        pltpu.VMEM((3, rows, 128), BF16),
        pltpu.VMEM((3, rows, 128), BF16),
        pltpu.VMEM((3 * nb, BLK, BLK), BF16),
        pltpu.VMEM((rows, 256), BF16),
        pltpu.VMEM((nb, HALF, D), F32),
        pltpu.VMEM((rows, D), BF16),
        pltpu.VMEM((rows, D), BF16),
        pltpu.VMEM((rows, D), F32),
        pltpu.VMEM((rows, D), BF16),
        pltpu.VMEM((rows, D), BF16),
        pltpu.VMEM((nb, HALF, D), F32),
        pltpu.VMEM((rows, 640), BF16),
        pltpu.VMEM((3, BLK, 128), F32),
        pltpu.VMEM((3, BLK, 128), F32),
        pltpu.VMEM((4, nb, 2, HALF, D), BF16),
        pltpu.VMEM((4, nb, HALF, D), BF16),
        pltpu.VMEM((4, nb, HALF, D), BF16),
        pltpu.VMEM((4, nb, HALF, D), BF16),
        pltpu.VMEM((nb, HALF, D), BF16),
        pltpu.VMEM((nb, HALF, D), F32),
        pltpu.VMEM((3, PARTS, PIECE, D), BF16),
        pltpu.VMEM((3, 4, PIECE, D), BF16),
        pltpu.VMEM((3, 4, PIECE, D), BF16),
        pltpu.VMEM((3, 3, PIECE, D), BF16),
        pltpu.VMEM((8, D), F32),
        pltpu.VMEM((3, 8, D), F32),
        pltpu.VMEM((2, 8, D), F32),
        pltpu.VMEM((4, 8, D), F32),
        dma((10,)),
        dma((4, 2, 3)),
        dma((4, 2, 3)),
        dma((4, 4)),
        dma((4, 4)),
        dma((4, nb)),
        dma((4, nb)),
        dma((4, nb)),
        dma((4, nb)),
        dma((2, nb)),
        dma((2, nb)),
        dma((2, nb)),
        dma((2, nb)),
        dma((3, 4)),
        dma((3, 4)),
        dma((3, 3)),
        dma((3, 3)),
        dma((6,)),
        dma((6,)),
    ]
    if inner:
        scratch += [pltpu.VMEM((PIECE, D), BF16), pltpu.VMEM((16, D), BF16), pltpu.VMEM((16, D), F32)]

    def kernel(*refs):
        layer_kernel(inner, nb, refs)

    return pl.pallas_call(
        kernel,
        out_shape=(
            jax.ShapeDtypeStruct((rows, D), BF16),
            jax.ShapeDtypeStruct((rows, D), F32),
            grads,
            grads,
            grads,
            jax.ShapeDtypeStruct((8, D), F32),
        ),
        in_specs=[anywhere, anywhere]
        + ([vmem, vmem, anywhere, anywhere, vmem, vmem, vmem, vmem] if inner else [vmem] * 4)
        + [pl.BlockSpec(memory_space=pltpu.SMEM)],
        out_specs=(anywhere, anywhere, vmem, vmem, vmem, vmem),
        scratch_shapes=scratch,
        compiler_params=pltpu.CompilerParams(
            collective_id=0, has_side_effects=True, vmem_limit_bytes=60 * 2**20
        ),
    )(*args)


def pack_heads(q, k, v, o):
    return jnp.concatenate(
        [
            q[..., :128], k[..., :128], v[..., :128],
            q[..., 128:], k[..., 128:], v[..., 128:], o[..., 128:], o[..., :128],
        ],
        axis=-1,
    )


def unpack_heads(w):
    q = jnp.concatenate([w[..., 0:128], w[..., 384:448]], axis=-1)
    k = jnp.concatenate([w[..., 128:256], w[..., 448:512]], axis=-1)
    v = jnp.concatenate([w[..., 256:384], w[..., 512:576]], axis=-1)
    o = jnp.concatenate([w[..., 640:768], w[..., 576:640]], axis=-1)
    return q, k, v, o


def unpack_kernel(mix_h, tok_h, ga, gu, gd, small, mix_o, tok_o, qkv_o, out_o, up_o, down_o, gains_o, shifts_o, bqkv_o, bup_o, tok_v, mix_v, sem):
    d = lax.axis_index("dp")
    moves = []
    for src, via, dst in ((tok_h, tok_v, tok_o), (mix_h, mix_v, mix_o)):
        for k in range(4):
            rows = slice(k * src.shape[0] // 4, (k + 1) * src.shape[0] // 4)
            sems = sem.at[len(moves)]
            load = pltpu.make_async_copy(src.at[rows], via.at[rows], sems)
            load.start()
            moves.append((load, pltpu.make_async_copy(via.at[rows], dst.at[rows], sems)))
    for load, store in moves:
        load.wait()
        store.start()
    own = gains_o.shape[1]
    for k in range(3):
        qkv_o[k, :, 0:128] = ga[:, 128 * k : 128 * k + 128]
    qkv_o[0, :, 128:192] = ga[:, 384:448]
    qkv_o[1, :, 128:192] = pltpu.roll(ga[:, 384:512], 64, 1)[:, 0:64]
    qkv_o[2, :, 128:192] = ga[:, 512:576]
    fill = jnp.zeros((128 - own, 128), F32)
    out_o[0:128, :] = jnp.concatenate([ga[:, 640:768], fill], axis=0).T[:, 0:own]
    out_o[128:192, :] = jnp.concatenate([ga[:, 512:640], fill], axis=0).T[64:128, 0:own]
    up_o[...] = gu[...]
    down_o[...] = gd[...]
    wide = pltpu.roll(small[...], D - d * own, 1)
    gains_o[...] = wide[0:2, 0:own]
    shifts_o[...] = wide[2:6, 0:own]
    for part in range(2):
        for h, at in enumerate((0, 64, 384) if part == 0 else (256, 320, 512)):
            per = bqkv_o.shape[2]
            slab = small[:, at // 128 * 128 : at // 128 * 128 + 128]
            turned = pltpu.roll(slab, 128 - at % 128 - d * per + 128 * (at % 128 // 64), 1)
            bqkv_o[h, part : part + 1, :] = turned[6:7, 0:per]
    for k in range(6):
        per = bup_o.shape[1]
        turned = pltpu.roll(small[:, 128 * k : 128 * k + 128], 128 - d * per, 1)
        bup_o[k : k + 1, :] = turned[7:8, 0:per]
    for _, store in moves:
        store.wait()


def body(tokens, cotangent, w_qkv, w_out, w_up, w_down, gains, shifts, b_qkv, b_up, clip_lengths):
    own = w_up.shape[0]
    dp = D // own
    if dp == 8:
        mixed, tgrad, ga, gu, gd, small = call_kernel(
            True, tokens, cotangent, w_qkv, w_out, w_up, w_down.T,
            gains, shifts, b_qkv.transpose(1, 0, 2), b_up, clip_lengths,
        )
        vmem = pl.BlockSpec(memory_space=pltpu.VMEM)
        anywhere = pl.BlockSpec(memory_space=pl.ANY)
        like = [mixed, tgrad, w_qkv, w_out, gu, gd, gains, shifts, b_qkv.transpose(1, 0, 2), b_up]
        outs = pl.pallas_call(
            unpack_kernel,
            out_shape=tuple(
                jax.ShapeDtypeStruct(a.shape, BF16 if i == 0 else F32) for i, a in enumerate(like)
            ),
            in_specs=[anywhere, anywhere] + [vmem] * 4,
            out_specs=tuple([anywhere, anywhere] + [vmem] * 8),
            scratch_shapes=[
                pltpu.VMEM(tgrad.shape, F32),
                pltpu.VMEM(mixed.shape, BF16),
                pltpu.SemaphoreType.DMA((8,)),
            ],
        )(mixed, tgrad, ga, gu, gd, small)
        return outs[:5] + (outs[5].T, outs[6], outs[7], outs[8].transpose(1, 0, 2), outs[9])

    d = lax.axis_index("dp")
    wide = jnp.concatenate([gains, shifts], axis=0)
    wide = lax.dynamic_update_slice(jnp.zeros((6, D), BF16), wide, (0, d * own))
    heads = b_qkv.shape[1]
    per_head = b_qkv.shape[2]
    full_head = per_head * dp
    bq = lax.dynamic_update_slice(
        jnp.zeros((2, heads, full_head), BF16), b_qkv, (0, 0, d * per_head)
    ).reshape(2, heads * full_head)
    none = jnp.zeros((heads * full_head,), BF16)
    bq = pack_heads(bq[0], none, bq[1], none)
    bu = lax.dynamic_update_slice(
        jnp.zeros((b_up.shape[0], b_up.shape[1] * dp), BF16), b_up, (0, d * b_up.shape[1])
    ).reshape(1, D)
    ws = jnp.concatenate([wide, bq[None], bu, jnp.zeros((8, D), BF16)], axis=0)
    ws = lax.psum(ws.astype(F32), "dp").astype(BF16)
    wa = pack_heads(w_qkv[0], w_qkv[1], w_qkv[2], w_out.T)
    wa, wu, wd = (
        lax.all_gather(w, "dp", axis=0, tiled=True).reshape(PARTS, PIECE, D)
        for w in (wa, w_up, w_down.T)
    )
    mixed, tgrad, ga, gu, gd, small = call_kernel(
        False, tokens, cotangent, ws, wa, wu, wd, clip_lengths
    )
    ga, gu, gd = (
        lax.psum_scatter(w.astype(F32).reshape(D, D), "dp", scatter_dimension=0, tiled=True)
        for w in (ga, gu, gd)
    )
    small = lax.psum(small, "dp")
    q, k, v, o = unpack_heads(ga)
    wide = lax.dynamic_slice(small[0:6], (0, d * own), (6, own))
    bq, _, bv, _ = unpack_heads(small[6])
    b_qkv_grad = jnp.stack([bq, bv]).reshape(2, heads, full_head)
    b_qkv_grad = lax.dynamic_slice(b_qkv_grad, (0, 0, d * per_head), (2, heads, per_head))
    b_up_grad = lax.dynamic_slice(
        small[7].reshape(b_up.shape[0], -1), (0, d * b_up.shape[1]), b_up.shape
    )
    return (
        mixed,
        tgrad,
        jnp.stack([q, k, v]),
        o.T,
        gu,
        gd.T,
        wide[0:2],
        wide[2:6],
        b_qkv_grad,
        b_up_grad,
    )


def solution(mesh):
    return jax.shard_map(
        body,
        mesh=mesh,
        in_specs=(
            P("dp", None),
            P("dp", None),
            P(None, "dp", "tp"),
            P("tp", "dp"),
            P("dp", "tp"),
            P("tp", "dp"),
            P(None, "dp"),
            P(None, "dp"),
            P(None, "tp", "dp"),
            P("tp", "dp"),
            P("dp", None),
        ),
        out_specs=(
            P("dp", None),
            P("dp", None),
            P(None, "dp", "tp"),
            P("tp", "dp"),
            P("dp", "tp"),
            P("tp", "dp"),
            P(None, "dp"),
            P(None, "dp"),
            P(None, "tp", "dp"),
            P("tp", "dp"),
        ),
        check_vma=False,
    )
```

```python
import functools
import math

import jax
import jax.numpy as jnp
from jax import lax
from jax.experimental import pallas as pl
from jax.experimental.pallas import tpu as pltpu
from jax.sharding import PartitionSpec as P

MESH = pl.DeviceIdType.MESH
F32 = jnp.float32
BF16 = jnp.bfloat16
D = 768
BLK = 512
HALF = 256
PARTS = 8
PIECE = D // PARTS
eps = 1e-06
masked = -1e30


def mm(a, b, ca, cb):
    return lax.dot_general(a, b, (((ca,), (cb,)), ((), ())), preferred_element_type=F32)


def standardize(v):
    centred = v - jnp.mean(v, axis=-1, keepdims=True)
    rstd = lax.rsqrt(jnp.mean(centred * centred, axis=-1, keepdims=True) + eps)
    return centred * rstd, rstd


def norm_back(grad, gain, z, rstd):
    n = grad * gain
    return (
        n - jnp.mean(n, axis=-1, keepdims=True) - z * jnp.mean(n * z, axis=-1, keepdims=True)
    ) * rstd


def layer_kernel(inner, nb, refs):
    if inner:
        (tok_h, cot_h, w_qkv, w_out, wu, wd, gains, shifts, b_qkv, b_up, lens) = refs[:11]
        wa, ws, wt = refs[-3:]
        refs = refs[11:-3]
    else:
        (tok_h, cot_h, ws, wa, wu, wd, lens) = refs[:7]
        refs = refs[7:]
    (mixed_h, tgrad_h, gra_o, gru_o, grd_o, small_o) = refs[:6]
    (
        tok, cot, g, gs, prm, nrm, qh, kh, vh, pr, att, mid, n2, act, dgl, hg, ml, mgr, dqkv,
        dka, dva, pb, rc, ry, mxs, gr, rx, hs, rz, sg, sgc, sgx, sgz,
        lsem, zss, zrs, xss, xrs, css, crs, yss, yrs, nss, nrs, oss, ors, rxs, rxr, rzs, rzr, sms, smr,
    ) = refs[6:]
    d = lax.axis_index("dp")
    t = lax.axis_index("tp")
    z = d // 2
    x = d % 2
    c = t % 2
    xn = d + 1 - 2 * x
    sib = t + 1 - 2 * c
    yn = lax.rem(t + 2, 4)
    later = []

    def remote(src, dst, s, r, dd, tt):
        return pltpu.make_async_remote_copy(
            src_ref=src, dst_ref=dst, send_sem=s, recv_sem=r, device_id=(dd, tt), device_id_type=MESH
        )

    def launch(copy, guard=None):
        if guard is None:
            copy.start()
        else:
            pl.when(guard)(copy.start)
        later.append((copy.wait_send, guard))

    bar = pltpu.get_barrier_semaphore()
    greet = [(d, sib), (d, yn)] + ([(xn, t)] if inner else [])
    greeted = len(greet)
    for who in greet:
        pl.semaphore_signal(bar, 1, device_id=who, device_id_type=MESH)
    if inner:
        for guard, who in ((z < 3, d + 2), (z > 0, d - 2)):

            @pl.when(guard)
            def _():
                pl.semaphore_signal(bar, 1, device_id=(who, t), device_id_type=MESH)

            greeted = greeted + guard.astype(jnp.int32)
    cp_tok = pltpu.make_async_copy(tok_h, tok, lsem.at[0])
    cp_tok.start()
    cp_cot = pltpu.make_async_copy(cot_h, cot, lsem.at[1])
    cp_cot.start()
    if inner:
        def spot(rows, shift):
            i = lax.broadcasted_iota(jnp.int32, (rows, 128), 0)
            return (lax.broadcasted_iota(jnp.int32, (rows, 128), 1) == i + shift).astype(F32).astype(BF16)

        for k in range(3):
            wa[:, 128 * k : 128 * k + 128] = w_qkv[k, :, 0:128]
        q2, k2, v2 = (w_qkv[k, :, 128:192] for k in range(3))
        wa[:, 384:512] = (mm(q2, spot(64, 0), 1, 0) + mm(k2, spot(64, 64), 1, 0)).astype(BF16)
        wa[:, 512:640] = (
            mm(v2, spot(64, 0), 1, 0) + mm(w_out[128:192, :], spot(64, 64), 0, 0)
        ).astype(BF16)
        wa[:, 640:768] = mm(w_out[0:128, :], spot(128, 0), 0, 0).astype(BF16)
        own = gains.shape[1]
        wt[...] = jnp.zeros_like(wt)
        wt[0:2, 0:own] = gains[...].astype(F32)
        wt[2:6, 0:own] = shifts[...].astype(F32)
        wide = pltpu.roll(wt[0:8], d * own, 1)
        wt[...] = jnp.zeros_like(wt)
        wt[0:8] = wide
        per = b_up.shape[1]
        sg[...] = jnp.zeros_like(sg)
        sg[0:6, 0:per] = b_up[...].astype(F32)
        turned = pltpu.roll(sg[0:8, 0:128], d * per, 1)
        for k in range(6):
            wt[7:8, 128 * k : 128 * k + 128] = turned[k : k + 1]
        per = b_qkv.shape[2]
        sg[...] = jnp.zeros_like(sg)
        for h in range(3):
            sg[h : h + 1, 0:per] = b_qkv[h, 0:1].astype(F32)
            sg[3 + h : 4 + h, 0:per] = b_qkv[h, 1:2].astype(F32)
        turned = pltpu.roll(sg[0:8, 0:128], d * per, 1)
        other = pltpu.roll(turned, 64, 1)
        wt[6:7, 0:128] = turned[0:1] + other[1:2]
        wt[6:7, 256:384] = turned[3:4] + other[4:5]
        wt[6:7, 384:512] = turned[2:3]
        wt[6:7, 512:640] = turned[5:6]
        ws[...] = wt[...].astype(BF16)
    pl.semaphore_wait(bar, greeted)

    shards = (wa, wu, wd, ws)

    def slot(m, i):
        return gs.at[i] if m == 3 else g.at[m, i]

    def zcopy(m, side, src, i, s):
        return remote(src, slot(m, i), zss.at[m, side, s], zrs.at[m, side, s], d + 2 - 4 * side, t)

    def xcopy(m, src, i, zsrc):
        return remote(src, slot(m, i), xss.at[m, zsrc], xrs.at[m, zsrc], xn, t)

    def gather_z(m):
        launch(zcopy(m, 0, shards[m], d, 0), z < 3)
        launch(zcopy(m, 1, shards[m], d, 0), z > 0)

    def gather_x(m):
        launch(xcopy(m, shards[m], d, z))

    def gather_step(m, s):
        for side in (0, 1):
            i = d - 2 * s if side == 0 else d + 2 * s
            here = z >= s if side == 0 else z + s <= 3
            onward = z < 3 if side == 0 else z > 0

            @pl.when(here)
            def _():
                zcopy(m, side, slot(m, i), i, s - 1).wait_recv()

            if s < 3:
                launch(zcopy(m, side, slot(m, i), i, s), jnp.logical_and(here, onward))
            launch(xcopy(m, slot(m, i), i, i // 2), here)

    def gather_end(m):
        for k in range(4):
            i = 2 * k + 1 - x
            xcopy(m, slot(m, i), i, k).wait_recv()

    def half_rows(b, j):
        return pl.ds(pl.multiple_of(b * BLK + lax.rem(1 - c + j, 2) * HALF, HALF), HALF)

    def own_rows(b):
        return pl.ds(pl.multiple_of(b * BLK + c * HALF, HALF), HALF)

    def ccopy(st, b):
        return remote(pb.at[st, b, 0], rc.at[st, b], css.at[st, b], crs.at[st, b], d, sib)

    def ycopy(st, b):
        return remote(pb.at[st, b, 1], ry.at[st, b], yss.at[st, b], yrs.at[st, b], d, yn)

    def sum_part(st, b, product):
        def one(j, carry):
            pb[st, b, j] = product(half_rows(b, j)).astype(BF16)

            @pl.when(j == 0)
            def _():
                ccopy(st, b).start()

            return carry

        lax.fori_loop(0, 2, one, 0)
        later.append((ccopy(st, b).wait_send, None))

    def sum_mid(st, b):
        ccopy(st, b).wait_recv()
        pb[st, b, 1] = (pb[st, b, 1].astype(F32) + rc[st, b].astype(F32)).astype(BF16)
        launch(ycopy(st, b))

    def sum_end(st, b):
        ycopy(st, b).wait_recv()
        return pb[st, b, 1].astype(F32) + ry[st, b].astype(F32)

    def share(buf, k, b):
        return remote(buf.at[own_rows(b)], buf.at[own_rows(b)], nss.at[k, b], nrs.at[k, b], d, sib)

    def shared(buf, k, b):
        rows = half_rows(b, 0)
        remote(buf.at[rows], buf.at[rows], nss.at[k, b], nrs.at[k, b], d, sib).wait_recv()

    lane = lax.broadcasted_iota(jnp.int32, (1, 128), 1)
    low = lane < 64

    def mat(m):
        return g[m].reshape(D, D)

    def chunks(b, n, fn, ready=None):
        def one(k, carry):
            i = k
            if ready is not None:
                pl.when(k == n // 2)(ready)
                i = lax.rem(c + k // (n // 2), 2) * (n // 2) + lax.rem(k, n // 2)
            fn(pl.ds(pl.multiple_of(b * BLK + i * (BLK // n), BLK // n), BLK // n), i)
            return carry

        lax.fori_loop(0, n, one, 0)

    def first_norm(b):
        def fn(rows, i):
            zz, _ = standardize(tok[rows].astype(F32))
            nrm[rows] = (zz * prm[0:1] + prm[2:3]).astype(BF16)

        chunks(b, 4, fn)

    def project(b):
        def fn(rows, i):
            p = mm(nrm[rows], mat(0), 1, 0) + prm[6:7]
            s0, s1, s2, s3, s4 = (p[:, 128 * k : 128 * k + 128] for k in range(5))
            for ref, s in ((qh, s0), (kh, s1), (vh, s2)):
                ref[0, rows] = jnp.where(low, s, 0.0).astype(BF16)
                ref[1, rows] = jnp.where(low, 0.0, s).astype(BF16)
            qh[2, rows] = jnp.where(low, s3, 0.0).astype(BF16)
            kh[2, rows] = jnp.where(low, pltpu.roll(s3, 64, 1), 0.0).astype(BF16)
            vh[2, rows] = jnp.where(low, s4, 0.0).astype(BF16)

        chunks(b, 2, fn)

    def attend(b):
        blk = slice(b * BLK, b * BLK + BLK)
        e0 = lens[b, 0]
        e1 = e0 + lens[b, 1]
        e2 = e1 + lens[b, 2]

        def clip_of(pos):
            return (
                (pos >= e0).astype(jnp.int32)
                + (pos >= e1).astype(jnp.int32)
                + (pos >= e2).astype(jnp.int32)
            )

        def fn(rows, i):
            q_clip = clip_of(lax.broadcasted_iota(jnp.int32, (1, HALF), 1) + i * HALF)
            k_clip = clip_of(lax.broadcasted_iota(jnp.int32, (BLK, 1), 0))
            same = q_clip == k_clip
            outs = []
            for h in range(3):
                s = mm(kh[h, blk], qh[h, rows], 1, 1) * 0.125
                s = jnp.where(same, s, masked)
                e = jnp.exp(s - jnp.max(s, axis=0, keepdims=True))
                p = (e / jnp.sum(e, axis=0, keepdims=True)).astype(BF16)
                pr[3 * b + h, :, pl.ds(pl.multiple_of(i * HALF, HALF), HALF)] = p
                outs.append(mm(vh[h, blk], p, 0, 0))
            att[rows, 0:128] = pltpu.roll(outs[2], 64, 0).T.astype(BF16)
            att[rows, 128:256] = (outs[0] + outs[1]).T.astype(BF16)

        chunks(b, 2, fn)

    def out_part(b):
        sum_part(0, b, lambda rows: mm(att[rows], g[0, :, :, 512:768].reshape(D, 256), 1, 1))

    def second_norm(b):
        rows = own_rows(b)
        m = tok[rows].astype(F32) + sum_end(0, b) + prm[4:5]
        mid[b] = m
        zz, _ = standardize(m)
        n2[rows] = (zz * prm[1:2] + prm[3:4]).astype(BF16)
        launch(share(n2, 0, b))

    def up(b):
        def fn(rows, i):
            h = mm(n2[rows], mat(1), 1, 0) + prm[7:8]
            cdf = 0.5 * (1.0 + lax.erf(h * (1.0 / math.sqrt(2.0))))
            act[rows] = (h * cdf).astype(BF16)
            dgl[rows] = cdf + h * (jnp.exp(-0.5 * h * h) * (1.0 / math.sqrt(2.0 * math.pi)))

        chunks(b, 4, fn, lambda: shared(n2, 0, b))

    def hidden_back(b):
        def product(rows):
            low_grad = (mm(cot[rows], mat(2), 1, 0) * dgl[rows]).astype(BF16)
            hg[rows] = low_grad
            sg[7:8] += jnp.sum(low_grad.astype(F32), axis=0, keepdims=True)
            return mm(low_grad, mat(1), 1, 1)

        sum_part(2, b, product)

    def middle_back(b):
        rows = own_rows(b)
        total = sum_end(2, b)
        zz, rstd = standardize(mid[b])
        out_grad = cot[rows].astype(F32)
        m = out_grad + norm_back(total, prm[1:2], zz, rstd)
        mgr[b] = m
        ml[rows] = m.astype(BF16)
        launch(share(ml, 1, b))
        sg[1:2] += jnp.sum(total * zz, axis=0, keepdims=True)
        sg[3:4] += jnp.sum(total, axis=0, keepdims=True)
        sg[4:5] += jnp.sum(m, axis=0, keepdims=True)
        sg[5:6] += jnp.sum(out_grad, axis=0, keepdims=True)

    def attend_back(b):
        blk = slice(b * BLK, b * BLK + BLK)
        dka[...] = jnp.zeros_like(dka)
        dva[...] = jnp.zeros_like(dva)

        def fn(rows, i):
            da = mm(ml[rows], g[0, :, :, 512:768].reshape(D, 256), 1, 0)
            d2, d01 = da[:, 0:128], da[:, 128:256]
            dos = (
                jnp.where(low, d01, 0.0).astype(BF16),
                jnp.where(low, 0.0, d01).astype(BF16),
                jnp.where(low, pltpu.roll(d2, 64, 1), 0.0).astype(BF16),
            )
            dqs = []
            for h in range(3):
                p = pr[3 * b + h, :, pl.ds(pl.multiple_of(i * HALF, HALF), HALF)]
                pf = p.astype(F32)
                dp = mm(vh[h, blk], dos[h], 1, 1)
                ds = (pf * (dp - jnp.sum(pf * dp, axis=0, keepdims=True))).astype(BF16)
                dqs.append(mm(kh[h, blk], ds, 0, 0))
                dka[h] += mm(ds, qh[h, rows], 1, 0)
                dva[h] += mm(p, dos[h], 1, 0)
            dqkv[rows, 0:128] = ((dqs[0] + dqs[1]) * 0.125).T.astype(BF16)
            dqkv[rows, 384:512] = (dqs[2] * 0.125).T.astype(BF16)

        chunks(b, 2, fn, lambda: shared(ml, 1, b))
        dqkv[blk, 128:256] = ((dka[0] + dka[1]) * 0.125).astype(BF16)
        dqkv[blk, 256:384] = (dva[0] + dva[1]).astype(BF16)
        dqkv[blk, 384:512] = (
            dqkv[blk, 384:512].astype(F32) + pltpu.roll(dka[2], 64, 1) * 0.125
        ).astype(BF16)
        dqkv[blk, 512:640] = dva[2].astype(BF16)
        sg[6:7, 0:640] += jnp.sum(dqkv[blk, 0:640].astype(F32), axis=0, keepdims=True)

    def in_part(b):
        def product(rows):
            part = mm(dqkv[rows, 0:640], g[0, :, :, 0:640].reshape(D, 640), 1, 1)
            zz, _ = standardize(tok[rows].astype(F32))
            sg[0:1] += jnp.sum(part * zz, axis=0, keepdims=True)
            sg[2:3] += jnp.sum(part, axis=0, keepdims=True)
            return part

        sum_part(3, b, product)

    def out_copies(k, buf, out, b):
        mine = pltpu.make_async_copy(buf.at[b], out.at[own_rows(b)], lsem.at[2 + 2 * k + b])
        mine.start()
        later.append((mine.wait, None))
        theirs = remote(buf.at[b], out.at[own_rows(b)], oss.at[k, b], ors.at[k, b], d, sib)
        launch(theirs)
        rows = half_rows(b, 0)
        back = remote(buf.at[b], out.at[rows], oss.at[k, b], ors.at[k, b], d, sib)
        later.append((back.wait_recv, None))

    def finish_mixed(b):
        mxs[b] = (mid[b] + sum_end(1, b) + prm[5:6]).astype(BF16)
        out_copies(0, mxs, mixed_h, b)

    def finish_tokens(b):
        total = sum_end(3, b)
        zz, rstd = standardize(tok[own_rows(b)].astype(F32))
        mgr[b] = mgr[b] + norm_back(total, prm[0:1], zz, rstd)
        out_copies(1, mgr, tgrad_h, b)

    def cut(q):
        return slice(384 * q, 384 * q + 384)

    def xred(m, q, k):
        return remote(
            gr.at[m, 2 * k + 1 - x, :, cut(q)], rx.at[m, k, :, cut(q)],
            rxs.at[m, q, k], rxr.at[m, q, k], xn, t,
        )

    zp = z + 1 - 2 * lax.rem(z, 2)
    zf = lax.rem(z + 2, 4)
    zpf = lax.rem(zp + 2, 4)

    def zred(m, q, k):
        src, to = ((zp, zp), (zpf, zp), (zf, zf))[k]
        return remote(
            hs.at[m, src, :, cut(q)], rz.at[m, k, :, cut(q)],
            rzs.at[m, q, k], rzr.at[m, q, k], 2 * to + x, t,
        )

    def weight_grad(m, product):
        for half in range(2):
            gr[m, 4 * half : 4 * half + 4] = product(cut(half)).astype(BF16).reshape(4, PIECE, D)

    def reduce_start(m, q):
        if inner:
            for k in range(4):
                launch(xred(m, q, k))

    outs = (gra_o, gru_o, grd_o)

    def reduce_mid(m, q):
        if not inner:
            return
        for k, zd in ((1, zpf), (0, zp), (2, zf), (3, z)):
            xred(m, q, zd).wait_recv()
            both = gr[m, 2 * zd + x, :, cut(q)].astype(F32) + rx[m, zd, :, cut(q)].astype(F32)
            if k < 3:
                hs[m, zd, :, cut(q)] = both.astype(BF16)
            else:
                outs[m][:, cut(q)] = both
            if k < 2:
                launch(zred(m, q, k))

    def reduce_far(m, q):
        if not inner:
            return
        zred(m, q, 1).wait_recv()
        far = hs[m, zf, :, cut(q)].astype(F32) + rz[m, 1, :, cut(q)].astype(F32)
        hs[m, zf, :, cut(q)] = far.astype(BF16)
        launch(zred(m, q, 2))

    def reduce_end(m):
        if not inner:
            outs[m][...] = gr[m]
            return
        for q in range(2):
            zred(m, q, 0).wait_recv()
            zred(m, q, 2).wait_recv()
            outs[m][:, cut(q)] += rz[m, 0, :, cut(q)].astype(F32) + rz[m, 2, :, cut(q)].astype(F32)

    def down_grad(cols):
        return mm(cot[:, cols], act[...], 0, 0)

    def up_grad(cols):
        return mm(n2[:, cols], hg[...], 0, 0)

    def in_grad(cols):
        a1 = mm(nrm[:, cols], dqkv[:, 0:640], 0, 0)
        a2 = mm(ml[:, cols], att[...], 0, 0)
        return jnp.concatenate(
            [a1[:, 0:512], a1[:, 512:640] + a2[:, 0:128], a2[:, 128:256]], axis=1
        )

    row = lax.broadcasted_iota(jnp.int32, (8, 1), 0)

    def small_c():
        return remote(sg, sgc.at[0], sms.at[0], smr.at[0], d, sib)

    def small_y():
        return remote(sgc.at[1], sgc.at[2], sms.at[1], smr.at[1], d, yn)

    def small_x():
        return remote(sgx.at[0], sgx.at[1], sms.at[2], smr.at[2], xn, t)

    def small_z(k):
        return remote(
            sgz.at[0], sgz.at[k], sms.at[2 + k], smr.at[2 + k], lax.rem(d + 2 * k, 8), t
        )

    def small_step(n):
        if n == 0:
            launch(small_c())
        elif n == 1:
            small_c().wait_recv()
            sgc[1] = sg[...] + jnp.where(row < 6, sgc[0], 0.0)
            launch(small_y())
        elif n == 2:
            small_y().wait_recv()
            both = sgc[1] + jnp.where(jnp.logical_or(row == 0, row == 2), sgc[2], 0.0)
            if inner:
                sgx[0] = both
                launch(small_x())
            else:
                small_o[...] = both
        elif n == 3 and inner:
            small_x().wait_recv()
            sgz[0] = sgx[0] + sgx[1]
            for k in (1, 2, 3):
                launch(small_z(k))
        elif n == 4 and inner:
            for k in (1, 2, 3):
                small_z(k).wait_recv()
            small_o[...] = (sgz[0] + sgz[1]) + (sgz[2] + sgz[3])

    sg[...] = jnp.zeros_like(sg)
    own_pieces = []
    for m in range(3 if not inner else 4):
        own_pieces.append(
            pltpu.make_async_copy(shards[m], slot(m, d) if inner else g.at[m], lsem.at[6 + m])
        )

    def add_parameters():
        if inner:
            own_pieces[3].wait()
            gather_end(3)
            total = gs[0].astype(F32)
            for i in range(1, PARTS):
                total = total + gs[i].astype(F32)
            prm[...] = total
        else:
            prm[...] = ws[...].astype(F32)

    def step(m, s):
        if inner:
            gather_step(m, s)

    if inner:
        for m in (0, 3):
            gather_z(m)
            gather_x(m)
    for cp in own_pieces:
        cp.start()
    step(0, 1)
    step(3, 1)
    step(0, 2)
    step(3, 2)
    if inner:
        gather_z(1)
    step(0, 3)
    step(3, 3)
    if inner:
        gather_x(1)
    add_parameters()
    cp_tok.wait()
    first_norm(0)
    step(1, 1)
    if inner:
        gather_z(2)
    for b in range(1, nb):
        first_norm(b)
    for cp in own_pieces[:3]:
        cp.wait()
    if inner:
        gather_end(0)
    step(1, 2)
    for b in range(nb):
        project(b)
        if b:
            sum_mid(0, b - 1)
            step(2, 1)
        else:
            step(1, 3)
            if inner:
                gather_x(2)
        attend(b)
        out_part(b)
    cp_cot.wait()
    sum_mid(0, nb - 1)
    step(2, 2)
    step(2, 3)
    if inner:
        gather_end(1)
    for b in range(nb):
        second_norm(b)
        up(b)
        if inner and b == 0:
            gather_end(2)
        if b == nb - 1:
            weight_grad(2, down_grad)
            reduce_start(2, 0)
            reduce_start(2, 1)
        hidden_back(b)
        if b == 0:
            sum_part(1, b, lambda rows: mm(act[rows], mat(2), 1, 1))
        sum_mid(2, b)
    for b in range(1, nb):
        sum_part(1, b, lambda rows: mm(act[rows], mat(2), 1, 1))
    weight_grad(1, up_grad)
    for b in range(nb):
        middle_back(b)
        attend_back(b)
        if b == 0:
            sum_mid(1, 0)
        if b == nb - 1:
            weight_grad(0, in_grad)
            reduce_start(0, 1)
            reduce_start(0, 0)
            for q in range(2):
                reduce_far(2, q)
        in_part(b)
        if b == nb - 1:
            small_step(0)
            small_step(1)
        sum_mid(3, b)
        if b == 0:
            reduce_start(1, 0)
            reduce_start(1, 1)
            for q in range(2):
                reduce_mid(2, q)
    for b in range(1, nb):
        sum_mid(1, b)
    for q in range(2):
        reduce_mid(1, q)
    finish_mixed(0)
    finish_tokens(0)
    for q in range(2):
        reduce_far(1, q)
    small_step(2)
    reduce_mid(0, 1)
    reduce_mid(0, 0)
    for b in range(1, nb):
        finish_tokens(b)
    reduce_far(0, 1)
    reduce_far(0, 0)
    small_step(3)
    reduce_end(2)
    reduce_end(1)
    small_step(4)
    reduce_end(0)
    for b in range(1, nb):
        finish_mixed(b)
    for wait, guard in later:
        if guard is None:
            wait()
        else:
            pl.when(guard)(wait)


def call_kernel(inner, *args):
    rows = args[0].shape[0]
    nb = rows // BLK
    vmem = pl.BlockSpec(memory_space=pltpu.VMEM)
    anywhere = pl.BlockSpec(memory_space=pl.ANY)
    grads = (
        jax.ShapeDtypeStruct((PIECE, D), F32)
        if inner
        else jax.ShapeDtypeStruct((PARTS, PIECE, D), BF16)
    )
    dma = pltpu.SemaphoreType.DMA
    scratch = [
        pltpu.VMEM((rows, D), BF16),
        pltpu.VMEM((rows, D), BF16),
        pltpu.VMEM((3, PARTS, PIECE, D), BF16),
        pltpu.VMEM((PARTS, 16, D), BF16),
        pltpu.VMEM((16, D), F32),
        pltpu.VMEM((rows, D), BF16),
        pltpu.VMEM((3, rows, 128), BF16),
        pltpu.VMEM((3, rows, 128), BF16),
        pltpu.VMEM((3, rows, 128), BF16),
        pltpu.VMEM((3 * nb, BLK, BLK), BF16),
        pltpu.VMEM((rows, 256), BF16),
        pltpu.VMEM((nb, HALF, D), F32),
        pltpu.VMEM((rows, D), BF16),
        pltpu.VMEM((rows, D), BF16),
        pltpu.VMEM((rows, D), F32),
        pltpu.VMEM((rows, D), BF16),
        pltpu.VMEM((rows, D), BF16),
        pltpu.VMEM((nb, HALF, D), F32),
        pltpu.VMEM((rows, 640), BF16),
        pltpu.VMEM((3, BLK, 128), F32),
        pltpu.VMEM((3, BLK, 128), F32),
        pltpu.VMEM((4, nb, 2, HALF, D), BF16),
        pltpu.VMEM((4, nb, HALF, D), BF16),
        pltpu.VMEM((4, nb, HALF, D), BF16),
        pltpu.VMEM((nb, HALF, D), BF16),
        pltpu.VMEM((3, PARTS, PIECE, D), BF16),
        pltpu.VMEM((3, 4, PIECE, D), BF16),
        pltpu.VMEM((3, 4, PIECE, D), BF16),
        pltpu.VMEM((3, 3, PIECE, D), BF16),
        pltpu.VMEM((8, D), F32),
        pltpu.VMEM((3, 8, D), F32),
        pltpu.VMEM((2, 8, D), F32),
        pltpu.VMEM((4, 8, D), F32),
        dma((10,)),
        dma((4, 2, 3)),
        dma((4, 2, 3)),
        dma((4, 4)),
        dma((4, 4)),
        dma((4, nb)),
        dma((4, nb)),
        dma((4, nb)),
        dma((4, nb)),
        dma((2, nb)),
        dma((2, nb)),
        dma((2, nb)),
        dma((2, nb)),
        dma((3, 2, 4)),
        dma((3, 2, 4)),
        dma((3, 2, 3)),
        dma((3, 2, 3)),
        dma((6,)),
        dma((6,)),
    ]
    if inner:
        scratch += [pltpu.VMEM((PIECE, D), BF16), pltpu.VMEM((16, D), BF16), pltpu.VMEM((16, D), F32)]

    def kernel(*refs):
        layer_kernel(inner, nb, refs)

    return pl.pallas_call(
        kernel,
        out_shape=(
            jax.ShapeDtypeStruct((rows, D), BF16),
            jax.ShapeDtypeStruct((rows, D), F32),
            grads,
            grads,
            grads,
            jax.ShapeDtypeStruct((8, D), F32),
        ),
        in_specs=[anywhere, anywhere]
        + ([vmem, vmem, anywhere, anywhere, vmem, vmem, vmem, vmem] if inner else [vmem] * 4)
        + [pl.BlockSpec(memory_space=pltpu.SMEM)],
        out_specs=(anywhere, anywhere, vmem, vmem, vmem, vmem),
        scratch_shapes=scratch,
        compiler_params=pltpu.CompilerParams(
            collective_id=0, has_side_effects=True, vmem_limit_bytes=60 * 2**20
        ),
    )(*args)


def pack_heads(q, k, v, o):
    return jnp.concatenate(
        [
            q[..., :128], k[..., :128], v[..., :128],
            q[..., 128:], k[..., 128:], v[..., 128:], o[..., 128:], o[..., :128],
        ],
        axis=-1,
    )


def unpack_heads(w):
    q = jnp.concatenate([w[..., 0:128], w[..., 384:448]], axis=-1)
    k = jnp.concatenate([w[..., 128:256], w[..., 448:512]], axis=-1)
    v = jnp.concatenate([w[..., 256:384], w[..., 512:576]], axis=-1)
    o = jnp.concatenate([w[..., 640:768], w[..., 576:640]], axis=-1)
    return q, k, v, o


def unpack_kernel(mix_h, tok_h, ga, gu, gd, small, mix_o, tok_o, qkv_o, out_o, up_o, down_o, gains_o, shifts_o, bqkv_o, bup_o, tok_v, mix_v, sem):
    d = lax.axis_index("dp")
    moves = []
    for src, via, dst in ((tok_h, tok_v, tok_o), (mix_h, mix_v, mix_o)):
        for k in range(4):
            rows = slice(k * src.shape[0] // 4, (k + 1) * src.shape[0] // 4)
            sems = sem.at[len(moves)]
            load = pltpu.make_async_copy(src.at[rows], via.at[rows], sems)
            load.start()
            moves.append((load, pltpu.make_async_copy(via.at[rows], dst.at[rows], sems)))
    for load, store in moves:
        load.wait()
        store.start()
    own = gains_o.shape[1]
    for k in range(3):
        qkv_o[k, :, 0:128] = ga[:, 128 * k : 128 * k + 128]
    qkv_o[0, :, 128:192] = ga[:, 384:448]
    qkv_o[1, :, 128:192] = pltpu.roll(ga[:, 384:512], 64, 1)[:, 0:64]
    qkv_o[2, :, 128:192] = ga[:, 512:576]
    fill = jnp.zeros((128 - own, 128), F32)
    out_o[0:128, :] = jnp.concatenate([ga[:, 640:768], fill], axis=0).T[:, 0:own]
    out_o[128:192, :] = jnp.concatenate([ga[:, 512:640], fill], axis=0).T[64:128, 0:own]
    up_o[...] = gu[...]
    down_o[...] = gd[...]
    wide = pltpu.roll(small[...], D - d * own, 1)
    gains_o[...] = wide[0:2, 0:own]
    shifts_o[...] = wide[2:6, 0:own]
    for part in range(2):
        for h, at in enumerate((0, 64, 384) if part == 0 else (256, 320, 512)):
            per = bqkv_o.shape[2]
            slab = small[:, at // 128 * 128 : at // 128 * 128 + 128]
            turned = pltpu.roll(slab, 128 - at % 128 - d * per + 128 * (at % 128 // 64), 1)
            bqkv_o[h, part : part + 1, :] = turned[6:7, 0:per]
    for k in range(6):
        per = bup_o.shape[1]
        turned = pltpu.roll(small[:, 128 * k : 128 * k + 128], 128 - d * per, 1)
        bup_o[k : k + 1, :] = turned[7:8, 0:per]
    for _, store in moves:
        store.wait()


def body(tokens, cotangent, w_qkv, w_out, w_up, w_down, gains, shifts, b_qkv, b_up, clip_lengths):
    own = w_up.shape[0]
    dp = D // own
    if dp == 8:
        mixed, tgrad, ga, gu, gd, small = call_kernel(
            True, tokens, cotangent, w_qkv, w_out, w_up, w_down.T,
            gains, shifts, b_qkv.transpose(1, 0, 2), b_up, clip_lengths,
        )
        vmem = pl.BlockSpec(memory_space=pltpu.VMEM)
        anywhere = pl.BlockSpec(memory_space=pl.ANY)
        like = [mixed, tgrad, w_qkv, w_out, gu, gd, gains, shifts, b_qkv.transpose(1, 0, 2), b_up]
        outs = pl.pallas_call(
            unpack_kernel,
            out_shape=tuple(
                jax.ShapeDtypeStruct(a.shape, BF16 if i == 0 else F32) for i, a in enumerate(like)
            ),
            in_specs=[anywhere, anywhere] + [vmem] * 4,
            out_specs=tuple([anywhere, anywhere] + [vmem] * 8),
            scratch_shapes=[
                pltpu.VMEM(tgrad.shape, F32),
                pltpu.VMEM(mixed.shape, BF16),
                pltpu.SemaphoreType.DMA((8,)),
            ],
        )(mixed, tgrad, ga, gu, gd, small)
        return outs[:5] + (outs[5].T, outs[6], outs[7], outs[8].transpose(1, 0, 2), outs[9])

    d = lax.axis_index("dp")
    wide = jnp.concatenate([gains, shifts], axis=0)
    wide = lax.dynamic_update_slice(jnp.zeros((6, D), BF16), wide, (0, d * own))
    heads = b_qkv.shape[1]
    per_head = b_qkv.shape[2]
    full_head = per_head * dp
    bq = lax.dynamic_update_slice(
        jnp.zeros((2, heads, full_head), BF16), b_qkv, (0, 0, d * per_head)
    ).reshape(2, heads * full_head)
    none = jnp.zeros((heads * full_head,), BF16)
    bq = pack_heads(bq[0], none, bq[1], none)
    bu = lax.dynamic_update_slice(
        jnp.zeros((b_up.shape[0], b_up.shape[1] * dp), BF16), b_up, (0, d * b_up.shape[1])
    ).reshape(1, D)
    ws = jnp.concatenate([wide, bq[None], bu, jnp.zeros((8, D), BF16)], axis=0)
    ws = lax.psum(ws.astype(F32), "dp").astype(BF16)
    wa = pack_heads(w_qkv[0], w_qkv[1], w_qkv[2], w_out.T)
    wa, wu, wd = (
        lax.all_gather(w, "dp", axis=0, tiled=True).reshape(PARTS, PIECE, D)
        for w in (wa, w_up, w_down.T)
    )
    mixed, tgrad, ga, gu, gd, small = call_kernel(
        False, tokens, cotangent, ws, wa, wu, wd, clip_lengths
    )
    ga, gu, gd = (
        lax.psum_scatter(w.astype(F32).reshape(D, D), "dp", scatter_dimension=0, tiled=True)
        for w in (ga, gu, gd)
    )
    small = lax.psum(small, "dp")
    q, k, v, o = unpack_heads(ga)
    wide = lax.dynamic_slice(small[0:6], (0, d * own), (6, own))
    bq, _, bv, _ = unpack_heads(small[6])
    b_qkv_grad = jnp.stack([bq, bv]).reshape(2, heads, full_head)
    b_qkv_grad = lax.dynamic_slice(b_qkv_grad, (0, 0, d * per_head), (2, heads, per_head))
    b_up_grad = lax.dynamic_slice(
        small[7].reshape(b_up.shape[0], -1), (0, d * b_up.shape[1]), b_up.shape
    )
    return (
        mixed,
        tgrad,
        jnp.stack([q, k, v]),
        o.T,
        gu,
        gd.T,
        wide[0:2],
        wide[2:6],
        b_qkv_grad,
        b_up_grad,
    )


def solution(mesh):
    return jax.shard_map(
        body,
        mesh=mesh,
        in_specs=(
            P("dp", None),
            P("dp", None),
            P(None, "dp", "tp"),
            P("tp", "dp"),
            P("dp", "tp"),
            P("tp", "dp"),
            P(None, "dp"),
            P(None, "dp"),
            P(None, "tp", "dp"),
            P("tp", "dp"),
            P("dp", None),
        ),
        out_specs=(
            P("dp", None),
            P("dp", None),
            P(None, "dp", "tp"),
            P("tp", "dp"),
            P("dp", "tp"),
            P("tp", "dp"),
            P(None, "dp"),
            P(None, "dp"),
            P(None, "tp", "dp"),
            P("tp", "dp"),
        ),
        check_vma=False,
    )
```

```python
import functools
import math

import jax
import jax.numpy as jnp
from jax import lax
from jax.experimental import pallas as pl
from jax.experimental.pallas import tpu as pltpu
from jax.sharding import PartitionSpec as P

MESH = pl.DeviceIdType.MESH
F32 = jnp.float32
BF16 = jnp.bfloat16
D = 768
BLK = 512
HALF = 256
PARTS = 8
PIECE = D // PARTS
eps = 1e-06
masked = -1e30


def mm(a, b, ca, cb):
    return lax.dot_general(a, b, (((ca,), (cb,)), ((), ())), preferred_element_type=F32)


def standardize(v):
    centred = v - jnp.mean(v, axis=-1, keepdims=True)
    rstd = lax.rsqrt(jnp.mean(centred * centred, axis=-1, keepdims=True) + eps)
    return centred * rstd, rstd


def norm_back(grad, gain, z, rstd):
    n = grad * gain
    return (
        n - jnp.mean(n, axis=-1, keepdims=True) - z * jnp.mean(n * z, axis=-1, keepdims=True)
    ) * rstd


def layer_kernel(inner, nb, refs):
    if inner:
        (tok_h, cot_h, w_qkv, w_out, wu, wd, gains, shifts, b_qkv, b_up, lens) = refs[:11]
        wa, ws, wt = refs[-3:]
        refs = refs[11:-3]
    else:
        (tok_h, cot_h, ws, wa, wu, wd, lens) = refs[:7]
        refs = refs[7:]
    (mixed_h, tgrad_h, gra_o, gru_o, grd_o, small_o) = refs[:6]
    (
        tok, cot, g, gs, prm, nrm, qh, kh, vh, pr, att, mid, n2, act, dgl, hg, ml, mgr, dqkv,
        dka, dva, pb, rc, ry, mxs, gr, rx, hs, rz, sg, sgc, sgx, sgz,
        lsem, zss, zrs, xss, xrs, css, crs, yss, yrs, nss, nrs, oss, ors, rxs, rxr, rzs, rzr, sms, smr,
    ) = refs[6:]
    d = lax.axis_index("dp")
    t = lax.axis_index("tp")
    z = d // 2
    x = d % 2
    c = t % 2
    xn = d + 1 - 2 * x
    sib = t + 1 - 2 * c
    yn = lax.rem(t + 2, 4)
    later = []

    def remote(src, dst, s, r, dd, tt):
        return pltpu.make_async_remote_copy(
            src_ref=src, dst_ref=dst, send_sem=s, recv_sem=r, device_id=(dd, tt), device_id_type=MESH
        )

    def launch(copy, guard=None):
        if guard is None:
            copy.start()
        else:
            pl.when(guard)(copy.start)
        later.append((copy.wait_send, guard))

    bar = pltpu.get_barrier_semaphore()
    greet = [(d, sib), (d, yn)] + ([(xn, t)] if inner else [])
    greeted = len(greet)
    for who in greet:
        pl.semaphore_signal(bar, 1, device_id=who, device_id_type=MESH)
    if inner:
        for guard, who in ((z < 3, d + 2), (z > 0, d - 2)):

            @pl.when(guard)
            def _():
                pl.semaphore_signal(bar, 1, device_id=(who, t), device_id_type=MESH)

            greeted = greeted + guard.astype(jnp.int32)
    cp_tok = pltpu.make_async_copy(tok_h, tok, lsem.at[0])
    cp_tok.start()
    cp_cot = pltpu.make_async_copy(cot_h, cot, lsem.at[1])
    cp_cot.start()
    if inner:
        def spot(rows, shift):
            i = lax.broadcasted_iota(jnp.int32, (rows, 128), 0)
            return (lax.broadcasted_iota(jnp.int32, (rows, 128), 1) == i + shift).astype(F32).astype(BF16)

        for k in range(3):
            wa[:, 128 * k : 128 * k + 128] = w_qkv[k, :, 0:128]
        q2, k2, v2 = (w_qkv[k, :, 128:192] for k in range(3))
        wa[:, 384:512] = (mm(q2, spot(64, 0), 1, 0) + mm(k2, spot(64, 64), 1, 0)).astype(BF16)
        wa[:, 512:640] = (
            mm(v2, spot(64, 0), 1, 0) + mm(w_out[128:192, :], spot(64, 64), 0, 0)
        ).astype(BF16)
        wa[:, 640:768] = mm(w_out[0:128, :], spot(128, 0), 0, 0).astype(BF16)
        own = gains.shape[1]
        wt[...] = jnp.zeros_like(wt)
        wt[0:2, 0:own] = gains[...].astype(F32)
        wt[2:6, 0:own] = shifts[...].astype(F32)
        wide = pltpu.roll(wt[0:8], d * own, 1)
        wt[...] = jnp.zeros_like(wt)
        wt[0:8] = wide
        per = b_up.shape[1]
        sg[...] = jnp.zeros_like(sg)
        sg[0:6, 0:per] = b_up[...].astype(F32)
        turned = pltpu.roll(sg[0:8, 0:128], d * per, 1)
        for k in range(6):
            wt[7:8, 128 * k : 128 * k + 128] = turned[k : k + 1]
        per = b_qkv.shape[2]
        sg[...] = jnp.zeros_like(sg)
        for h in range(3):
            sg[h : h + 1, 0:per] = b_qkv[h, 0:1].astype(F32)
            sg[3 + h : 4 + h, 0:per] = b_qkv[h, 1:2].astype(F32)
        turned = pltpu.roll(sg[0:8, 0:128], d * per, 1)
        other = pltpu.roll(turned, 64, 1)
        wt[6:7, 0:128] = turned[0:1] + other[1:2]
        wt[6:7, 256:384] = turned[3:4] + other[4:5]
        wt[6:7, 384:512] = turned[2:3]
        wt[6:7, 512:640] = turned[5:6]
        ws[...] = wt[...].astype(BF16)
    pl.semaphore_wait(bar, greeted)

    shards = (wa, wu, wd, ws)

    def slot(m, i):
        return gs.at[i] if m == 3 else g.at[m, i]

    def zcopy(m, side, src, i, s):
        return remote(src, slot(m, i), zss.at[m, side, s], zrs.at[m, side, s], d + 2 - 4 * side, t)

    def xcopy(m, src, i, zsrc):
        return remote(src, slot(m, i), xss.at[m, zsrc], xrs.at[m, zsrc], xn, t)

    def gather_z(m):
        launch(zcopy(m, 0, shards[m], d, 0), z < 3)
        launch(zcopy(m, 1, shards[m], d, 0), z > 0)

    def gather_x(m):
        launch(xcopy(m, shards[m], d, z))

    def gather_step(m, s):
        for side in (0, 1):
            i = d - 2 * s if side == 0 else d + 2 * s
            here = z >= s if side == 0 else z + s <= 3
            onward = z < 3 if side == 0 else z > 0

            @pl.when(here)
            def _():
                zcopy(m, side, slot(m, i), i, s - 1).wait_recv()

            if s < 3:
                launch(zcopy(m, side, slot(m, i), i, s), jnp.logical_and(here, onward))
            launch(xcopy(m, slot(m, i), i, i // 2), here)

    def gather_end(m):
        for k in range(4):
            i = 2 * k + 1 - x
            xcopy(m, slot(m, i), i, k).wait_recv()

    def half_rows(b, j):
        return pl.ds(pl.multiple_of(b * BLK + lax.rem(1 - c + j, 2) * HALF, HALF), HALF)

    def own_rows(b):
        return pl.ds(pl.multiple_of(b * BLK + c * HALF, HALF), HALF)

    def ccopy(st, b):
        return remote(pb.at[st, b, 0], rc.at[st, b], css.at[st, b], crs.at[st, b], d, sib)

    def ycopy(st, b):
        return remote(pb.at[st, b, 1], ry.at[st, b], yss.at[st, b], yrs.at[st, b], d, yn)

    def sum_part(st, b, product):
        def one(j, carry):
            pb[st, b, j] = product(half_rows(b, j)).astype(BF16)

            @pl.when(j == 0)
            def _():
                ccopy(st, b).start()

            return carry

        lax.fori_loop(0, 2, one, 0)
        later.append((ccopy(st, b).wait_send, None))

    def sum_mid(st, b):
        ccopy(st, b).wait_recv()
        pb[st, b, 1] = (pb[st, b, 1].astype(F32) + rc[st, b].astype(F32)).astype(BF16)
        launch(ycopy(st, b))

    def sum_end(st, b):
        ycopy(st, b).wait_recv()
        return pb[st, b, 1].astype(F32) + ry[st, b].astype(F32)

    def share(buf, k, b):
        return remote(buf.at[own_rows(b)], buf.at[own_rows(b)], nss.at[k, b], nrs.at[k, b], d, sib)

    def shared(buf, k, b):
        rows = half_rows(b, 0)
        remote(buf.at[rows], buf.at[rows], nss.at[k, b], nrs.at[k, b], d, sib).wait_recv()

    lane = lax.broadcasted_iota(jnp.int32, (1, 128), 1)
    low = lane < 64

    def mat(m):
        return g[m].reshape(D, D)

    def chunks(b, n, fn, ready=None):
        def one(k, carry):
            i = k
            if ready is not None:
                pl.when(k == n // 2)(ready)
                i = lax.rem(c + k // (n // 2), 2) * (n // 2) + lax.rem(k, n // 2)
            fn(pl.ds(pl.multiple_of(b * BLK + i * (BLK // n), BLK // n), BLK // n), i)
            return carry

        lax.fori_loop(0, n, one, 0)

    def first_norm(b):
        def fn(rows, i):
            zz, _ = standardize(tok[rows].astype(F32))
            nrm[rows] = (zz * prm[0:1] + prm[2:3]).astype(BF16)

        chunks(b, 4, fn)

    def project(b):
        def fn(rows, i):
            p = mm(nrm[rows], mat(0), 1, 0) + prm[6:7]
            s0, s1, s2, s3, s4 = (p[:, 128 * k : 128 * k + 128] for k in range(5))
            for ref, s in ((qh, s0), (kh, s1), (vh, s2)):
                ref[0, rows] = jnp.where(low, s, 0.0).astype(BF16)
                ref[1, rows] = jnp.where(low, 0.0, s).astype(BF16)
            qh[2, rows] = jnp.where(low, s3, 0.0).astype(BF16)
            kh[2, rows] = jnp.where(low, pltpu.roll(s3, 64, 1), 0.0).astype(BF16)
            vh[2, rows] = jnp.where(low, s4, 0.0).astype(BF16)

        chunks(b, 2, fn)

    def attend(b):
        blk = slice(b * BLK, b * BLK + BLK)
        e0 = lens[b, 0]
        e1 = e0 + lens[b, 1]
        e2 = e1 + lens[b, 2]

        def clip_of(pos):
            return (
                (pos >= e0).astype(jnp.int32)
                + (pos >= e1).astype(jnp.int32)
                + (pos >= e2).astype(jnp.int32)
            )

        def fn(rows, i):
            q_clip = clip_of(lax.broadcasted_iota(jnp.int32, (1, HALF), 1) + i * HALF)
            k_clip = clip_of(lax.broadcasted_iota(jnp.int32, (BLK, 1), 0))
            same = q_clip == k_clip
            outs = []
            for h in range(3):
                s = mm(kh[h, blk], qh[h, rows], 1, 1) * 0.125
                s = jnp.where(same, s, masked)
                e = jnp.exp(s - jnp.max(s, axis=0, keepdims=True))
                p = (e / jnp.sum(e, axis=0, keepdims=True)).astype(BF16)
                pr[3 * b + h, :, pl.ds(pl.multiple_of(i * HALF, HALF), HALF)] = p
                outs.append(mm(vh[h, blk], p, 0, 0))
            att[rows, 0:128] = pltpu.roll(outs[2], 64, 0).T.astype(BF16)
            att[rows, 128:256] = (outs[0] + outs[1]).T.astype(BF16)

        chunks(b, 2, fn)

    def out_part(b):
        sum_part(0, b, lambda rows: mm(att[rows], g[0, :, :, 512:768].reshape(D, 256), 1, 1))

    def second_norm(b):
        rows = own_rows(b)
        m = tok[rows].astype(F32) + sum_end(0, b) + prm[4:5]
        mid[b] = m
        zz, _ = standardize(m)
        n2[rows] = (zz * prm[1:2] + prm[3:4]).astype(BF16)
        launch(share(n2, 0, b))

    def up(b):
        def fn(rows, i):
            h = mm(n2[rows], mat(1), 1, 0) + prm[7:8]
            cdf = 0.5 * (1.0 + lax.erf(h * (1.0 / math.sqrt(2.0))))
            act[rows] = (h * cdf).astype(BF16)
            dgl[rows] = cdf + h * (jnp.exp(-0.5 * h * h) * (1.0 / math.sqrt(2.0 * math.pi)))

        chunks(b, 4, fn, lambda: shared(n2, 0, b))

    def hidden_back(b):
        def product(rows):
            low_grad = (mm(cot[rows], mat(2), 1, 0) * dgl[rows]).astype(BF16)
            hg[rows] = low_grad
            sg[7:8] += jnp.sum(low_grad.astype(F32), axis=0, keepdims=True)
            return mm(low_grad, mat(1), 1, 1)

        sum_part(2, b, product)

    def middle_back(b):
        rows = own_rows(b)
        total = sum_end(2, b)
        zz, rstd = standardize(mid[b])
        out_grad = cot[rows].astype(F32)
        m = out_grad + norm_back(total, prm[1:2], zz, rstd)
        mgr[b] = m
        ml[rows] = m.astype(BF16)
        launch(share(ml, 1, b))
        sg[1:2] += jnp.sum(total * zz, axis=0, keepdims=True)
        sg[3:4] += jnp.sum(total, axis=0, keepdims=True)
        sg[4:5] += jnp.sum(m, axis=0, keepdims=True)
        sg[5:6] += jnp.sum(out_grad, axis=0, keepdims=True)

    def attend_back(b):
        blk = slice(b * BLK, b * BLK + BLK)
        dka[...] = jnp.zeros_like(dka)
        dva[...] = jnp.zeros_like(dva)

        def fn(rows, i):
            da = mm(ml[rows], g[0, :, :, 512:768].reshape(D, 256), 1, 0)
            d2, d01 = da[:, 0:128], da[:, 128:256]
            dos = (
                jnp.where(low, d01, 0.0).astype(BF16),
                jnp.where(low, 0.0, d01).astype(BF16),
                jnp.where(low, pltpu.roll(d2, 64, 1), 0.0).astype(BF16),
            )
            dqs = []
            for h in range(3):
                p = pr[3 * b + h, :, pl.ds(pl.multiple_of(i * HALF, HALF), HALF)]
                pf = p.astype(F32)
                dp = mm(vh[h, blk], dos[h], 1, 1)
                ds = (pf * (dp - jnp.sum(pf * dp, axis=0, keepdims=True))).astype(BF16)
                dqs.append(mm(kh[h, blk], ds, 0, 0))
                dka[h] += mm(ds, qh[h, rows], 1, 0)
                dva[h] += mm(p, dos[h], 1, 0)
            dqkv[rows, 0:128] = ((dqs[0] + dqs[1]) * 0.125).T.astype(BF16)
            dqkv[rows, 384:512] = (dqs[2] * 0.125).T.astype(BF16)

        chunks(b, 2, fn, lambda: shared(ml, 1, b))
        dqkv[blk, 128:256] = ((dka[0] + dka[1]) * 0.125).astype(BF16)
        dqkv[blk, 256:384] = (dva[0] + dva[1]).astype(BF16)
        dqkv[blk, 384:512] = (
            dqkv[blk, 384:512].astype(F32) + pltpu.roll(dka[2], 64, 1) * 0.125
        ).astype(BF16)
        dqkv[blk, 512:640] = dva[2].astype(BF16)
        sg[6:7, 0:640] += jnp.sum(dqkv[blk, 0:640].astype(F32), axis=0, keepdims=True)

    def in_part(b):
        def product(rows):
            part = mm(dqkv[rows, 0:640], g[0, :, :, 0:640].reshape(D, 640), 1, 1)
            zz, _ = standardize(tok[rows].astype(F32))
            sg[0:1] += jnp.sum(part * zz, axis=0, keepdims=True)
            sg[2:3] += jnp.sum(part, axis=0, keepdims=True)
            return part

        sum_part(3, b, product)

    def out_copies(k, buf, out, b):
        mine = pltpu.make_async_copy(buf.at[b], out.at[own_rows(b)], lsem.at[2 + 2 * k + b])
        mine.start()
        later.append((mine.wait, None))
        theirs = remote(buf.at[b], out.at[own_rows(b)], oss.at[k, b], ors.at[k, b], d, sib)
        launch(theirs)
        rows = half_rows(b, 0)
        back = remote(buf.at[b], out.at[rows], oss.at[k, b], ors.at[k, b], d, sib)
        later.append((back.wait_recv, None))

    def finish_mixed(b):
        mxs[b] = (mid[b] + sum_end(1, b) + prm[5:6]).astype(BF16)
        out_copies(0, mxs, mixed_h, b)

    def finish_tokens(b):
        total = sum_end(3, b)
        zz, rstd = standardize(tok[own_rows(b)].astype(F32))
        mgr[b] = mgr[b] + norm_back(total, prm[0:1], zz, rstd)
        out_copies(1, mgr, tgrad_h, b)

    def cut(q):
        return slice(384 * q, 384 * q + 384)

    def xred(m, q, k):
        return remote(
            gr.at[m, 2 * k + 1 - x, :, cut(q)], rx.at[m, k, :, cut(q)],
            rxs.at[m, q, k], rxr.at[m, q, k], xn, t,
        )

    zp = z + 1 - 2 * lax.rem(z, 2)
    zf = lax.rem(z + 2, 4)
    zpf = lax.rem(zp + 2, 4)

    def zred(m, q, k):
        src, to = ((zp, zp), (zpf, zp), (zf, zf))[k]
        return remote(
            hs.at[m, src, :, cut(q)], rz.at[m, k, :, cut(q)],
            rzs.at[m, q, k], rzr.at[m, q, k], 2 * to + x, t,
        )

    def weight_grad(m, product):
        for half in range(2):
            gr[m, 4 * half : 4 * half + 4] = product(cut(half)).astype(BF16).reshape(4, PIECE, D)

    def reduce_start(m, q):
        if inner:
            for k in range(4):
                launch(xred(m, q, k))

    outs = (gra_o, gru_o, grd_o)

    def reduce_mid(m, q):
        if not inner:
            return
        for k, zd in ((1, zpf), (0, zp), (2, zf), (3, z)):
            xred(m, q, zd).wait_recv()
            both = gr[m, 2 * zd + x, :, cut(q)].astype(F32) + rx[m, zd, :, cut(q)].astype(F32)
            if k < 3:
                hs[m, zd, :, cut(q)] = both.astype(BF16)
            else:
                outs[m][:, cut(q)] = both
            if k < 2:
                launch(zred(m, q, k))

    def reduce_far(m, q):
        if not inner:
            return
        zred(m, q, 1).wait_recv()
        far = hs[m, zf, :, cut(q)].astype(F32) + rz[m, 1, :, cut(q)].astype(F32)
        hs[m, zf, :, cut(q)] = far.astype(BF16)
        launch(zred(m, q, 2))

    def reduce_end(m):
        if not inner:
            outs[m][...] = gr[m]
            return
        for q in range(2):
            zred(m, q, 0).wait_recv()
            zred(m, q, 2).wait_recv()
            outs[m][:, cut(q)] += rz[m, 0, :, cut(q)].astype(F32) + rz[m, 2, :, cut(q)].astype(F32)

    def down_grad(cols):
        return mm(cot[:, cols], act[...], 0, 0)

    def up_grad(cols):
        return mm(n2[:, cols], hg[...], 0, 0)

    def in_grad(cols):
        a1 = mm(nrm[:, cols], dqkv[:, 0:640], 0, 0)
        a2 = mm(ml[:, cols], att[...], 0, 0)
        return jnp.concatenate(
            [a1[:, 0:512], a1[:, 512:640] + a2[:, 0:128], a2[:, 128:256]], axis=1
        )

    row = lax.broadcasted_iota(jnp.int32, (8, 1), 0)

    def small_c():
        return remote(sg, sgc.at[0], sms.at[0], smr.at[0], d, sib)

    def small_y():
        return remote(sgc.at[1], sgc.at[2], sms.at[1], smr.at[1], d, yn)

    def small_x():
        return remote(sgx.at[0], sgx.at[1], sms.at[2], smr.at[2], xn, t)

    def small_z(k):
        return remote(
            sgz.at[0], sgz.at[k], sms.at[2 + k], smr.at[2 + k], lax.rem(d + 2 * k, 8), t
        )

    def small_step(n):
        if n == 0:
            launch(small_c())
        elif n == 1:
            small_c().wait_recv()
            sgc[1] = sg[...] + jnp.where(row < 6, sgc[0], 0.0)
            launch(small_y())
        elif n == 2:
            small_y().wait_recv()
            both = sgc[1] + jnp.where(jnp.logical_or(row == 0, row == 2), sgc[2], 0.0)
            if inner:
                sgx[0] = both
                launch(small_x())
            else:
                small_o[...] = both
        elif n == 3 and inner:
            small_x().wait_recv()
            sgz[0] = sgx[0] + sgx[1]
            for k in (1, 2, 3):
                launch(small_z(k))
        elif n == 4 and inner:
            for k in (1, 2, 3):
                small_z(k).wait_recv()
            small_o[...] = (sgz[0] + sgz[1]) + (sgz[2] + sgz[3])

    sg[...] = jnp.zeros_like(sg)
    own_pieces = []
    for m in range(3 if not inner else 4):
        own_pieces.append(
            pltpu.make_async_copy(shards[m], slot(m, d) if inner else g.at[m], lsem.at[6 + m])
        )

    def add_parameters():
        if inner:
            own_pieces[3].wait()
            gather_end(3)
            total = gs[0].astype(F32)
            for i in range(1, PARTS):
                total = total + gs[i].astype(F32)
            prm[...] = total
        else:
            prm[...] = ws[...].astype(F32)

    def step(m, s):
        if inner:
            gather_step(m, s)

    if inner:
        for m in (0, 3):
            gather_z(m)
            gather_x(m)
    for cp in own_pieces:
        cp.start()
    step(0, 1)
    step(3, 1)
    step(0, 2)
    step(3, 2)
    if inner:
        gather_z(1)
    step(0, 3)
    step(3, 3)
    if inner:
        gather_x(1)
    add_parameters()
    cp_tok.wait()
    first_norm(0)
    step(1, 1)
    if inner:
        gather_z(2)
    for b in range(1, nb):
        first_norm(b)
    for cp in own_pieces[:3]:
        cp.wait()
    if inner:
        gather_end(0)
    step(1, 2)
    project(0)
    attend(0)
    out_part(0)
    step(1, 3)
    if inner:
        gather_x(2)
    sum_mid(0, 0)
    step(2, 1)
    project(1)
    attend(1)
    out_part(1)
    step(2, 2)
    cp_cot.wait()
    sum_mid(0, 1)
    step(2, 3)
    if inner:
        gather_end(1)
    for b in range(nb):
        second_norm(b)
        up(b)
        if inner and b == 0:
            gather_end(2)
        if b == nb - 1:
            weight_grad(2, down_grad)
            reduce_start(2, 0)
            reduce_start(2, 1)
        hidden_back(b)
        if b == 0:
            sum_part(1, b, lambda rows: mm(act[rows], mat(2), 1, 1))
        sum_mid(2, b)
    for b in range(1, nb):
        sum_part(1, b, lambda rows: mm(act[rows], mat(2), 1, 1))
    weight_grad(1, up_grad)
    for b in range(nb):
        middle_back(b)
        attend_back(b)
        if b == 0:
            sum_mid(1, 0)
            reduce_start(1, 0)
            reduce_start(1, 1)
        if b == nb - 1:
            weight_grad(0, in_grad)
            reduce_start(0, 1)
            reduce_start(0, 0)
            for q in range(2):
                reduce_far(2, q)
        in_part(b)
        if b == nb - 1:
            small_step(0)
            small_step(1)
        sum_mid(3, b)
        if b == 0:
            for q in range(2):
                reduce_mid(2, q)
    for b in range(1, nb):
        sum_mid(1, b)
    for q in range(2):
        reduce_mid(1, q)
    finish_mixed(0)
    finish_tokens(0)
    for q in range(2):
        reduce_far(1, q)
    small_step(2)
    reduce_mid(0, 1)
    reduce_mid(0, 0)
    for b in range(1, nb):
        finish_tokens(b)
    reduce_far(0, 1)
    reduce_far(0, 0)
    small_step(3)
    reduce_end(2)
    reduce_end(1)
    small_step(4)
    reduce_end(0)
    for b in range(1, nb):
        finish_mixed(b)
    for wait, guard in later:
        if guard is None:
            wait()
        else:
            pl.when(guard)(wait)


def call_kernel(inner, *args):
    rows = args[0].shape[0]
    nb = rows // BLK
    vmem = pl.BlockSpec(memory_space=pltpu.VMEM)
    anywhere = pl.BlockSpec(memory_space=pl.ANY)
    grads = (
        jax.ShapeDtypeStruct((PIECE, D), F32)
        if inner
        else jax.ShapeDtypeStruct((PARTS, PIECE, D), BF16)
    )
    dma = pltpu.SemaphoreType.DMA
    scratch = [
        pltpu.VMEM((rows, D), BF16),
        pltpu.VMEM((rows, D), BF16),
        pltpu.VMEM((3, PARTS, PIECE, D), BF16),
        pltpu.VMEM((PARTS, 16, D), BF16),
        pltpu.VMEM((16, D), F32),
        pltpu.VMEM((rows, D), BF16),
        pltpu.VMEM((3, rows, 128), BF16),
        pltpu.VMEM((3, rows, 128), BF16),
        pltpu.VMEM((3, rows, 128), BF16),
        pltpu.VMEM((3 * nb, BLK, BLK), BF16),
        pltpu.VMEM((rows, 256), BF16),
        pltpu.VMEM((nb, HALF, D), F32),
        pltpu.VMEM((rows, D), BF16),
        pltpu.VMEM((rows, D), BF16),
        pltpu.VMEM((rows, D), F32),
        pltpu.VMEM((rows, D), BF16),
        pltpu.VMEM((rows, D), BF16),
        pltpu.VMEM((nb, HALF, D), F32),
        pltpu.VMEM((rows, 640), BF16),
        pltpu.VMEM((3, BLK, 128), F32),
        pltpu.VMEM((3, BLK, 128), F32),
        pltpu.VMEM((4, nb, 2, HALF, D), BF16),
        pltpu.VMEM((4, nb, HALF, D), BF16),
        pltpu.VMEM((4, nb, HALF, D), BF16),
        pltpu.VMEM((nb, HALF, D), BF16),
        pltpu.VMEM((3, PARTS, PIECE, D), BF16),
        pltpu.VMEM((3, 4, PIECE, D), BF16),
        pltpu.VMEM((3, 4, PIECE, D), BF16),
        pltpu.VMEM((3, 3, PIECE, D), BF16),
        pltpu.VMEM((8, D), F32),
        pltpu.VMEM((3, 8, D), F32),
        pltpu.VMEM((2, 8, D), F32),
        pltpu.VMEM((4, 8, D), F32),
        dma((10,)),
        dma((4, 2, 3)),
        dma((4, 2, 3)),
        dma((4, 4)),
        dma((4, 4)),
        dma((4, nb)),
        dma((4, nb)),
        dma((4, nb)),
        dma((4, nb)),
        dma((2, nb)),
        dma((2, nb)),
        dma((2, nb)),
        dma((2, nb)),
        dma((3, 2, 4)),
        dma((3, 2, 4)),
        dma((3, 2, 3)),
        dma((3, 2, 3)),
        dma((6,)),
        dma((6,)),
    ]
    if inner:
        scratch += [pltpu.VMEM((PIECE, D), BF16), pltpu.VMEM((16, D), BF16), pltpu.VMEM((16, D), F32)]

    def kernel(*refs):
        layer_kernel(inner, nb, refs)

    return pl.pallas_call(
        kernel,
        out_shape=(
            jax.ShapeDtypeStruct((rows, D), BF16),
            jax.ShapeDtypeStruct((rows, D), F32),
            grads,
            grads,
            grads,
            jax.ShapeDtypeStruct((8, D), F32),
        ),
        in_specs=[anywhere, anywhere]
        + ([vmem, vmem, anywhere, anywhere, vmem, vmem, vmem, vmem] if inner else [vmem] * 4)
        + [pl.BlockSpec(memory_space=pltpu.SMEM)],
        out_specs=(anywhere, anywhere, vmem, vmem, vmem, vmem),
        scratch_shapes=scratch,
        compiler_params=pltpu.CompilerParams(
            collective_id=0, has_side_effects=True, vmem_limit_bytes=60 * 2**20
        ),
    )(*args)


def pack_heads(q, k, v, o):
    return jnp.concatenate(
        [
            q[..., :128], k[..., :128], v[..., :128],
            q[..., 128:], k[..., 128:], v[..., 128:], o[..., 128:], o[..., :128],
        ],
        axis=-1,
    )


def unpack_heads(w):
    q = jnp.concatenate([w[..., 0:128], w[..., 384:448]], axis=-1)
    k = jnp.concatenate([w[..., 128:256], w[..., 448:512]], axis=-1)
    v = jnp.concatenate([w[..., 256:384], w[..., 512:576]], axis=-1)
    o = jnp.concatenate([w[..., 640:768], w[..., 576:640]], axis=-1)
    return q, k, v, o


def unpack_kernel(mix_h, tok_h, ga, gu, gd, small, mix_o, tok_o, qkv_o, out_o, up_o, down_o, gains_o, shifts_o, bqkv_o, bup_o, tok_v, mix_v, sem):
    d = lax.axis_index("dp")
    moves = []
    for src, via, dst in ((tok_h, tok_v, tok_o), (mix_h, mix_v, mix_o)):
        for k in range(4):
            rows = slice(k * src.shape[0] // 4, (k + 1) * src.shape[0] // 4)
            sems = sem.at[len(moves)]
            load = pltpu.make_async_copy(src.at[rows], via.at[rows], sems)
            load.start()
            moves.append((load, pltpu.make_async_copy(via.at[rows], dst.at[rows], sems)))
    for load, store in moves:
        load.wait()
        store.start()
    own = gains_o.shape[1]
    for k in range(3):
        qkv_o[k, :, 0:128] = ga[:, 128 * k : 128 * k + 128]
    qkv_o[0, :, 128:192] = ga[:, 384:448]
    qkv_o[1, :, 128:192] = pltpu.roll(ga[:, 384:512], 64, 1)[:, 0:64]
    qkv_o[2, :, 128:192] = ga[:, 512:576]
    fill = jnp.zeros((128 - own, 128), F32)
    out_o[0:128, :] = jnp.concatenate([ga[:, 640:768], fill], axis=0).T[:, 0:own]
    out_o[128:192, :] = jnp.concatenate([ga[:, 512:640], fill], axis=0).T[64:128, 0:own]
    up_o[...] = gu[...]
    down_o[...] = gd[...]
    wide = pltpu.roll(small[...], D - d * own, 1)
    gains_o[...] = wide[0:2, 0:own]
    shifts_o[...] = wide[2:6, 0:own]
    for part in range(2):
        for h, at in enumerate((0, 64, 384) if part == 0 else (256, 320, 512)):
            per = bqkv_o.shape[2]
            slab = small[:, at // 128 * 128 : at // 128 * 128 + 128]
            turned = pltpu.roll(slab, 128 - at % 128 - d * per + 128 * (at % 128 // 64), 1)
            bqkv_o[h, part : part + 1, :] = turned[6:7, 0:per]
    for k in range(6):
        per = bup_o.shape[1]
        turned = pltpu.roll(small[:, 128 * k : 128 * k + 128], 128 - d * per, 1)
        bup_o[k : k + 1, :] = turned[7:8, 0:per]
    for _, store in moves:
        store.wait()


def body(tokens, cotangent, w_qkv, w_out, w_up, w_down, gains, shifts, b_qkv, b_up, clip_lengths):
    own = w_up.shape[0]
    dp = D // own
    if dp == 8:
        mixed, tgrad, ga, gu, gd, small = call_kernel(
            True, tokens, cotangent, w_qkv, w_out, w_up, w_down.T,
            gains, shifts, b_qkv.transpose(1, 0, 2), b_up, clip_lengths,
        )
        vmem = pl.BlockSpec(memory_space=pltpu.VMEM)
        anywhere = pl.BlockSpec(memory_space=pl.ANY)
        like = [mixed, tgrad, w_qkv, w_out, gu, gd, gains, shifts, b_qkv.transpose(1, 0, 2), b_up]
        outs = pl.pallas_call(
            unpack_kernel,
            out_shape=tuple(
                jax.ShapeDtypeStruct(a.shape, BF16 if i == 0 else F32) for i, a in enumerate(like)
            ),
            in_specs=[anywhere, anywhere] + [vmem] * 4,
            out_specs=tuple([anywhere, anywhere] + [vmem] * 8),
            scratch_shapes=[
                pltpu.VMEM(tgrad.shape, F32),
                pltpu.VMEM(mixed.shape, BF16),
                pltpu.SemaphoreType.DMA((8,)),
            ],
        )(mixed, tgrad, ga, gu, gd, small)
        return outs[:5] + (outs[5].T, outs[6], outs[7], outs[8].transpose(1, 0, 2), outs[9])

    d = lax.axis_index("dp")
    wide = jnp.concatenate([gains, shifts], axis=0)
    wide = lax.dynamic_update_slice(jnp.zeros((6, D), BF16), wide, (0, d * own))
    heads = b_qkv.shape[1]
    per_head = b_qkv.shape[2]
    full_head = per_head * dp
    bq = lax.dynamic_update_slice(
        jnp.zeros((2, heads, full_head), BF16), b_qkv, (0, 0, d * per_head)
    ).reshape(2, heads * full_head)
    none = jnp.zeros((heads * full_head,), BF16)
    bq = pack_heads(bq[0], none, bq[1], none)
    bu = lax.dynamic_update_slice(
        jnp.zeros((b_up.shape[0], b_up.shape[1] * dp), BF16), b_up, (0, d * b_up.shape[1])
    ).reshape(1, D)
    ws = jnp.concatenate([wide, bq[None], bu, jnp.zeros((8, D), BF16)], axis=0)
    ws = lax.psum(ws.astype(F32), "dp").astype(BF16)
    wa = pack_heads(w_qkv[0], w_qkv[1], w_qkv[2], w_out.T)
    wa, wu, wd = (
        lax.all_gather(w, "dp", axis=0, tiled=True).reshape(PARTS, PIECE, D)
        for w in (wa, w_up, w_down.T)
    )
    mixed, tgrad, ga, gu, gd, small = call_kernel(
        False, tokens, cotangent, ws, wa, wu, wd, clip_lengths
    )
    ga, gu, gd = (
        lax.psum_scatter(w.astype(F32).reshape(D, D), "dp", scatter_dimension=0, tiled=True)
        for w in (ga, gu, gd)
    )
    small = lax.psum(small, "dp")
    q, k, v, o = unpack_heads(ga)
    wide = lax.dynamic_slice(small[0:6], (0, d * own), (6, own))
    bq, _, bv, _ = unpack_heads(small[6])
    b_qkv_grad = jnp.stack([bq, bv]).reshape(2, heads, full_head)
    b_qkv_grad = lax.dynamic_slice(b_qkv_grad, (0, 0, d * per_head), (2, heads, per_head))
    b_up_grad = lax.dynamic_slice(
        small[7].reshape(b_up.shape[0], -1), (0, d * b_up.shape[1]), b_up.shape
    )
    return (
        mixed,
        tgrad,
        jnp.stack([q, k, v]),
        o.T,
        gu,
        gd.T,
        wide[0:2],
        wide[2:6],
        b_qkv_grad,
        b_up_grad,
    )


def solution(mesh):
    return jax.shard_map(
        body,
        mesh=mesh,
        in_specs=(
            P("dp", None),
            P("dp", None),
            P(None, "dp", "tp"),
            P("tp", "dp"),
            P("dp", "tp"),
            P("tp", "dp"),
            P(None, "dp"),
            P(None, "dp"),
            P(None, "tp", "dp"),
            P("tp", "dp"),
            P("dp", None),
        ),
        out_specs=(
            P("dp", None),
            P("dp", None),
            P(None, "dp", "tp"),
            P("tp", "dp"),
            P("dp", "tp"),
            P("tp", "dp"),
            P(None, "dp"),
            P(None, "dp"),
            P(None, "tp", "dp"),
            P("tp", "dp"),
        ),
        check_vma=False,
    )
```

```python
import functools
import math

import jax
import jax.numpy as jnp
from jax import lax
from jax.experimental import pallas as pl
from jax.experimental.pallas import tpu as pltpu
from jax.sharding import PartitionSpec as P

MESH = pl.DeviceIdType.MESH
F32 = jnp.float32
BF16 = jnp.bfloat16
D = 768
BLK = 512
HALF = 256
PARTS = 8
PIECE = D // PARTS
eps = 1e-06
masked = -1e30


def mm(a, b, ca, cb):
    return lax.dot_general(a, b, (((ca,), (cb,)), ((), ())), preferred_element_type=F32)


def standardize(v):
    centred = v - jnp.mean(v, axis=-1, keepdims=True)
    rstd = lax.rsqrt(jnp.mean(centred * centred, axis=-1, keepdims=True) + eps)
    return centred * rstd, rstd


def norm_back(grad, gain, z, rstd):
    n = grad * gain
    return (
        n - jnp.mean(n, axis=-1, keepdims=True) - z * jnp.mean(n * z, axis=-1, keepdims=True)
    ) * rstd


def layer_kernel(inner, nb, refs):
    if inner:
        (tok_h, cot_h, w_qkv, w_out, wu, wd, gains, shifts, b_qkv, b_up, lens) = refs[:11]
        wa, ws, wt = refs[-3:]
        refs = refs[11:-3]
    else:
        (tok_h, cot_h, ws, wa, wu, wd, lens) = refs[:7]
        refs = refs[7:]
    (mixed_h, tgrad_h, gra_o, gru_o, grd_o, small_o) = refs[:6]
    (
        tok, cot, g, gs, prm, nrm, qh, kh, vh, pr, att, mid, n2, act, dgl, hg, ml, mgr, dqkv,
        dka, dva, pb, rc, ry, mxs, gr, rx, hs, rz, sg, sgc, sgx, sgz,
        lsem, zss, zrs, xss, xrs, css, crs, yss, yrs, nss, nrs, oss, ors, rxs, rxr, rzs, rzr, sms, smr,
    ) = refs[6:]
    d = lax.axis_index("dp")
    t = lax.axis_index("tp")
    z = d // 2
    x = d % 2
    c = t % 2
    xn = d + 1 - 2 * x
    sib = t + 1 - 2 * c
    yn = lax.rem(t + 2, 4)
    later = []

    def remote(src, dst, s, r, dd, tt):
        return pltpu.make_async_remote_copy(
            src_ref=src, dst_ref=dst, send_sem=s, recv_sem=r, device_id=(dd, tt), device_id_type=MESH
        )

    def launch(copy, guard=None):
        if guard is None:
            copy.start()
        else:
            pl.when(guard)(copy.start)
        later.append((copy.wait_send, guard))

    bar = pltpu.get_barrier_semaphore()
    greet = [(d, sib), (d, yn)] + ([(xn, t)] if inner else [])
    greeted = len(greet)
    for who in greet:
        pl.semaphore_signal(bar, 1, device_id=who, device_id_type=MESH)
    if inner:
        for guard, who in ((z < 3, d + 2), (z > 0, d - 2)):

            @pl.when(guard)
            def _():
                pl.semaphore_signal(bar, 1, device_id=(who, t), device_id_type=MESH)

            greeted = greeted + guard.astype(jnp.int32)
    cp_tok = pltpu.make_async_copy(tok_h, tok, lsem.at[0])
    cp_tok.start()
    cp_cot = pltpu.make_async_copy(cot_h, cot, lsem.at[1])
    cp_cot.start()
    if inner:
        def spot(rows, shift):
            i = lax.broadcasted_iota(jnp.int32, (rows, 128), 0)
            return (lax.broadcasted_iota(jnp.int32, (rows, 128), 1) == i + shift).astype(F32).astype(BF16)

        for k in range(3):
            wa[:, 128 * k : 128 * k + 128] = w_qkv[k, :, 0:128]
        q2, k2, v2 = (w_qkv[k, :, 128:192] for k in range(3))
        wa[:, 384:512] = (mm(q2, spot(64, 0), 1, 0) + mm(k2, spot(64, 64), 1, 0)).astype(BF16)
        wa[:, 512:640] = (
            mm(v2, spot(64, 0), 1, 0) + mm(w_out[128:192, :], spot(64, 64), 0, 0)
        ).astype(BF16)
        wa[:, 640:768] = mm(w_out[0:128, :], spot(128, 0), 0, 0).astype(BF16)
        own = gains.shape[1]
        wt[...] = jnp.zeros_like(wt)
        wt[0:2, 0:own] = gains[...].astype(F32)
        wt[2:6, 0:own] = shifts[...].astype(F32)
        wide = pltpu.roll(wt[0:8], d * own, 1)
        wt[...] = jnp.zeros_like(wt)
        wt[0:8] = wide
        per = b_up.shape[1]
        sg[...] = jnp.zeros_like(sg)
        sg[0:6, 0:per] = b_up[...].astype(F32)
        turned = pltpu.roll(sg[0:8, 0:128], d * per, 1)
        for k in range(6):
            wt[7:8, 128 * k : 128 * k + 128] = turned[k : k + 1]
        per = b_qkv.shape[2]
        sg[...] = jnp.zeros_like(sg)
        for h in range(3):
            sg[h : h + 1, 0:per] = b_qkv[h, 0:1].astype(F32)
            sg[3 + h : 4 + h, 0:per] = b_qkv[h, 1:2].astype(F32)
        turned = pltpu.roll(sg[0:8, 0:128], d * per, 1)
        other = pltpu.roll(turned, 64, 1)
        wt[6:7, 0:128] = turned[0:1] + other[1:2]
        wt[6:7, 256:384] = turned[3:4] + other[4:5]
        wt[6:7, 384:512] = turned[2:3]
        wt[6:7, 512:640] = turned[5:6]
        ws[...] = wt[...].astype(BF16)
    pl.semaphore_wait(bar, greeted)

    shards = (wa, wu, wd, ws)

    def slot(m, i):
        return gs.at[i] if m == 3 else g.at[m, i]

    def zcopy(m, side, src, i, s):
        return remote(src, slot(m, i), zss.at[m, side, s], zrs.at[m, side, s], d + 2 - 4 * side, t)

    def xcopy(m, src, i, zsrc):
        return remote(src, slot(m, i), xss.at[m, zsrc], xrs.at[m, zsrc], xn, t)

    def gather_z(m):
        launch(zcopy(m, 0, shards[m], d, 0), z < 3)
        launch(zcopy(m, 1, shards[m], d, 0), z > 0)

    def gather_x(m):
        launch(xcopy(m, shards[m], d, z))

    def gather_step(m, s):
        for side in (0, 1):
            i = d - 2 * s if side == 0 else d + 2 * s
            here = z >= s if side == 0 else z + s <= 3
            onward = z < 3 if side == 0 else z > 0

            @pl.when(here)
            def _():
                zcopy(m, side, slot(m, i), i, s - 1).wait_recv()

            if s < 3:
                launch(zcopy(m, side, slot(m, i), i, s), jnp.logical_and(here, onward))
            launch(xcopy(m, slot(m, i), i, i // 2), here)

    def gather_end(m):
        for k in range(4):
            i = 2 * k + 1 - x
            xcopy(m, slot(m, i), i, k).wait_recv()

    def half_rows(b, j):
        return pl.ds(pl.multiple_of(b * BLK + lax.rem(1 - c + j, 2) * HALF, HALF), HALF)

    def own_rows(b):
        return pl.ds(pl.multiple_of(b * BLK + c * HALF, HALF), HALF)

    def ccopy(st, b):
        return remote(pb.at[st, b, 0], rc.at[st, b], css.at[st, b], crs.at[st, b], d, sib)

    def ycopy(st, b):
        return remote(pb.at[st, b, 1], ry.at[st, b], yss.at[st, b], yrs.at[st, b], d, yn)

    def sum_part(st, b, product):
        def one(j, carry):
            pb[st, b, j] = product(half_rows(b, j)).astype(BF16)

            @pl.when(j == 0)
            def _():
                ccopy(st, b).start()

            return carry

        lax.fori_loop(0, 2, one, 0)
        later.append((ccopy(st, b).wait_send, None))

    def sum_mid(st, b):
        ccopy(st, b).wait_recv()
        pb[st, b, 1] = (pb[st, b, 1].astype(F32) + rc[st, b].astype(F32)).astype(BF16)
        launch(ycopy(st, b))

    def sum_end(st, b):
        ycopy(st, b).wait_recv()
        return pb[st, b, 1].astype(F32) + ry[st, b].astype(F32)

    def share(buf, k, b):
        return remote(buf.at[own_rows(b)], buf.at[own_rows(b)], nss.at[k, b], nrs.at[k, b], d, sib)

    def shared(buf, k, b):
        rows = half_rows(b, 0)
        remote(buf.at[rows], buf.at[rows], nss.at[k, b], nrs.at[k, b], d, sib).wait_recv()

    lane = lax.broadcasted_iota(jnp.int32, (1, 128), 1)
    low = lane < 64

    def mat(m):
        return g[m].reshape(D, D)

    def chunks(b, n, fn, ready=None):
        def one(k, carry):
            i = k
            if ready is not None:
                pl.when(k == n // 2)(ready)
                i = lax.rem(c + k // (n // 2), 2) * (n // 2) + lax.rem(k, n // 2)
            fn(pl.ds(pl.multiple_of(b * BLK + i * (BLK // n), BLK // n), BLK // n), i)
            return carry

        lax.fori_loop(0, n, one, 0)

    def first_norm(b):
        def fn(rows, i):
            zz, _ = standardize(tok[rows].astype(F32))
            nrm[rows] = (zz * prm[0:1] + prm[2:3]).astype(BF16)

        chunks(b, 4, fn)

    def project(b):
        def fn(rows, i):
            p = mm(nrm[rows], mat(0), 1, 0) + prm[6:7]
            s0, s1, s2, s3, s4 = (p[:, 128 * k : 128 * k + 128] for k in range(5))
            for ref, s in ((qh, s0), (kh, s1), (vh, s2)):
                ref[0, rows] = jnp.where(low, s, 0.0).astype(BF16)
                ref[1, rows] = jnp.where(low, 0.0, s).astype(BF16)
            qh[2, rows] = jnp.where(low, s3, 0.0).astype(BF16)
            kh[2, rows] = jnp.where(low, pltpu.roll(s3, 64, 1), 0.0).astype(BF16)
            vh[2, rows] = jnp.where(low, s4, 0.0).astype(BF16)

        chunks(b, 2, fn)

    def attend(b):
        blk = slice(b * BLK, b * BLK + BLK)
        e0 = lens[b, 0]
        e1 = e0 + lens[b, 1]
        e2 = e1 + lens[b, 2]

        def clip_of(pos):
            return (
                (pos >= e0).astype(jnp.int32)
                + (pos >= e1).astype(jnp.int32)
                + (pos >= e2).astype(jnp.int32)
            )

        def fn(rows, i):
            q_clip = clip_of(lax.broadcasted_iota(jnp.int32, (1, HALF), 1) + i * HALF)
            k_clip = clip_of(lax.broadcasted_iota(jnp.int32, (BLK, 1), 0))
            same = q_clip == k_clip
            outs = []
            for h in range(3):
                s = mm(kh[h, blk], qh[h, rows], 1, 1) * 0.125
                s = jnp.where(same, s, masked)
                e = jnp.exp(s - jnp.max(s, axis=0, keepdims=True))
                p = (e / jnp.sum(e, axis=0, keepdims=True)).astype(BF16)
                pr[3 * b + h, :, pl.ds(pl.multiple_of(i * HALF, HALF), HALF)] = p
                outs.append(mm(vh[h, blk], p, 0, 0))
            att[rows, 0:128] = pltpu.roll(outs[2], 64, 0).T.astype(BF16)
            att[rows, 128:256] = (outs[0] + outs[1]).T.astype(BF16)

        chunks(b, 2, fn)

    def out_part(b):
        sum_part(0, b, lambda rows: mm(att[rows], g[0, :, :, 512:768].reshape(D, 256), 1, 1))

    def second_norm(b):
        rows = own_rows(b)
        m = tok[rows].astype(F32) + sum_end(0, b) + prm[4:5]
        mid[b] = m
        zz, _ = standardize(m)
        n2[rows] = (zz * prm[1:2] + prm[3:4]).astype(BF16)
        launch(share(n2, 0, b))

    def up(b):
        def fn(rows, i):
            h = mm(n2[rows], mat(1), 1, 0) + prm[7:8]
            cdf = 0.5 * (1.0 + lax.erf(h * (1.0 / math.sqrt(2.0))))
            act[rows] = (h * cdf).astype(BF16)
            dgl[rows] = cdf + h * (jnp.exp(-0.5 * h * h) * (1.0 / math.sqrt(2.0 * math.pi)))

        chunks(b, 4, fn, lambda: shared(n2, 0, b))

    def hidden_back(b):
        def product(rows):
            low_grad = (mm(cot[rows], mat(2), 1, 0) * dgl[rows]).astype(BF16)
            hg[rows] = low_grad
            sg[7:8] += jnp.sum(low_grad.astype(F32), axis=0, keepdims=True)
            return mm(low_grad, mat(1), 1, 1)

        sum_part(2, b, product)

    def middle_back(b):
        rows = own_rows(b)
        total = sum_end(2, b)
        zz, rstd = standardize(mid[b])
        out_grad = cot[rows].astype(F32)
        m = out_grad + norm_back(total, prm[1:2], zz, rstd)
        mgr[b] = m
        ml[rows] = m.astype(BF16)
        launch(share(ml, 1, b))
        sg[1:2] += jnp.sum(total * zz, axis=0, keepdims=True)
        sg[3:4] += jnp.sum(total, axis=0, keepdims=True)
        sg[4:5] += jnp.sum(m, axis=0, keepdims=True)
        sg[5:6] += jnp.sum(out_grad, axis=0, keepdims=True)

    def attend_back(b):
        blk = slice(b * BLK, b * BLK + BLK)
        dka[...] = jnp.zeros_like(dka)
        dva[...] = jnp.zeros_like(dva)

        def fn(rows, i):
            da = mm(ml[rows], g[0, :, :, 512:768].reshape(D, 256), 1, 0)
            d2, d01 = da[:, 0:128], da[:, 128:256]
            dos = (
                jnp.where(low, d01, 0.0).astype(BF16),
                jnp.where(low, 0.0, d01).astype(BF16),
                jnp.where(low, pltpu.roll(d2, 64, 1), 0.0).astype(BF16),
            )
            dqs = []
            for h in range(3):
                p = pr[3 * b + h, :, pl.ds(pl.multiple_of(i * HALF, HALF), HALF)]
                pf = p.astype(F32)
                dp = mm(vh[h, blk], dos[h], 1, 1)
                ds = (pf * (dp - jnp.sum(pf * dp, axis=0, keepdims=True))).astype(BF16)
                dqs.append(mm(kh[h, blk], ds, 0, 0))
                dka[h] += mm(ds, qh[h, rows], 1, 0)
                dva[h] += mm(p, dos[h], 1, 0)
            dqkv[rows, 0:128] = ((dqs[0] + dqs[1]) * 0.125).T.astype(BF16)
            dqkv[rows, 384:512] = (dqs[2] * 0.125).T.astype(BF16)

        chunks(b, 2, fn, lambda: shared(ml, 1, b))
        dqkv[blk, 128:256] = ((dka[0] + dka[1]) * 0.125).astype(BF16)
        dqkv[blk, 256:384] = (dva[0] + dva[1]).astype(BF16)
        dqkv[blk, 384:512] = (
            dqkv[blk, 384:512].astype(F32) + pltpu.roll(dka[2], 64, 1) * 0.125
        ).astype(BF16)
        dqkv[blk, 512:640] = dva[2].astype(BF16)
        sg[6:7, 0:640] += jnp.sum(dqkv[blk, 0:640].astype(F32), axis=0, keepdims=True)

    def in_part(b):
        def product(rows):
            part = mm(dqkv[rows, 0:640], g[0, :, :, 0:640].reshape(D, 640), 1, 1)
            zz, _ = standardize(tok[rows].astype(F32))
            sg[0:1] += jnp.sum(part * zz, axis=0, keepdims=True)
            sg[2:3] += jnp.sum(part, axis=0, keepdims=True)
            return part

        sum_part(3, b, product)

    def out_copies(k, buf, out, b):
        mine = pltpu.make_async_copy(buf.at[b], out.at[own_rows(b)], lsem.at[2 + 2 * k + b])
        mine.start()
        later.append((mine.wait, None))
        theirs = remote(buf.at[b], out.at[own_rows(b)], oss.at[k, b], ors.at[k, b], d, sib)
        launch(theirs)
        rows = half_rows(b, 0)
        back = remote(buf.at[b], out.at[rows], oss.at[k, b], ors.at[k, b], d, sib)
        later.append((back.wait_recv, None))

    def finish_mixed(b):
        mxs[b] = (mid[b] + sum_end(1, b) + prm[5:6]).astype(BF16)
        out_copies(0, mxs, mixed_h, b)

    def finish_tokens(b):
        total = sum_end(3, b)
        zz, rstd = standardize(tok[own_rows(b)].astype(F32))
        mgr[b] = mgr[b] + norm_back(total, prm[0:1], zz, rstd)
        out_copies(1, mgr, tgrad_h, b)

    def cut(q):
        return slice(384 * q, 384 * q + 384)

    def xred(m, q, k):
        return remote(
            gr.at[m, 2 * k + 1 - x, :, cut(q)], rx.at[m, k, :, cut(q)],
            rxs.at[m, q, k], rxr.at[m, q, k], xn, t,
        )

    zp = z + 1 - 2 * lax.rem(z, 2)
    zf = lax.rem(z + 2, 4)
    zpf = lax.rem(zp + 2, 4)

    def zred(m, q, k):
        ahead = lax.rem(z + k + 1, 4)
        src, to = ((zp, zp), (zpf, zp), (zf, zf))[k] if m < 2 else (ahead, ahead)
        return remote(
            hs.at[m, src, :, cut(q)], rz.at[m, k, :, cut(q)],
            rzs.at[m, q, k], rzr.at[m, q, k], 2 * to + x, t,
        )

    def weight_grad(m, product):
        for half in range(2):
            gr[m, 4 * half : 4 * half + 4] = product(cut(half)).astype(BF16).reshape(4, PIECE, D)

    def reduce_start(m, q):
        if inner:
            for k in range(4):
                launch(xred(m, q, k))

    outs = (gra_o, gru_o, grd_o)

    def reduce_mid(m, q):
        if not inner:
            return
        places = ((1, zpf), (0, zp), (2, zf), (3, z))
        if m == 2:
            places = tuple((k, lax.rem(z + k + 1, 4)) for k in (1, 0, 2, 3))
        for k, zd in places:
            xred(m, q, zd).wait_recv()
            both = gr[m, 2 * zd + x, :, cut(q)].astype(F32) + rx[m, zd, :, cut(q)].astype(F32)
            if k < 3:
                hs[m, zd, :, cut(q)] = both.astype(BF16)
            else:
                outs[m][:, cut(q)] = both
            if k < (2 if m < 2 else 3):
                launch(zred(m, q, k))

    def reduce_far(m, q):
        if not inner or m == 2:
            return
        zred(m, q, 1).wait_recv()
        far = hs[m, zf, :, cut(q)].astype(F32) + rz[m, 1, :, cut(q)].astype(F32)
        hs[m, zf, :, cut(q)] = far.astype(BF16)
        launch(zred(m, q, 2))

    def reduce_end(m):
        if not inner:
            outs[m][...] = gr[m]
            return
        for q in range(2):
            for k in (0, 2) if m < 2 else (0, 1, 2):
                zred(m, q, k).wait_recv()
                outs[m][:, cut(q)] += rz[m, k, :, cut(q)].astype(F32)

    def down_grad(cols):
        return mm(cot[:, cols], act[...], 0, 0)

    def up_grad(cols):
        return mm(n2[:, cols], hg[...], 0, 0)

    def in_grad(cols):
        a1 = mm(nrm[:, cols], dqkv[:, 0:640], 0, 0)
        a2 = mm(ml[:, cols], att[...], 0, 0)
        return jnp.concatenate(
            [a1[:, 0:512], a1[:, 512:640] + a2[:, 0:128], a2[:, 128:256]], axis=1
        )

    row = lax.broadcasted_iota(jnp.int32, (8, 1), 0)

    def small_c():
        return remote(sg, sgc.at[0], sms.at[0], smr.at[0], d, sib)

    def small_y():
        return remote(sgc.at[1], sgc.at[2], sms.at[1], smr.at[1], d, yn)

    def small_x():
        return remote(sgx.at[0], sgx.at[1], sms.at[2], smr.at[2], xn, t)

    def small_z(k):
        return remote(
            sgz.at[0], sgz.at[k], sms.at[2 + k], smr.at[2 + k], lax.rem(d + 2 * k, 8), t
        )

    def small_step(n):
        if n == 0:
            launch(small_c())
        elif n == 1:
            small_c().wait_recv()
            sgc[1] = sg[...] + jnp.where(row < 6, sgc[0], 0.0)
            launch(small_y())
        elif n == 2:
            small_y().wait_recv()
            both = sgc[1] + jnp.where(jnp.logical_or(row == 0, row == 2), sgc[2], 0.0)
            if inner:
                sgx[0] = both
                launch(small_x())
            else:
                small_o[...] = both
        elif n == 3 and inner:
            small_x().wait_recv()
            sgz[0] = sgx[0] + sgx[1]
            for k in (1, 2, 3):
                launch(small_z(k))
        elif n == 4 and inner:
            for k in (1, 2, 3):
                small_z(k).wait_recv()
            small_o[...] = (sgz[0] + sgz[1]) + (sgz[2] + sgz[3])

    sg[...] = jnp.zeros_like(sg)
    own_pieces = []
    for m in range(3 if not inner else 4):
        own_pieces.append(
            pltpu.make_async_copy(shards[m], slot(m, d) if inner else g.at[m], lsem.at[6 + m])
        )

    def add_parameters():
        if inner:
            own_pieces[3].wait()
            gather_end(3)
            total = gs[0].astype(F32)
            for i in range(1, PARTS):
                total = total + gs[i].astype(F32)
            prm[...] = total
        else:
            prm[...] = ws[...].astype(F32)

    def step(m, s):
        if inner:
            gather_step(m, s)

    if inner:
        for m in (0, 3):
            gather_z(m)
            gather_x(m)
    for cp in own_pieces:
        cp.start()
    step(0, 1)
    step(3, 1)
    step(0, 2)
    step(3, 2)
    if inner:
        gather_z(1)
    step(0, 3)
    step(3, 3)
    if inner:
        gather_x(1)
    step(1, 1)
    add_parameters()
    cp_tok.wait()
    first_norm(0)
    if inner:
        gather_z(2)
    for b in range(1, nb):
        first_norm(b)
    for cp in own_pieces[:3]:
        cp.wait()
    if inner:
        gather_end(0)
    step(1, 2)
    project(0)
    attend(0)
    out_part(0)
    step(1, 3)
    if inner:
        gather_x(2)
    sum_mid(0, 0)
    step(2, 1)
    project(1)
    attend(1)
    out_part(1)
    step(2, 2)
    cp_cot.wait()
    sum_mid(0, 1)
    step(2, 3)
    if inner:
        gather_end(1)
    for b in range(nb):
        second_norm(b)
        up(b)
        if inner and b == 0:
            gather_end(2)
        if b == nb - 1:
            weight_grad(2, down_grad)
            reduce_start(2, 0)
            reduce_start(2, 1)
        hidden_back(b)
        if b == 0:
            sum_part(1, b, lambda rows: mm(act[rows], mat(2), 1, 1))
        sum_mid(2, b)
    for b in range(1, nb):
        sum_part(1, b, lambda rows: mm(act[rows], mat(2), 1, 1))
    weight_grad(1, up_grad)
    for b in range(nb):
        middle_back(b)
        attend_back(b)
        if b == 0:
            sum_mid(1, 0)
            reduce_start(1, 0)
            reduce_start(1, 1)
        if b == nb - 1:
            weight_grad(0, in_grad)
            reduce_start(0, 1)
            reduce_start(0, 0)
            for q in range(2):
                reduce_far(2, q)
        in_part(b)
        if b == nb - 1:
            small_step(0)
            small_step(1)
        sum_mid(3, b)
        if b == 0:
            for q in range(2):
                reduce_mid(2, q)
    for b in range(1, nb):
        sum_mid(1, b)
    for q in range(2):
        reduce_mid(1, q)
    finish_mixed(0)
    finish_tokens(0)
    for q in range(2):
        reduce_far(1, q)
    small_step(2)
    reduce_mid(0, 1)
    reduce_mid(0, 0)
    for b in range(1, nb):
        finish_tokens(b)
    reduce_far(0, 1)
    reduce_far(0, 0)
    small_step(3)
    reduce_end(2)
    reduce_end(1)
    small_step(4)
    reduce_end(0)
    for b in range(1, nb):
        finish_mixed(b)
    for wait, guard in later:
        if guard is None:
            wait()
        else:
            pl.when(guard)(wait)


def call_kernel(inner, *args):
    rows = args[0].shape[0]
    nb = rows // BLK
    vmem = pl.BlockSpec(memory_space=pltpu.VMEM)
    anywhere = pl.BlockSpec(memory_space=pl.ANY)
    grads = (
        jax.ShapeDtypeStruct((PIECE, D), F32)
        if inner
        else jax.ShapeDtypeStruct((PARTS, PIECE, D), BF16)
    )
    dma = pltpu.SemaphoreType.DMA
    scratch = [
        pltpu.VMEM((rows, D), BF16),
        pltpu.VMEM((rows, D), BF16),
        pltpu.VMEM((3, PARTS, PIECE, D), BF16),
        pltpu.VMEM((PARTS, 16, D), BF16),
        pltpu.VMEM((16, D), F32),
        pltpu.VMEM((rows, D), BF16),
        pltpu.VMEM((3, rows, 128), BF16),
        pltpu.VMEM((3, rows, 128), BF16),
        pltpu.VMEM((3, rows, 128), BF16),
        pltpu.VMEM((3 * nb, BLK, BLK), BF16),
        pltpu.VMEM((rows, 256), BF16),
        pltpu.VMEM((nb, HALF, D), F32),
        pltpu.VMEM((rows, D), BF16),
        pltpu.VMEM((rows, D), BF16),
        pltpu.VMEM((rows, D), F32),
        pltpu.VMEM((rows, D), BF16),
        pltpu.VMEM((rows, D), BF16),
        pltpu.VMEM((nb, HALF, D), F32),
        pltpu.VMEM((rows, 640), BF16),
        pltpu.VMEM((3, BLK, 128), F32),
        pltpu.VMEM((3, BLK, 128), F32),
        pltpu.VMEM((4, nb, 2, HALF, D), BF16),
        pltpu.VMEM((4, nb, HALF, D), BF16),
        pltpu.VMEM((4, nb, HALF, D), BF16),
        pltpu.VMEM((nb, HALF, D), BF16),
        pltpu.VMEM((3, PARTS, PIECE, D), BF16),
        pltpu.VMEM((3, 4, PIECE, D), BF16),
        pltpu.VMEM((3, 4, PIECE, D), BF16),
        pltpu.VMEM((3, 3, PIECE, D), BF16),
        pltpu.VMEM((8, D), F32),
        pltpu.VMEM((3, 8, D), F32),
        pltpu.VMEM((2, 8, D), F32),
        pltpu.VMEM((4, 8, D), F32),
        dma((10,)),
        dma((4, 2, 3)),
        dma((4, 2, 3)),
        dma((4, 4)),
        dma((4, 4)),
        dma((4, nb)),
        dma((4, nb)),
        dma((4, nb)),
        dma((4, nb)),
        dma((2, nb)),
        dma((2, nb)),
        dma((2, nb)),
        dma((2, nb)),
        dma((3, 2, 4)),
        dma((3, 2, 4)),
        dma((3, 2, 3)),
        dma((3, 2, 3)),
        dma((6,)),
        dma((6,)),
    ]
    if inner:
        scratch += [pltpu.VMEM((PIECE, D), BF16), pltpu.VMEM((16, D), BF16), pltpu.VMEM((16, D), F32)]

    def kernel(*refs):
        layer_kernel(inner, nb, refs)

    return pl.pallas_call(
        kernel,
        out_shape=(
            jax.ShapeDtypeStruct((rows, D), BF16),
            jax.ShapeDtypeStruct((rows, D), F32),
            grads,
            grads,
            grads,
            jax.ShapeDtypeStruct((8, D), F32),
        ),
        in_specs=[anywhere, anywhere]
        + ([vmem, vmem, anywhere, anywhere, vmem, vmem, vmem, vmem] if inner else [vmem] * 4)
        + [pl.BlockSpec(memory_space=pltpu.SMEM)],
        out_specs=(anywhere, anywhere, vmem, vmem, vmem, vmem),
        scratch_shapes=scratch,
        compiler_params=pltpu.CompilerParams(
            collective_id=0, has_side_effects=True, vmem_limit_bytes=60 * 2**20
        ),
    )(*args)


def pack_heads(q, k, v, o):
    return jnp.concatenate(
        [
            q[..., :128], k[..., :128], v[..., :128],
            q[..., 128:], k[..., 128:], v[..., 128:], o[..., 128:], o[..., :128],
        ],
        axis=-1,
    )


def unpack_heads(w):
    q = jnp.concatenate([w[..., 0:128], w[..., 384:448]], axis=-1)
    k = jnp.concatenate([w[..., 128:256], w[..., 448:512]], axis=-1)
    v = jnp.concatenate([w[..., 256:384], w[..., 512:576]], axis=-1)
    o = jnp.concatenate([w[..., 640:768], w[..., 576:640]], axis=-1)
    return q, k, v, o


def unpack_kernel(mix_h, tok_h, ga, gu, gd, small, mix_o, tok_o, qkv_o, out_o, up_o, down_o, gains_o, shifts_o, bqkv_o, bup_o, tok_v, mix_v, sem):
    d = lax.axis_index("dp")
    moves = []
    for src, via, dst in ((tok_h, tok_v, tok_o), (mix_h, mix_v, mix_o)):
        for k in range(2):
            rows = slice(k * src.shape[0] // 2, (k + 1) * src.shape[0] // 2)
            sems = sem.at[len(moves)]
            load = pltpu.make_async_copy(src.at[rows], via.at[rows], sems)
            load.start()
            moves.append((load, pltpu.make_async_copy(via.at[rows], dst.at[rows], sems)))
    for load, store in moves:
        load.wait()
        store.start()
    own = gains_o.shape[1]
    for k in range(3):
        qkv_o[k, :, 0:128] = ga[:, 128 * k : 128 * k + 128]
    qkv_o[0, :, 128:192] = ga[:, 384:448]
    qkv_o[1, :, 128:192] = pltpu.roll(ga[:, 384:512], 64, 1)[:, 0:64]
    qkv_o[2, :, 128:192] = ga[:, 512:576]
    fill = jnp.zeros((128 - own, 128), F32)
    out_o[0:128, :] = jnp.concatenate([ga[:, 640:768], fill], axis=0).T[:, 0:own]
    out_o[128:192, :] = jnp.concatenate([ga[:, 512:640], fill], axis=0).T[64:128, 0:own]
    up_o[...] = gu[...]
    down_o[...] = gd[...]
    wide = pltpu.roll(small[...], D - d * own, 1)
    gains_o[...] = wide[0:2, 0:own]
    shifts_o[...] = wide[2:6, 0:own]
    for part in range(2):
        for h, at in enumerate((0, 64, 384) if part == 0 else (256, 320, 512)):
            per = bqkv_o.shape[2]
            slab = small[:, at // 128 * 128 : at // 128 * 128 + 128]
            turned = pltpu.roll(slab, 128 - at % 128 - d * per + 128 * (at % 128 // 64), 1)
            bqkv_o[h, part : part + 1, :] = turned[6:7, 0:per]
    for k in range(6):
        per = bup_o.shape[1]
        turned = pltpu.roll(small[:, 128 * k : 128 * k + 128], 128 - d * per, 1)
        bup_o[k : k + 1, :] = turned[7:8, 0:per]
    for _, store in moves:
        store.wait()


def body(tokens, cotangent, w_qkv, w_out, w_up, w_down, gains, shifts, b_qkv, b_up, clip_lengths):
    own = w_up.shape[0]
    dp = D // own
    if dp == 8:
        mixed, tgrad, ga, gu, gd, small = call_kernel(
            True, tokens, cotangent, w_qkv, w_out, w_up, w_down.T,
            gains, shifts, b_qkv.transpose(1, 0, 2), b_up, clip_lengths,
        )
        vmem = pl.BlockSpec(memory_space=pltpu.VMEM)
        anywhere = pl.BlockSpec(memory_space=pl.ANY)
        like = [mixed, tgrad, w_qkv, w_out, gu, gd, gains, shifts, b_qkv.transpose(1, 0, 2), b_up]
        outs = pl.pallas_call(
            unpack_kernel,
            out_shape=tuple(
                jax.ShapeDtypeStruct(a.shape, BF16 if i == 0 else F32) for i, a in enumerate(like)
            ),
            in_specs=[anywhere, anywhere] + [vmem] * 4,
            out_specs=tuple([anywhere, anywhere] + [vmem] * 8),
            scratch_shapes=[
                pltpu.VMEM(tgrad.shape, F32),
                pltpu.VMEM(mixed.shape, BF16),
                pltpu.SemaphoreType.DMA((8,)),
            ],
        )(mixed, tgrad, ga, gu, gd, small)
        return outs[:5] + (outs[5].T, outs[6], outs[7], outs[8].transpose(1, 0, 2), outs[9])

    d = lax.axis_index("dp")
    wide = jnp.concatenate([gains, shifts], axis=0)
    wide = lax.dynamic_update_slice(jnp.zeros((6, D), BF16), wide, (0, d * own))
    heads = b_qkv.shape[1]
    per_head = b_qkv.shape[2]
    full_head = per_head * dp
    bq = lax.dynamic_update_slice(
        jnp.zeros((2, heads, full_head), BF16), b_qkv, (0, 0, d * per_head)
    ).reshape(2, heads * full_head)
    none = jnp.zeros((heads * full_head,), BF16)
    bq = pack_heads(bq[0], none, bq[1], none)
    bu = lax.dynamic_update_slice(
        jnp.zeros((b_up.shape[0], b_up.shape[1] * dp), BF16), b_up, (0, d * b_up.shape[1])
    ).reshape(1, D)
    ws = jnp.concatenate([wide, bq[None], bu, jnp.zeros((8, D), BF16)], axis=0)
    ws = lax.psum(ws.astype(F32), "dp").astype(BF16)
    wa = pack_heads(w_qkv[0], w_qkv[1], w_qkv[2], w_out.T)
    wa, wu, wd = (
        lax.all_gather(w, "dp", axis=0, tiled=True).reshape(PARTS, PIECE, D)
        for w in (wa, w_up, w_down.T)
    )
    mixed, tgrad, ga, gu, gd, small = call_kernel(
        False, tokens, cotangent, ws, wa, wu, wd, clip_lengths
    )
    ga, gu, gd = (
        lax.psum_scatter(w.astype(F32).reshape(D, D), "dp", scatter_dimension=0, tiled=True)
        for w in (ga, gu, gd)
    )
    small = lax.psum(small, "dp")
    q, k, v, o = unpack_heads(ga)
    wide = lax.dynamic_slice(small[0:6], (0, d * own), (6, own))
    bq, _, bv, _ = unpack_heads(small[6])
    b_qkv_grad = jnp.stack([bq, bv]).reshape(2, heads, full_head)
    b_qkv_grad = lax.dynamic_slice(b_qkv_grad, (0, 0, d * per_head), (2, heads, per_head))
    b_up_grad = lax.dynamic_slice(
        small[7].reshape(b_up.shape[0], -1), (0, d * b_up.shape[1]), b_up.shape
    )
    return (
        mixed,
        tgrad,
        jnp.stack([q, k, v]),
        o.T,
        gu,
        gd.T,
        wide[0:2],
        wide[2:6],
        b_qkv_grad,
        b_up_grad,
    )


def solution(mesh):
    return jax.shard_map(
        body,
        mesh=mesh,
        in_specs=(
            P("dp", None),
            P("dp", None),
            P(None, "dp", "tp"),
            P("tp", "dp"),
            P("dp", "tp"),
            P("tp", "dp"),
            P(None, "dp"),
            P(None, "dp"),
            P(None, "tp", "dp"),
            P("tp", "dp"),
            P("dp", None),
        ),
        out_specs=(
            P("dp", None),
            P("dp", None),
            P(None, "dp", "tp"),
            P("tp", "dp"),
            P("dp", "tp"),
            P("tp", "dp"),
            P(None, "dp"),
            P(None, "dp"),
            P(None, "tp", "dp"),
            P("tp", "dp"),
        ),
        check_vma=False,
    )
```

```python
import functools
import math

import jax
import jax.numpy as jnp
from jax import lax
from jax.experimental import pallas as pl
from jax.experimental.pallas import tpu as pltpu
from jax.sharding import PartitionSpec as P

MESH = pl.DeviceIdType.MESH
F32 = jnp.float32
BF16 = jnp.bfloat16
D = 768
BLK = 512
HALF = 256
PARTS = 8
PIECE = D // PARTS
eps = 1e-06
masked = -1e30


def mm(a, b, ca, cb):
    return lax.dot_general(a, b, (((ca,), (cb,)), ((), ())), preferred_element_type=F32)


def standardize(v):
    centred = v - jnp.mean(v, axis=-1, keepdims=True)
    rstd = lax.rsqrt(jnp.mean(centred * centred, axis=-1, keepdims=True) + eps)
    return centred * rstd, rstd


def norm_back(grad, gain, z, rstd):
    n = grad * gain
    return (
        n - jnp.mean(n, axis=-1, keepdims=True) - z * jnp.mean(n * z, axis=-1, keepdims=True)
    ) * rstd


def layer_kernel(inner, nb, refs):
    if inner:
        (tok_h, cot_h, w_qkv, w_out, wu, wd, gains, shifts, b_qkv, b_up, lens) = refs[:11]
        wa, ws, wt = refs[-3:]
        refs = refs[11:-3]
    else:
        (tok_h, cot_h, ws, wa, wu, wd, lens) = refs[:7]
        refs = refs[7:]
    (mixed_h, tgrad_h, gra_o, gru_o, grd_o, small_o) = refs[:6]
    (
        tok, cot, g, gs, prm, nrm, qh, kh, vh, pr, att, mid, n2, act, dgl, hg, ml, mgr, dqkv,
        dka, dva, pb, rc, ry, mxs, gr, rx, hs, rz, sg, sgc, sgx, sgz,
        lsem, zss, zrs, xss, xrs, css, crs, yss, yrs, nss, nrs, oss, ors, rxs, rxr, rzs, rzr, sms, smr,
    ) = refs[6:]
    d = lax.axis_index("dp")
    t = lax.axis_index("tp")
    z = d // 2
    x = d % 2
    c = t % 2
    xn = d + 1 - 2 * x
    sib = t + 1 - 2 * c
    yn = lax.rem(t + 2, 4)
    later = []

    def remote(src, dst, s, r, dd, tt):
        return pltpu.make_async_remote_copy(
            src_ref=src, dst_ref=dst, send_sem=s, recv_sem=r, device_id=(dd, tt), device_id_type=MESH
        )

    def launch(copy, guard=None):
        if guard is None:
            copy.start()
        else:
            pl.when(guard)(copy.start)
        later.append((copy.wait_send, guard))

    bar = pltpu.get_barrier_semaphore()
    greet = [(d, sib), (d, yn)] + ([(xn, t)] if inner else [])
    greeted = len(greet)
    for who in greet:
        pl.semaphore_signal(bar, 1, device_id=who, device_id_type=MESH)
    if inner:
        for guard, who in ((z < 3, d + 2), (z > 0, d - 2)):

            @pl.when(guard)
            def _():
                pl.semaphore_signal(bar, 1, device_id=(who, t), device_id_type=MESH)

            greeted = greeted + guard.astype(jnp.int32)
    cp_tok = pltpu.make_async_copy(tok_h, tok, lsem.at[0])
    cp_tok.start()
    cp_cot = pltpu.make_async_copy(cot_h, cot, lsem.at[1])
    cp_cot.start()
    if inner:
        def spot(rows, shift):
            i = lax.broadcasted_iota(jnp.int32, (rows, 128), 0)
            return (lax.broadcasted_iota(jnp.int32, (rows, 128), 1) == i + shift).astype(F32).astype(BF16)

        for k in range(3):
            wa[:, 128 * k : 128 * k + 128] = w_qkv[k, :, 0:128]
        q2, k2, v2 = (w_qkv[k, :, 128:192] for k in range(3))
        wa[:, 384:512] = (mm(q2, spot(64, 0), 1, 0) + mm(k2, spot(64, 64), 1, 0)).astype(BF16)
        wa[:, 512:640] = (
            mm(v2, spot(64, 0), 1, 0) + mm(w_out[128:192, :], spot(64, 64), 0, 0)
        ).astype(BF16)
        wa[:, 640:768] = mm(w_out[0:128, :], spot(128, 0), 0, 0).astype(BF16)
        own = gains.shape[1]
        wt[...] = jnp.zeros_like(wt)
        wt[0:2, 0:own] = gains[...].astype(F32)
        wt[2:6, 0:own] = shifts[...].astype(F32)
        wide = pltpu.roll(wt[0:8], d * own, 1)
        wt[...] = jnp.zeros_like(wt)
        wt[0:8] = wide
        per = b_up.shape[1]
        sg[...] = jnp.zeros_like(sg)
        sg[0:6, 0:per] = b_up[...].astype(F32)
        turned = pltpu.roll(sg[0:8, 0:128], d * per, 1)
        for k in range(6):
            wt[7:8, 128 * k : 128 * k + 128] = turned[k : k + 1]
        per = b_qkv.shape[2]
        sg[...] = jnp.zeros_like(sg)
        for h in range(3):
            sg[h : h + 1, 0:per] = b_qkv[h, 0:1].astype(F32)
            sg[3 + h : 4 + h, 0:per] = b_qkv[h, 1:2].astype(F32)
        turned = pltpu.roll(sg[0:8, 0:128], d * per, 1)
        other = pltpu.roll(turned, 64, 1)
        wt[6:7, 0:128] = turned[0:1] + other[1:2]
        wt[6:7, 256:384] = turned[3:4] + other[4:5]
        wt[6:7, 384:512] = turned[2:3]
        wt[6:7, 512:640] = turned[5:6]
        ws[...] = wt[...].astype(BF16)
    pl.semaphore_wait(bar, greeted)

    shards = (wa, wu, wd, ws)

    def slot(m, i):
        return gs.at[i] if m == 3 else g.at[m, i]

    def zcopy(m, side, src, i, s):
        return remote(src, slot(m, i), zss.at[m, side, s], zrs.at[m, side, s], d + 2 - 4 * side, t)

    def xcopy(m, src, i, zsrc):
        return remote(src, slot(m, i), xss.at[m, zsrc], xrs.at[m, zsrc], xn, t)

    def gather_z(m):
        launch(zcopy(m, 0, shards[m], d, 0), z < 3)
        launch(zcopy(m, 1, shards[m], d, 0), z > 0)

    def gather_x(m):
        launch(xcopy(m, shards[m], d, z))

    def gather_step(m, s):
        for side in (0, 1):
            i = d - 2 * s if side == 0 else d + 2 * s
            here = z >= s if side == 0 else z + s <= 3
            onward = z < 3 if side == 0 else z > 0

            @pl.when(here)
            def _():
                zcopy(m, side, slot(m, i), i, s - 1).wait_recv()

            if s < 3:
                launch(zcopy(m, side, slot(m, i), i, s), jnp.logical_and(here, onward))
            launch(xcopy(m, slot(m, i), i, i // 2), here)

    def gather_end(m):
        for k in range(4):
            i = 2 * k + 1 - x
            xcopy(m, slot(m, i), i, k).wait_recv()

    def half_rows(b, j):
        return pl.ds(pl.multiple_of(b * BLK + lax.rem(1 - c + j, 2) * HALF, HALF), HALF)

    def own_rows(b):
        return pl.ds(pl.multiple_of(b * BLK + c * HALF, HALF), HALF)

    def ccopy(st, b):
        return remote(pb.at[st, b, 0], rc.at[st, b], css.at[st, b], crs.at[st, b], d, sib)

    def ycopy(st, b):
        return remote(pb.at[st, b, 1], ry.at[st, b], yss.at[st, b], yrs.at[st, b], d, yn)

    def sum_part(st, b, product):
        def one(j, carry):
            pb[st, b, j] = product(half_rows(b, j)).astype(BF16)

            @pl.when(j == 0)
            def _():
                ccopy(st, b).start()

            return carry

        lax.fori_loop(0, 2, one, 0)
        later.append((ccopy(st, b).wait_send, None))

    def sum_mid(st, b):
        ccopy(st, b).wait_recv()
        pb[st, b, 1] = (pb[st, b, 1].astype(F32) + rc[st, b].astype(F32)).astype(BF16)
        launch(ycopy(st, b))

    def sum_end(st, b):
        ycopy(st, b).wait_recv()
        return pb[st, b, 1].astype(F32) + ry[st, b].astype(F32)

    def share(buf, k, b):
        return remote(buf.at[own_rows(b)], buf.at[own_rows(b)], nss.at[k, b], nrs.at[k, b], d, sib)

    def shared(buf, k, b):
        rows = half_rows(b, 0)
        remote(buf.at[rows], buf.at[rows], nss.at[k, b], nrs.at[k, b], d, sib).wait_recv()

    lane = lax.broadcasted_iota(jnp.int32, (1, 128), 1)
    low = lane < 64

    def mat(m):
        return g[m].reshape(D, D)

    def chunks(b, n, fn, ready=None):
        def one(k, carry):
            i = k
            if ready is not None:
                pl.when(k == n // 2)(ready)
                i = lax.rem(c + k // (n // 2), 2) * (n // 2) + lax.rem(k, n // 2)
            fn(pl.ds(pl.multiple_of(b * BLK + i * (BLK // n), BLK // n), BLK // n), i)
            return carry

        lax.fori_loop(0, n, one, 0)

    def first_norm(b):
        def fn(rows, i):
            zz, _ = standardize(tok[rows].astype(F32))
            nrm[rows] = (zz * prm[0:1] + prm[2:3]).astype(BF16)

        chunks(b, 4, fn)

    def project(b):
        def fn(rows, i):
            p = mm(nrm[rows], mat(0), 1, 0) + prm[6:7]
            s0, s1, s2, s3, s4 = (p[:, 128 * k : 128 * k + 128] for k in range(5))
            for ref, s in ((qh, s0), (kh, s1), (vh, s2)):
                ref[0, rows] = jnp.where(low, s, 0.0).astype(BF16)
                ref[1, rows] = jnp.where(low, 0.0, s).astype(BF16)
            qh[2, rows] = jnp.where(low, s3, 0.0).astype(BF16)
            kh[2, rows] = jnp.where(low, pltpu.roll(s3, 64, 1), 0.0).astype(BF16)
            vh[2, rows] = jnp.where(low, s4, 0.0).astype(BF16)

        chunks(b, 2, fn)

    def attend(b):
        blk = slice(b * BLK, b * BLK + BLK)
        e0 = lens[b, 0]
        e1 = e0 + lens[b, 1]
        e2 = e1 + lens[b, 2]

        def clip_of(pos):
            return (
                (pos >= e0).astype(jnp.int32)
                + (pos >= e1).astype(jnp.int32)
                + (pos >= e2).astype(jnp.int32)
            )

        def fn(rows, i):
            q_clip = clip_of(lax.broadcasted_iota(jnp.int32, (1, HALF), 1) + i * HALF)
            k_clip = clip_of(lax.broadcasted_iota(jnp.int32, (BLK, 1), 0))
            same = q_clip == k_clip
            outs = []
            for h in range(3):
                s = mm(kh[h, blk], qh[h, rows], 1, 1) * 0.125
                s = jnp.where(same, s, masked)
                e = jnp.exp(s - jnp.max(s, axis=0, keepdims=True))
                p = (e / jnp.sum(e, axis=0, keepdims=True)).astype(BF16)
                pr[3 * b + h, :, pl.ds(pl.multiple_of(i * HALF, HALF), HALF)] = p
                outs.append(mm(vh[h, blk], p, 0, 0))
            att[rows, 0:128] = pltpu.roll(outs[2], 64, 0).T.astype(BF16)
            att[rows, 128:256] = (outs[0] + outs[1]).T.astype(BF16)

        chunks(b, 2, fn)

    def out_part(b):
        sum_part(0, b, lambda rows: mm(att[rows], g[0, :, :, 512:768].reshape(D, 256), 1, 1))

    def second_norm(b):
        rows = own_rows(b)
        m = tok[rows].astype(F32) + sum_end(0, b) + prm[4:5]
        mid[b] = m
        zz, _ = standardize(m)
        n2[rows] = (zz * prm[1:2] + prm[3:4]).astype(BF16)
        launch(share(n2, 0, b))

    def up(b):
        def fn(rows, i):
            h = mm(n2[rows], mat(1), 1, 0) + prm[7:8]
            cdf = 0.5 * (1.0 + lax.erf(h * (1.0 / math.sqrt(2.0))))
            act[rows] = (h * cdf).astype(BF16)
            dgl[rows] = cdf + h * (jnp.exp(-0.5 * h * h) * (1.0 / math.sqrt(2.0 * math.pi)))

        chunks(b, 4, fn, lambda: shared(n2, 0, b))

    def hidden_back(b):
        def product(rows):
            low_grad = (mm(cot[rows], mat(2), 1, 0) * dgl[rows]).astype(BF16)
            hg[rows] = low_grad
            sg[7:8] += jnp.sum(low_grad.astype(F32), axis=0, keepdims=True)
            return mm(low_grad, mat(1), 1, 1)

        sum_part(2, b, product)

    def middle_back(b):
        rows = own_rows(b)
        total = sum_end(2, b)
        zz, rstd = standardize(mid[b])
        out_grad = cot[rows].astype(F32)
        m = out_grad + norm_back(total, prm[1:2], zz, rstd)
        mgr[b] = m
        ml[rows] = m.astype(BF16)
        launch(share(ml, 1, b))
        sg[1:2] += jnp.sum(total * zz, axis=0, keepdims=True)
        sg[3:4] += jnp.sum(total, axis=0, keepdims=True)
        sg[4:5] += jnp.sum(m, axis=0, keepdims=True)
        sg[5:6] += jnp.sum(out_grad, axis=0, keepdims=True)

    def attend_back(b):
        blk = slice(b * BLK, b * BLK + BLK)
        dka[...] = jnp.zeros_like(dka)
        dva[...] = jnp.zeros_like(dva)

        def fn(rows, i):
            da = mm(ml[rows], g[0, :, :, 512:768].reshape(D, 256), 1, 0)
            d2, d01 = da[:, 0:128], da[:, 128:256]
            dos = (
                jnp.where(low, d01, 0.0).astype(BF16),
                jnp.where(low, 0.0, d01).astype(BF16),
                jnp.where(low, pltpu.roll(d2, 64, 1), 0.0).astype(BF16),
            )
            dqs = []
            for h in range(3):
                p = pr[3 * b + h, :, pl.ds(pl.multiple_of(i * HALF, HALF), HALF)]
                pf = p.astype(F32)
                dp = mm(vh[h, blk], dos[h], 1, 1)
                ds = (pf * (dp - jnp.sum(pf * dp, axis=0, keepdims=True))).astype(BF16)
                dqs.append(mm(kh[h, blk], ds, 0, 0))
                dka[h] += mm(ds, qh[h, rows], 1, 0)
                dva[h] += mm(p, dos[h], 1, 0)
            dqkv[rows, 0:128] = ((dqs[0] + dqs[1]) * 0.125).T.astype(BF16)
            dqkv[rows, 384:512] = (dqs[2] * 0.125).T.astype(BF16)

        chunks(b, 2, fn, lambda: shared(ml, 1, b))
        dqkv[blk, 128:256] = ((dka[0] + dka[1]) * 0.125).astype(BF16)
        dqkv[blk, 256:384] = (dva[0] + dva[1]).astype(BF16)
        dqkv[blk, 384:512] = (
            dqkv[blk, 384:512].astype(F32) + pltpu.roll(dka[2], 64, 1) * 0.125
        ).astype(BF16)
        dqkv[blk, 512:640] = dva[2].astype(BF16)
        sg[6:7, 0:640] += jnp.sum(dqkv[blk, 0:640].astype(F32), axis=0, keepdims=True)

    def in_part(b):
        def product(rows):
            part = mm(dqkv[rows, 0:640], g[0, :, :, 0:640].reshape(D, 640), 1, 1)
            zz, _ = standardize(tok[rows].astype(F32))
            sg[0:1] += jnp.sum(part * zz, axis=0, keepdims=True)
            sg[2:3] += jnp.sum(part, axis=0, keepdims=True)
            return part

        sum_part(3, b, product)

    def out_copies(k, buf, out, b):
        mine = pltpu.make_async_copy(buf.at[b], out.at[own_rows(b)], lsem.at[2 + 2 * k + b])
        mine.start()
        later.append((mine.wait, None))
        theirs = remote(buf.at[b], out.at[own_rows(b)], oss.at[k, b], ors.at[k, b], d, sib)
        launch(theirs)
        rows = half_rows(b, 0)
        back = remote(buf.at[b], out.at[rows], oss.at[k, b], ors.at[k, b], d, sib)
        later.append((back.wait_recv, None))

    def finish_mixed(b):
        mxs[b] = (mid[b] + sum_end(1, b) + prm[5:6]).astype(BF16)
        out_copies(0, mxs, mixed_h, b)

    def finish_tokens(b):
        total = sum_end(3, b)
        zz, rstd = standardize(tok[own_rows(b)].astype(F32))
        mgr[b] = mgr[b] + norm_back(total, prm[0:1], zz, rstd)
        out_copies(1, mgr, tgrad_h, b)

    def cut(q):
        return slice(384 * q, 384 * q + 384)

    def xred(m, q, k):
        return remote(
            gr.at[m, 2 * k + 1 - x, :, cut(q)], rx.at[m, k, :, cut(q)],
            rxs.at[m, q, k], rxr.at[m, q, k], xn, t,
        )

    zp = z + 1 - 2 * lax.rem(z, 2)
    zf = lax.rem(z + 2, 4)
    zpf = lax.rem(zp + 2, 4)

    def zred(m, q, k):
        ahead = lax.rem(z + k + 1, 4)
        src, to = ((zp, zp), (zpf, zp), (zf, zf))[k] if m < 2 else (ahead, ahead)
        return remote(
            hs.at[m, src, :, cut(q)], rz.at[m, k, :, cut(q)],
            rzs.at[m, q, k], rzr.at[m, q, k], 2 * to + x, t,
        )

    def weight_grad(m, product):
        for half in range(2):
            gr[m, 4 * half : 4 * half + 4] = product(cut(half)).astype(BF16).reshape(4, PIECE, D)

    def reduce_start(m, q):
        if inner:
            for k in range(4):
                launch(xred(m, q, k))

    outs = (gra_o, gru_o, grd_o)

    def reduce_mid(m, q):
        if not inner:
            return
        places = ((1, zpf), (0, zp), (2, zf), (3, z))
        if m == 2:
            places = tuple((k, lax.rem(z + k + 1, 4)) for k in (1, 0, 2, 3))
        for k, zd in places:
            xred(m, q, zd).wait_recv()
            both = gr[m, 2 * zd + x, :, cut(q)].astype(F32) + rx[m, zd, :, cut(q)].astype(F32)
            if k < 3:
                hs[m, zd, :, cut(q)] = both.astype(BF16)
            else:
                outs[m][:, cut(q)] = both
            if k < (2 if m < 2 else 3):
                launch(zred(m, q, k))

    def reduce_far(m, q):
        if not inner or m == 2:
            return
        zred(m, q, 1).wait_recv()
        far = hs[m, zf, :, cut(q)].astype(F32) + rz[m, 1, :, cut(q)].astype(F32)
        hs[m, zf, :, cut(q)] = far.astype(BF16)
        launch(zred(m, q, 2))

    def reduce_end(m):
        if not inner:
            outs[m][...] = gr[m]
            return
        for q in range(2):
            for k in (0, 2) if m < 2 else (0, 1, 2):
                zred(m, q, k).wait_recv()
                outs[m][:, cut(q)] += rz[m, k, :, cut(q)].astype(F32)

    def down_grad(cols):
        return mm(cot[:, cols], act[...], 0, 0)

    def up_grad(cols):
        return mm(n2[:, cols], hg[...], 0, 0)

    def in_grad(cols):
        a1 = mm(nrm[:, cols], dqkv[:, 0:640], 0, 0)
        a2 = mm(ml[:, cols], att[...], 0, 0)
        return jnp.concatenate(
            [a1[:, 0:512], a1[:, 512:640] + a2[:, 0:128], a2[:, 128:256]], axis=1
        )

    row = lax.broadcasted_iota(jnp.int32, (8, 1), 0)

    def small_c():
        return remote(sg, sgc.at[0], sms.at[0], smr.at[0], d, sib)

    def small_y():
        return remote(sgc.at[1], sgc.at[2], sms.at[1], smr.at[1], d, yn)

    def small_x():
        return remote(sgx.at[0], sgx.at[1], sms.at[2], smr.at[2], xn, t)

    def small_z(k):
        return remote(
            sgz.at[0], sgz.at[k], sms.at[2 + k], smr.at[2 + k], lax.rem(d + 2 * k, 8), t
        )

    def small_step(n):
        if n == 0:
            launch(small_c())
        elif n == 1:
            small_c().wait_recv()
            sgc[1] = sg[...] + jnp.where(row < 6, sgc[0], 0.0)
            launch(small_y())
        elif n == 2:
            small_y().wait_recv()
            both = sgc[1] + jnp.where(jnp.logical_or(row == 0, row == 2), sgc[2], 0.0)
            if inner:
                sgx[0] = both
                launch(small_x())
            else:
                small_o[...] = both
        elif n == 3 and inner:
            small_x().wait_recv()
            sgz[0] = sgx[0] + sgx[1]
            for k in (1, 2, 3):
                launch(small_z(k))
        elif n == 4 and inner:
            for k in (1, 2, 3):
                small_z(k).wait_recv()
            small_o[...] = (sgz[0] + sgz[1]) + (sgz[2] + sgz[3])

    sg[...] = jnp.zeros_like(sg)
    own_pieces = []
    for m in range(3 if not inner else 4):
        own_pieces.append(
            pltpu.make_async_copy(shards[m], slot(m, d) if inner else g.at[m], lsem.at[6 + m])
        )

    def add_parameters():
        if inner:
            own_pieces[3].wait()
            gather_end(3)
            total = gs[0].astype(F32)
            for i in range(1, PARTS):
                total = total + gs[i].astype(F32)
            prm[...] = total
        else:
            prm[...] = ws[...].astype(F32)

    def step(m, s):
        if inner:
            gather_step(m, s)

    if inner:
        for m in (0, 3):
            gather_z(m)
            gather_x(m)
    for cp in own_pieces:
        cp.start()
    step(0, 1)
    step(3, 1)
    step(0, 2)
    step(3, 2)
    if inner:
        gather_z(1)
    step(0, 3)
    step(3, 3)
    if inner:
        gather_x(1)
    step(1, 1)
    add_parameters()
    cp_tok.wait()
    first_norm(0)
    if inner:
        gather_z(2)
    for b in range(1, nb):
        first_norm(b)
    for cp in own_pieces[:3]:
        cp.wait()
    if inner:
        gather_end(0)
    step(1, 2)
    project(0)
    attend(0)
    out_part(0)
    step(1, 3)
    if inner:
        gather_x(2)
    sum_mid(0, 0)
    step(2, 1)
    project(1)
    attend(1)
    out_part(1)
    step(2, 2)
    cp_cot.wait()
    sum_mid(0, 1)
    step(2, 3)
    if inner:
        gather_end(1)
    for b in range(nb):
        second_norm(b)
        up(b)
        if inner and b == 0:
            gather_end(2)
        if b == nb - 1:
            weight_grad(2, down_grad)
            reduce_start(2, 0)
            reduce_start(2, 1)
        hidden_back(b)
        if b == 0:
            sum_part(1, b, lambda rows: mm(act[rows], mat(2), 1, 1))
        sum_mid(2, b)
    for b in range(1, nb):
        sum_part(1, b, lambda rows: mm(act[rows], mat(2), 1, 1))
    weight_grad(1, up_grad)
    for b in range(nb):
        middle_back(b)
        attend_back(b)
        if b == 0:
            sum_mid(1, 0)
            reduce_start(1, 0)
            reduce_start(1, 1)
        if b == nb - 1:
            weight_grad(0, in_grad)
            reduce_start(0, 1)
            for q in range(2):
                reduce_far(2, q)
        in_part(b)
        if b == nb - 1:
            small_step(0)
            small_step(1)
        sum_mid(3, b)
        if b == 0:
            for q in range(2):
                reduce_mid(2, q)
    reduce_start(0, 0)
    for b in range(1, nb):
        sum_mid(1, b)
    for q in range(2):
        reduce_mid(1, q)
    finish_mixed(0)
    finish_tokens(0)
    for q in range(2):
        reduce_far(1, q)
    small_step(2)
    reduce_mid(0, 1)
    reduce_far(0, 1)
    reduce_mid(0, 0)
    reduce_far(0, 0)
    for b in range(1, nb):
        finish_tokens(b)
    small_step(3)
    reduce_end(2)
    reduce_end(1)
    small_step(4)
    reduce_end(0)
    for b in range(1, nb):
        finish_mixed(b)
    for wait, guard in later:
        if guard is None:
            wait()
        else:
            pl.when(guard)(wait)


def call_kernel(inner, *args):
    rows = args[0].shape[0]
    nb = rows // BLK
    vmem = pl.BlockSpec(memory_space=pltpu.VMEM)
    anywhere = pl.BlockSpec(memory_space=pl.ANY)
    grads = (
        jax.ShapeDtypeStruct((PIECE, D), F32)
        if inner
        else jax.ShapeDtypeStruct((PARTS, PIECE, D), BF16)
    )
    dma = pltpu.SemaphoreType.DMA
    scratch = [
        pltpu.VMEM((rows, D), BF16),
        pltpu.VMEM((rows, D), BF16),
        pltpu.VMEM((3, PARTS, PIECE, D), BF16),
        pltpu.VMEM((PARTS, 16, D), BF16),
        pltpu.VMEM((16, D), F32),
        pltpu.VMEM((rows, D), BF16),
        pltpu.VMEM((3, rows, 128), BF16),
        pltpu.VMEM((3, rows, 128), BF16),
        pltpu.VMEM((3, rows, 128), BF16),
        pltpu.VMEM((3 * nb, BLK, BLK), BF16),
        pltpu.VMEM((rows, 256), BF16),
        pltpu.VMEM((nb, HALF, D), F32),
        pltpu.VMEM((rows, D), BF16),
        pltpu.VMEM((rows, D), BF16),
        pltpu.VMEM((rows, D), F32),
        pltpu.VMEM((rows, D), BF16),
        pltpu.VMEM((rows, D), BF16),
        pltpu.VMEM((nb, HALF, D), F32),
        pltpu.VMEM((rows, 640), BF16),
        pltpu.VMEM((3, BLK, 128), F32),
        pltpu.VMEM((3, BLK, 128), F32),
        pltpu.VMEM((4, nb, 2, HALF, D), BF16),
        pltpu.VMEM((4, nb, HALF, D), BF16),
        pltpu.VMEM((4, nb, HALF, D), BF16),
        pltpu.VMEM((nb, HALF, D), BF16),
        pltpu.VMEM((3, PARTS, PIECE, D), BF16),
        pltpu.VMEM((3, 4, PIECE, D), BF16),
        pltpu.VMEM((3, 4, PIECE, D), BF16),
        pltpu.VMEM((3, 3, PIECE, D), BF16),
        pltpu.VMEM((8, D), F32),
        pltpu.VMEM((3, 8, D), F32),
        pltpu.VMEM((2, 8, D), F32),
        pltpu.VMEM((4, 8, D), F32),
        dma((10,)),
        dma((4, 2, 3)),
        dma((4, 2, 3)),
        dma((4, 4)),
        dma((4, 4)),
        dma((4, nb)),
        dma((4, nb)),
        dma((4, nb)),
        dma((4, nb)),
        dma((2, nb)),
        dma((2, nb)),
        dma((2, nb)),
        dma((2, nb)),
        dma((3, 2, 4)),
        dma((3, 2, 4)),
        dma((3, 2, 3)),
        dma((3, 2, 3)),
        dma((6,)),
        dma((6,)),
    ]
    if inner:
        scratch += [pltpu.VMEM((PIECE, D), BF16), pltpu.VMEM((16, D), BF16), pltpu.VMEM((16, D), F32)]

    def kernel(*refs):
        layer_kernel(inner, nb, refs)

    return pl.pallas_call(
        kernel,
        out_shape=(
            jax.ShapeDtypeStruct((rows, D), BF16),
            jax.ShapeDtypeStruct((rows, D), F32),
            grads,
            grads,
            grads,
            jax.ShapeDtypeStruct((8, D), F32),
        ),
        in_specs=[anywhere, anywhere]
        + ([vmem, vmem, anywhere, anywhere, vmem, vmem, vmem, vmem] if inner else [vmem] * 4)
        + [pl.BlockSpec(memory_space=pltpu.SMEM)],
        out_specs=(anywhere, anywhere, vmem, vmem, vmem, vmem),
        scratch_shapes=scratch,
        compiler_params=pltpu.CompilerParams(
            collective_id=0, has_side_effects=True, vmem_limit_bytes=60 * 2**20
        ),
    )(*args)


def pack_heads(q, k, v, o):
    return jnp.concatenate(
        [
            q[..., :128], k[..., :128], v[..., :128],
            q[..., 128:], k[..., 128:], v[..., 128:], o[..., 128:], o[..., :128],
        ],
        axis=-1,
    )


def unpack_heads(w):
    q = jnp.concatenate([w[..., 0:128], w[..., 384:448]], axis=-1)
    k = jnp.concatenate([w[..., 128:256], w[..., 448:512]], axis=-1)
    v = jnp.concatenate([w[..., 256:384], w[..., 512:576]], axis=-1)
    o = jnp.concatenate([w[..., 640:768], w[..., 576:640]], axis=-1)
    return q, k, v, o


def unpack_kernel(mix_h, tok_h, ga, gu, gd, small, mix_o, tok_o, qkv_o, out_o, up_o, down_o, gains_o, shifts_o, bqkv_o, bup_o, tok_v, mix_v, sem):
    d = lax.axis_index("dp")
    moves = []
    for src, via, dst in ((tok_h, tok_v, tok_o), (mix_h, mix_v, mix_o)):
        for k in range(2):
            rows = slice(k * src.shape[0] // 2, (k + 1) * src.shape[0] // 2)
            sems = sem.at[len(moves)]
            load = pltpu.make_async_copy(src.at[rows], via.at[rows], sems)
            load.start()
            moves.append((load, pltpu.make_async_copy(via.at[rows], dst.at[rows], sems)))
    for load, store in moves:
        load.wait()
        store.start()
    own = gains_o.shape[1]
    for k in range(3):
        qkv_o[k, :, 0:128] = ga[:, 128 * k : 128 * k + 128]
    qkv_o[0, :, 128:192] = ga[:, 384:448]
    qkv_o[1, :, 128:192] = pltpu.roll(ga[:, 384:512], 64, 1)[:, 0:64]
    qkv_o[2, :, 128:192] = ga[:, 512:576]
    fill = jnp.zeros((128 - own, 128), F32)
    out_o[0:128, :] = jnp.concatenate([ga[:, 640:768], fill], axis=0).T[:, 0:own]
    out_o[128:192, :] = jnp.concatenate([ga[:, 512:640], fill], axis=0).T[64:128, 0:own]
    up_o[...] = gu[...]
    down_o[...] = gd[...]
    wide = pltpu.roll(small[...], D - d * own, 1)
    gains_o[...] = wide[0:2, 0:own]
    shifts_o[...] = wide[2:6, 0:own]
    for part in range(2):
        for h, at in enumerate((0, 64, 384) if part == 0 else (256, 320, 512)):
            per = bqkv_o.shape[2]
            slab = small[:, at // 128 * 128 : at // 128 * 128 + 128]
            turned = pltpu.roll(slab, 128 - at % 128 - d * per + 128 * (at % 128 // 64), 1)
            bqkv_o[h, part : part + 1, :] = turned[6:7, 0:per]
    for k in range(6):
        per = bup_o.shape[1]
        turned = pltpu.roll(small[:, 128 * k : 128 * k + 128], 128 - d * per, 1)
        bup_o[k : k + 1, :] = turned[7:8, 0:per]
    for _, store in moves:
        store.wait()


def body(tokens, cotangent, w_qkv, w_out, w_up, w_down, gains, shifts, b_qkv, b_up, clip_lengths):
    own = w_up.shape[0]
    dp = D // own
    if dp == 8:
        mixed, tgrad, ga, gu, gd, small = call_kernel(
            True, tokens, cotangent, w_qkv, w_out, w_up, w_down.T,
            gains, shifts, b_qkv.transpose(1, 0, 2), b_up, clip_lengths,
        )
        vmem = pl.BlockSpec(memory_space=pltpu.VMEM)
        anywhere = pl.BlockSpec(memory_space=pl.ANY)
        like = [mixed, tgrad, w_qkv, w_out, gu, gd, gains, shifts, b_qkv.transpose(1, 0, 2), b_up]
        outs = pl.pallas_call(
            unpack_kernel,
            out_shape=tuple(
                jax.ShapeDtypeStruct(a.shape, BF16 if i == 0 else F32) for i, a in enumerate(like)
            ),
            in_specs=[anywhere, anywhere] + [vmem] * 4,
            out_specs=tuple([anywhere, anywhere] + [vmem] * 8),
            scratch_shapes=[
                pltpu.VMEM(tgrad.shape, F32),
                pltpu.VMEM(mixed.shape, BF16),
                pltpu.SemaphoreType.DMA((8,)),
            ],
        )(mixed, tgrad, ga, gu, gd, small)
        return outs[:5] + (outs[5].T, outs[6], outs[7], outs[8].transpose(1, 0, 2), outs[9])

    d = lax.axis_index("dp")
    wide = jnp.concatenate([gains, shifts], axis=0)
    wide = lax.dynamic_update_slice(jnp.zeros((6, D), BF16), wide, (0, d * own))
    heads = b_qkv.shape[1]
    per_head = b_qkv.shape[2]
    full_head = per_head * dp
    bq = lax.dynamic_update_slice(
        jnp.zeros((2, heads, full_head), BF16), b_qkv, (0, 0, d * per_head)
    ).reshape(2, heads * full_head)
    none = jnp.zeros((heads * full_head,), BF16)
    bq = pack_heads(bq[0], none, bq[1], none)
    bu = lax.dynamic_update_slice(
        jnp.zeros((b_up.shape[0], b_up.shape[1] * dp), BF16), b_up, (0, d * b_up.shape[1])
    ).reshape(1, D)
    ws = jnp.concatenate([wide, bq[None], bu, jnp.zeros((8, D), BF16)], axis=0)
    ws = lax.psum(ws.astype(F32), "dp").astype(BF16)
    wa = pack_heads(w_qkv[0], w_qkv[1], w_qkv[2], w_out.T)
    wa, wu, wd = (
        lax.all_gather(w, "dp", axis=0, tiled=True).reshape(PARTS, PIECE, D)
        for w in (wa, w_up, w_down.T)
    )
    mixed, tgrad, ga, gu, gd, small = call_kernel(
        False, tokens, cotangent, ws, wa, wu, wd, clip_lengths
    )
    ga, gu, gd = (
        lax.psum_scatter(w.astype(F32).reshape(D, D), "dp", scatter_dimension=0, tiled=True)
        for w in (ga, gu, gd)
    )
    small = lax.psum(small, "dp")
    q, k, v, o = unpack_heads(ga)
    wide = lax.dynamic_slice(small[0:6], (0, d * own), (6, own))
    bq, _, bv, _ = unpack_heads(small[6])
    b_qkv_grad = jnp.stack([bq, bv]).reshape(2, heads, full_head)
    b_qkv_grad = lax.dynamic_slice(b_qkv_grad, (0, 0, d * per_head), (2, heads, per_head))
    b_up_grad = lax.dynamic_slice(
        small[7].reshape(b_up.shape[0], -1), (0, d * b_up.shape[1]), b_up.shape
    )
    return (
        mixed,
        tgrad,
        jnp.stack([q, k, v]),
        o.T,
        gu,
        gd.T,
        wide[0:2],
        wide[2:6],
        b_qkv_grad,
        b_up_grad,
    )


def solution(mesh):
    return jax.shard_map(
        body,
        mesh=mesh,
        in_specs=(
            P("dp", None),
            P("dp", None),
            P(None, "dp", "tp"),
            P("tp", "dp"),
            P("dp", "tp"),
            P("tp", "dp"),
            P(None, "dp"),
            P(None, "dp"),
            P(None, "tp", "dp"),
            P("tp", "dp"),
            P("dp", None),
        ),
        out_specs=(
            P("dp", None),
            P("dp", None),
            P(None, "dp", "tp"),
            P("tp", "dp"),
            P("dp", "tp"),
            P("tp", "dp"),
            P(None, "dp"),
            P(None, "dp"),
            P(None, "tp", "dp"),
            P("tp", "dp"),
        ),
        check_vma=False,
    )
```
